32 devices in a mesh: section: 2 (over x), dp: 16 (over z, y, core).
Axes of the slice: x: 2, y: 2, z: 4, core: 2. Of those that a mesh axis runs over, the one named last changes fastest.
Arguments:
- text: bfloat16 [4096, 768], P('dp', 'section'), may hold values from -6 to 6
- image: bfloat16 [64, 576, 768], P('dp', 'section'), may hold values from -6 to 6
- lengths: int32 [64], P('dp'), may hold values from 5 to 64
- self_gain: bfloat16 [2, 768], P('section', 'dp'), may hold values from 0.25 to 1.75
- self_shift: bfloat16 [2, 768], P('section', 'dp'), may hold values from -1.75 to 1.75
- heads_in: bfloat16 [2, 768, 2304], P('section', 'dp'), may hold values from -0.3125 to 0.3125
- heads_out: bfloat16 [2, 768, 768], P('section', 'dp'), may hold values from -0.21875 to 0.21875
- feed_gain: bfloat16 [2, 768], P('section', 'dp'), may hold values from 0.25 to 1.75
- feed_shift: bfloat16 [2, 768], P('section', 'dp'), may hold values from -1.75 to 1.75
- up_weight: bfloat16 [2, 768, 3072], P('section', 'dp'), may hold values from -0.21875 to 0.21875
- up_bias: bfloat16 [2, 3072], P('section', 'dp'), may hold values from -1.75 to 1.75
- down_weight: bfloat16 [2, 3072, 768], P('section', 'dp'), may hold values from -0.109375 to 0.109375
- down_bias: bfloat16 [2, 768], P('section', 'dp'), may hold values from -1.75 to 1.75
- cross_gain: bfloat16 [768], P(('section', 'dp')), may hold values from 0.25 to 1.75
- cross_shift: bfloat16 [768], P(('section', 'dp')), may hold values from -1.75 to 1.75
- cross_query: bfloat16 [768, 768], P(('section', 'dp')), may hold values from -0.3125 to 0.3125
- cross_keys: bfloat16 [768, 1536], P(('section', 'dp')), may hold values from -0.21875 to 0.21875
- cross_out: bfloat16 [768, 768], P(('section', 'dp')), may hold values from -0.4375 to 0.4375
- cotangent: bfloat16 [4096, 768], P('dp', 'section'), may hold values from -6 to 6
Outputs:
- layer_out: float32 [4096, 768], P('dp', 'section')
- text_grad: float32 [4096, 768], P('dp', 'section')
- image_grad: float32 [64, 576, 768], P('dp', 'section')
- self_gain_grad: float32 [2, 768], P('section', 'dp')
- self_shift_grad: float32 [2, 768], P('section', 'dp')
- heads_in_grad: float32 [2, 768, 2304], P('section', 'dp')
- heads_out_grad: float32 [2, 768, 768], P('section', 'dp')
- feed_gain_grad: float32 [2, 768], P('section', 'dp')
- feed_shift_grad: float32 [2, 768], P('section', 'dp')
- up_weight_grad: float32 [2, 768, 3072], P('section', 'dp')
- up_bias_grad: float32 [2, 3072], P('section', 'dp')
- down_weight_grad: float32 [2, 3072, 768], P('section', 'dp')
- down_bias_grad: float32 [2, 768], P('section', 'dp')
- cross_gain_grad: float32 [768], P(('section', 'dp'))
- cross_shift_grad: float32 [768], P(('section', 'dp'))
- cross_query_grad: float32 [768, 768], P(('section', 'dp'))
- cross_keys_grad: float32 [768, 1536], P(('section', 'dp'))
- cross_out_grad: float32 [768, 768], P(('section', 'dp'))
The draws below stay inside these ranges and needn't reach their ends.
Inputs may be any that keep to these rules, and one draw needn't show every extreme that they name: `lengths`: a caption of length n holds its tokens in its first n of 64 slots; the rest is padding.
All inputs are finite; a program needn't handle non-finite values.
Results may differ from the reference program's by a relative error of at most 0.025.
Values may be sent and summed in bfloat16 or wider, within the bound.
No kernel may reach another device: no remote copies, remote signals or barrier semaphores. Data moves between devices by JAX's collectives and lax.ppermute only.
A program may use at most 320 MiB of HBM per device.

```python
import math
import jax
import jax.numpy as jnp
from jax import lax

D = 768
HEADS = 12
HEAD_DIM = 64
FF = 3072
IMG = 576
SLOTS = 64
CAPTIONS = 64
TOKENS = 4096
N_SECTION = 2


def place_ends(values, own_key, smallest, largest):
    dims = values.shape
    spot = [jax.random.randint(jax.random.fold_in(own_key, axis), (), 0, dims[axis]) for axis in range(len(dims))]
    values = values.at[tuple(spot)].set(smallest)
    longest = dims.index(max(dims))
    spot[longest] = (spot[longest] + 1) % dims[longest]
    return values.at[tuple(spot)].set(largest)


def levels(stream_key, shape, cuts, smallest, top_value):
    loudness = 1.0
    for position, blocks in cuts:
        heights = jax.random.uniform(jax.random.fold_in(jax.random.fold_in(stream_key, 6), position), (blocks,), jnp.float32, smallest / len(cuts), top_value / len(cuts))
        loudness = loudness * jnp.repeat(jnp.exp(heights), shape[position] // blocks).reshape((-1,) + (1,) * (len(shape) - 1 - position))
    return loudness


def bell_draw(rng, dims, scale, limit, cuts=(), held_as=jnp.bfloat16):
    array = scale * jax.random.normal(rng, dims, jnp.float32)
    if cuts:
        array = array * levels(rng, dims, cuts, -0.22, 0.18)
    return jnp.clip(array, -limit, limit).astype(held_as)


def setup_inputs(seed: int = 0) -> dict:
    key_of = jax.random.split(jax.random.key(seed), 20)
    text = bell_draw(key_of[0], (TOKENS, D), 1.0, 6.0, ((0, 16), (1, 2)))
    image = bell_draw(key_of[1], (CAPTIONS, IMG, D), 1.0, 6.0, ((0, 16), (1, 2)))
    lengths = place_ends(jax.random.randint(key_of[2], (CAPTIONS,), 5, SLOTS + 1), jax.random.fold_in(key_of[2], 1), 5, SLOTS).astype(jnp.int32)
    self_gain = jnp.clip(1.0 + 0.15 * jax.random.normal(key_of[3], (N_SECTION, D), jnp.float32), 0.25, 1.75).astype(jnp.bfloat16)
    self_shift = bell_draw(key_of[4], (N_SECTION, D), 0.3, 1.75, ((0, 2), (1, 16)))
    heads_in = bell_draw(key_of[5], (N_SECTION, D, 3 * D), (D // 2) ** -0.5, 0.3125, ((0, 2), (1, 16)))
    heads_out = bell_draw(key_of[6], (N_SECTION, D, D), D ** -0.5, 0.21875, ((0, 2), (1, 16)))
    feed_gain = jnp.clip(1.0 + 0.15 * jax.random.normal(key_of[7], (N_SECTION, D), jnp.float32), 0.25, 1.75).astype(jnp.bfloat16)
    feed_shift = bell_draw(key_of[8], (N_SECTION, D), 0.3, 1.75, ((0, 2), (1, 16)))
    up_weight = bell_draw(key_of[9], (N_SECTION, D, FF), D ** -0.5, 0.21875, ((0, 2), (1, 16)))
    up_bias = bell_draw(key_of[10], (N_SECTION, FF), 0.3, 1.75, ((0, 2), (1, 16)))
    down_weight = bell_draw(key_of[11], (N_SECTION, FF, D), FF ** -0.5, 0.109375, ((0, 2), (1, 16)))
    down_bias = bell_draw(key_of[12], (N_SECTION, D), 0.3, 1.75, ((0, 2), (1, 16)))
    cross_gain = jnp.clip(1.0 + 0.15 * jax.random.normal(key_of[13], (D,), jnp.float32), 0.25, 1.75).astype(jnp.bfloat16)
    cross_shift = bell_draw(key_of[14], (D,), 0.3, 1.75, ((0, 32),))
    cross_query = bell_draw(key_of[15], (D, D), (D // 2) ** -0.5, 0.3125, ((0, 32),))
    cross_keys = bell_draw(key_of[16], (D, 2 * D), D ** -0.5, 0.21875, ((0, 32),))
    cross_out = bell_draw(key_of[17], (D, D), (D // 4) ** -0.5, 0.4375, ((0, 32),))
    cotangent = bell_draw(key_of[18], (TOKENS, D), 1.0, 6.0, ((0, 16), (1, 2)))
    return {"text": text, "image": image, "lengths": lengths, "self_gain": self_gain, "self_shift": self_shift, "heads_in": heads_in, "heads_out": heads_out, "feed_gain": feed_gain, "feed_shift": feed_shift, "up_weight": up_weight, "up_bias": up_bias, "down_weight": down_weight, "down_bias": down_bias, "cross_gain": cross_gain, "cross_shift": cross_shift, "cross_query": cross_query, "cross_keys": cross_keys, "cross_out": cross_out, "cotangent": cotangent}


@jax.custom_vjp
def low(v):
    return lax.optimization_barrier(v.astype(jnp.bfloat16)).astype(jnp.float32)

@jax.custom_vjp
def low_back(v):
    return v

def low_keep(v):
    return (low(v), None)

def low_pass(kept, grad):
    return (grad,)

def back_keep(v):
    return (v, None)

def back_low(kept, grad):
    return (low(grad),)
low.defvjp(low_keep, low_pass)
low_back.defvjp(back_keep, back_low)
EPS = 1e-05
MASKED = -1000000000.0
EXACT = lax.Precision.HIGHEST

def norm(values, gain, shift):
    centred = values - lax.optimization_barrier(jnp.mean(values, -1, keepdims=True))
    spread = lax.optimization_barrier(jnp.mean(centred * centred, -1, keepdims=True))
    return centred * lax.rsqrt(spread + EPS) * gain + shift

def softmax_rows(scores):
    top = lax.optimization_barrier(jnp.max(scores, -1, keepdims=True))
    raised = jnp.exp(scores - top)
    return raised / lax.optimization_barrier(jnp.sum(raised, -1, keepdims=True))

def product(left, right):
    return jnp.dot(left, right, precision=EXACT, preferred_element_type=jnp.float32)

def attend(queries, keys, values, keep):
    scores = jnp.einsum('cqhd,ckhd->chqk', queries, keys, precision=EXACT) * HEAD_DIM ** (-0.5)
    scores = low_back(scores)
    if keep is not None:
        scores = jnp.where(keep, scores, MASKED)
    chances = low(softmax_rows(scores))
    return jnp.einsum('chqk,ckhd->cqhd', chances, values, precision=EXACT)

def layer(inputs, keep, weights, cross):
    self_gain, self_shift, heads_in, heads_out, feed_gain, feed_shift, up_weight, up_bias, down_weight, down_bias = weights
    rows, width = inputs.shape
    captions = keep.shape[0]
    slots = rows // captions
    normed = low(norm(inputs, self_gain, self_shift))
    projected = low_back(low(product(normed, heads_in))).reshape(captions, slots, 3, HEADS, HEAD_DIM)
    mixed = attend(projected[:, :, 0], projected[:, :, 1], projected[:, :, 2], keep)
    mixed = low_back(low(mixed.reshape(rows, width)))
    current = inputs + low_back(product(mixed, heads_out))
    if cross is not None:
        cross_gain, cross_shift, cross_query, cross_out, pairs = cross
        cross_normed = low(norm(current, cross_gain, cross_shift))
        queries = low_back(low(product(cross_normed, cross_query))).reshape(captions, slots, HEADS, HEAD_DIM)
        split = pairs.reshape(captions, pairs.shape[1], 2, HEADS, HEAD_DIM)
        cross_mixed = attend(queries, split[:, :, 0], split[:, :, 1], None)
        cross_mixed = low_back(low(cross_mixed.reshape(rows, width)))
        current = current + low_back(product(cross_mixed, cross_out))
    feed_normed = low(norm(current, feed_gain, feed_shift))
    raised = low_back(product(feed_normed, up_weight) + up_bias)
    active = low(jax.nn.gelu(raised, approximate=False))
    return current + low_back(product(active, down_weight)) + down_bias

def two_layers(text_block, image_block, length_block, section_weights, cross_weights):
    captions = length_block.shape[0]
    place = jnp.arange(SLOTS)
    causal = (place[None, :] <= place[:, None])[None, :, :]
    filled = place[None, None, :] < length_block[:, None, None]
    keep = (causal & filled)[:, None, :, :]
    first_weights = tuple((weight[0] for weight in section_weights))
    later_weights = tuple((weight[1] for weight in section_weights))
    hidden = low_back(low(layer(text_block, keep, first_weights, None)))
    cross_gain, cross_shift, cross_query, cross_keys, cross_out = cross_weights
    pairs = low_back(low(product(image_block.reshape(captions * IMG, D), cross_keys))).reshape(captions, IMG, 2 * D)
    return layer(hidden, keep, later_weights, (cross_gain, cross_shift, cross_query, cross_out, pairs))

def forward(text, image, section_weights, cross_weights, lengths):
    count = math.gcd(CAPTIONS, max(1, 4096 // SLOTS))
    blocks = CAPTIONS // count
    checked = jax.checkpoint(two_layers)

    def run(carry, block):
        text_block, image_block, length_block = block
        return (carry, checked(text_block, image_block, length_block, section_weights, cross_weights))
    _, results = lax.scan(run, jnp.zeros((), jnp.float32), (text.reshape(blocks, count * SLOTS, D), image.reshape(blocks, count, IMG, D), lengths.reshape(blocks, count)))
    return results.reshape(CAPTIONS * SLOTS, D)

def reference(text, image, lengths, self_gain, self_shift, heads_in, heads_out, feed_gain, feed_shift, up_weight, up_bias, down_weight, down_bias, cross_gain, cross_shift, cross_query, cross_keys, cross_out, cotangent):
    section_weights = tuple((weight.astype(jnp.float32) for weight in (self_gain, self_shift, heads_in, heads_out, feed_gain, feed_shift, up_weight, up_bias, down_weight, down_bias)))
    cross_weights = tuple((weight.astype(jnp.float32) for weight in (cross_gain, cross_shift, cross_query, cross_keys, cross_out)))

    def wrapped(text_wide, image_wide, section_set, cross_set):
        return forward(text_wide, image_wide, section_set, cross_set, lengths)
    layer_out, pullback = jax.vjp(wrapped, text.astype(jnp.float32), image.astype(jnp.float32), section_weights, cross_weights)
    text_grad, image_grad, section_grads, cross_grads = pullback(cotangent.astype(jnp.float32))
    return (layer_out, text_grad, image_grad, section_grads[0], section_grads[1], section_grads[2], section_grads[3], section_grads[4], section_grads[5], section_grads[6], section_grads[7], section_grads[8], section_grads[9], cross_grads[0], cross_grads[1], cross_grads[2], cross_grads[3], cross_grads[4])
```

```python
import jax
import jax.numpy as jnp
from jax import lax
from jax.sharding import PartitionSpec as P

HEADS = 12
HEAD_DIM = 64
EPS = 1e-05
MASKED = -1000000000.0
F32 = jnp.float32
BF16 = jnp.bfloat16


def swap(value):
    return lax.ppermute(value, "section", [(0, 1), (1, 0)])


def side(own, other, section, axis):
    first = jnp.where(section == 0, own, other)
    later = jnp.where(section == 0, other, own)
    return jnp.concatenate([first, later], axis)


def pick(section, first, later):
    return jnp.where(section == 0, first, later)


def low(values):
    return values.astype(BF16)


def norm_stats(values):
    mean = jnp.mean(values, -1, keepdims=True)
    centred = values - mean
    scale = lax.rsqrt(jnp.mean(centred * centred, -1, keepdims=True) + EPS)
    return centred * scale, scale


def norm(values, gain, shift):
    unit, _ = norm_stats(values)
    return low(unit * gain + shift)


def norm_back(values, gain, grad):
    unit, scale = norm_stats(values)
    wide = grad * gain
    inner = wide - jnp.mean(wide, -1, keepdims=True) - unit * jnp.mean(wide * unit, -1, keepdims=True)
    return inner * scale, jnp.sum(grad * unit, 0), jnp.sum(grad, 0)


def dot(left, right):
    return jnp.dot(left, right, preferred_element_type=F32)


def dot_tn(left, right):
    return lax.dot_general(left, right, (((0,), (0,)), ((), ())), preferred_element_type=F32)


def dot_nt(left, right):
    return lax.dot_general(left, right, (((1,), (1,)), ((), ())), preferred_element_type=F32)


def gelu(values):
    return 0.5 * values * (1.0 + lax.erf(values * 0.5**0.5))


def gelu_slope(values):
    return 0.5 * (1.0 + lax.erf(values * 0.5**0.5)) + values * jnp.exp(-0.5 * values * values) * 0.3989422804014327


def softmax_rows(scores):
    raised = jnp.exp(scores - jnp.max(scores, -1, keepdims=True))
    return raised / jnp.sum(raised, -1, keepdims=True)


def split_heads(values, captions):
    rows, width = values.shape
    return values.reshape(captions, rows // captions, width // HEAD_DIM, HEAD_DIM)


def scores_of(queries, keys):
    return jnp.einsum("cqhd,ckhd->chqk", queries, keys, preferred_element_type=F32) * HEAD_DIM**-0.5


def mix(chances, values):
    return jnp.einsum("chqk,ckhd->cqhd", chances, values, preferred_element_type=F32)


def attend_back(queries, keys, values, chances, slope):
    grad_low = low(slope)
    scale = HEAD_DIM**-0.5
    query_part = jnp.einsum("chqk,ckhd->cqhd", grad_low, keys, preferred_element_type=F32) * scale
    key_part = jnp.einsum("chqk,cqhd->ckhd", grad_low, queries, preferred_element_type=F32) * scale
    return query_part, key_part


def body(
    text,
    image,
    lengths,
    self_gain,
    self_shift,
    heads_in,
    heads_out,
    feed_gain,
    feed_shift,
    up_weight,
    up_bias,
    down_weight,
    down_bias,
    cross_gain,
    cross_shift,
    cross_query,
    cross_keys,
    cross_out,
    cotangent,
):
    section = lax.axis_index("section")
    count = lax.axis_size("dp")
    captions, half_image, width = image.shape
    rows = text.shape[0]
    slots = rows // captions
    piece = heads_in.shape[1]
    cross_piece = cross_query.shape[0]
    half = width // 2
    folds = down_weight.shape[1] // (2 * piece)
    half_ff = folds * width

    def halves(index):
        into = heads_in[0].reshape(piece, 3, 2, half)[:, :, index].reshape(piece, 3 * half)
        up = up_weight[0].reshape(piece, count, 2, folds, piece)[:, :, index]
        up = up.transpose(0, 2, 1, 3).reshape(piece, half_ff)
        down = down_weight[0].reshape(2, folds, piece, width)[index]
        down = down.transpose(1, 0, 2).reshape(piece, folds * width)
        bias = up_bias[0].reshape(2, folds, piece)[index]
        vectors = jnp.stack([self_gain[0], self_shift[0], feed_gain[0], feed_shift[0], down_bias[0]] + [bias[i] for i in range(folds)], 1)
        return jnp.concatenate([into, heads_out[0], vectors], 1), jnp.concatenate([up, down], 1)

    attn_0, feed_0 = halves(0)
    attn_1, feed_1 = halves(1)
    own_attn, own_feed = pick(section, attn_0, attn_1), pick(section, feed_0, feed_1)
    got_attn, got_feed = swap(pick(section, attn_1, attn_0)), swap(pick(section, feed_1, feed_0))
    layer_attn = (pick(section, own_attn, got_attn), pick(section, got_attn, own_attn))
    layer_feed = (pick(section, own_feed, got_feed), pick(section, got_feed, own_feed))
    own_cross = jnp.concatenate([cross_query, cross_keys, cross_out, cross_gain[:, None], cross_shift[:, None]], 1)
    both_cross = side(own_cross, swap(own_cross), section, 1)
    cross_width = own_cross.shape[1]

    def gather(value):
        return lax.all_gather(value, "dp", axis=0, tiled=True)

    attn = [gather(layer_attn[0])]
    cross_all = gather(both_cross)
    feed = [gather(layer_feed[0])]
    attn.append(gather(layer_attn[1]))
    feed.append(gather(layer_feed[1]))
    cross_full = jnp.concatenate([cross_all[:, :cross_width], cross_all[:, cross_width:]], 0)
    cross_query_w = cross_full[:, :width]
    cross_keys_w = cross_full[:, width : 3 * width]
    cross_out_w = cross_full[:, 3 * width : 4 * width]
    cross_gain_w = cross_full[:, 4 * width].astype(F32)
    cross_shift_w = cross_full[:, 4 * width + 1].astype(F32)

    def layer_weights(index):
        a, f = attn[index], feed[index]
        vectors = a[:, 3 * half + width :].astype(F32).T
        bias = vectors[5:].reshape(half_ff)
        down = jnp.concatenate([f[:, half_ff + i * width : half_ff + (i + 1) * width] for i in range(folds)], 0)
        return dict(
            into=a[:, : 3 * half], out=a[:, 3 * half : 3 * half + width], up=f[:, :half_ff], down=down,
            self_gain=vectors[0], self_shift=vectors[1], feed_gain=vectors[2], feed_shift=vectors[3],
            down_bias=vectors[4], up_bias=bias,
        )

    place = jnp.arange(slots)
    keep = ((place[None, :] <= place[:, None])[None] & (place[None, None, :] < lengths[:, None, None]))[:, None]

    whole_text = side(text, swap(text), section, 1)
    whole_cot = side(cotangent, swap(cotangent), section, 1)

    def self_forward(inputs, w):
        normed = norm(inputs, w["self_gain"], w["self_shift"])
        projected = low(dot(normed, w["into"]))
        queries, keys, values = (split_heads(projected[:, i * half : (i + 1) * half], captions) for i in range(3))
        scores = jnp.where(keep, scores_of(queries, keys), MASKED)
        chances = softmax_rows(scores)
        mixed = low(mix(low(chances), values)).reshape(rows, half)
        mixed_all = side(mixed, swap(mixed), section, 1)
        current = inputs + dot(mixed_all, w["out"])
        return current, (normed, queries, keys, values, chances, mixed_all)

    def feed_forward(current, w):
        normed = norm(current, w["feed_gain"], w["feed_shift"])
        raised = dot(normed, w["up"]) + w["up_bias"]
        active = low(gelu(raised))
        part = low(dot(active, w["down"]))
        return part, (normed, raised, active)

    w0, w1 = layer_weights(0), layer_weights(1)
    flat_image = image.reshape(captions * half_image, width)
    pairs = low(dot(flat_image, cross_keys_w))
    image_keys = split_heads(pairs[:, :width], captions)
    image_values = split_heads(pairs[:, width:], captions)

    text32 = whole_text.astype(F32)
    mid_0, saved_0 = self_forward(text32, w0)
    part_0, feed_saved_0 = feed_forward(mid_0, w0)
    hidden = low(mid_0 + (part_0.astype(F32) + swap(part_0).astype(F32)) + w0["down_bias"]).astype(F32)

    first_1, saved_1 = self_forward(hidden, w1)
    cross_normed = norm(first_1, cross_gain_w, cross_shift_w)
    cross_queries = split_heads(low(dot(cross_normed, cross_query_w)), captions)
    cross_scores = scores_of(cross_queries, image_keys)
    top = jnp.max(cross_scores, -1, keepdims=True)
    raised_scores = jnp.exp(cross_scores - top)
    total = jnp.sum(raised_scores, -1, keepdims=True)
    part_mix = low(mix(low(raised_scores), image_values))
    stats = jnp.concatenate([top, total], -1)
    other_mix, other_stats = swap(part_mix), swap(stats)
    best = jnp.maximum(top, other_stats[..., :1])
    own_weight = jnp.exp(top - best)
    other_weight = jnp.exp(other_stats[..., :1] - best)
    inverse = 1.0 / (total * own_weight + other_stats[..., 1:] * other_weight)
    own_factor, other_factor = own_weight * inverse, other_weight * inverse
    flip = lambda v: v.transpose(0, 2, 1, 3)
    cross_mixed = flip(own_factor) * part_mix.astype(F32) + flip(other_factor) * other_mix.astype(F32)
    cross_chances = raised_scores * own_factor
    cross_mixed_low = low(cross_mixed).reshape(rows, width)
    mid_1 = first_1 + dot(cross_mixed_low, cross_out_w)
    part_1, feed_saved_1 = feed_forward(mid_1, w1)
    own_part = pick(section, part_1[:, :half], part_1[:, half:])
    got_part = swap(pick(section, part_1[:, half:], part_1[:, :half]))
    own_cols = lambda v: pick(section, v[..., :half], v[..., half:])
    layer_out = own_cols(mid_1) + own_part.astype(F32) + got_part.astype(F32) + own_cols(w1["down_bias"])

    def feed_back(grad, current, saved, w):
        normed, raised, active = saved
        grad_low = low(grad)
        down_grad = dot_tn(active, grad_low)
        grad_raised = low(dot_nt(grad_low, w["down"]) * gelu_slope(raised))
        up_grad = dot_tn(normed, grad_raised)
        bias_grad = jnp.sum(grad_raised.astype(F32), 0)
        part = low(dot_nt(grad_raised, w["up"]))
        inner = part.astype(F32) + swap(part).astype(F32)
        step, gain_grad, shift_grad = norm_back(current, w["feed_gain"], inner)
        down_cols = jnp.concatenate([down_grad[i * width : (i + 1) * width] for i in range(folds)], 1)
        return step + grad, low(jnp.concatenate([up_grad, down_cols], 1)), (gain_grad, shift_grad, jnp.sum(grad, 0), bias_grad)

    def self_back(grad, inputs, saved, w):
        normed, queries, keys, values, chances, mixed_all = saved
        grad_low = low(grad)
        out_rows = pick(section, w["out"][:half], w["out"][half:])
        grad_mixed = split_heads(low(dot_nt(grad_low, out_rows)), captions)
        grad_chances = jnp.einsum("cqhd,ckhd->chqk", grad_mixed, values, preferred_element_type=F32)
        slope = chances * (grad_chances - jnp.sum(grad_chances * chances, -1, keepdims=True))
        query_part, key_part = attend_back(queries, keys, values, chances, slope)
        value_part = jnp.einsum("chqk,cqhd->ckhd", low(chances), grad_mixed, preferred_element_type=F32)
        grad_projected = low(jnp.concatenate([v.reshape(rows, half) for v in (query_part, key_part, value_part)], 1))
        into_grad = low(dot_tn(normed, grad_projected))
        part = low(dot_nt(grad_projected, w["into"]))
        inner = part.astype(F32) + swap(part).astype(F32)
        step, gain_grad, shift_grad = norm_back(inputs, w["self_gain"], inner)
        return step + grad, into_grad, grad_low, (gain_grad, shift_grad)

    def scatter(value):
        return lax.psum_scatter(value, "dp", scatter_dimension=0, tiled=True)

    cot32 = whole_cot.astype(F32)
    grad_mid_1, feed_grad_1, feed_vec_1 = feed_back(cot32, mid_1, feed_saved_1, w1)
    feed_got_1 = scatter(feed_grad_1)
    branch_low = low(grad_mid_1)
    own_mixed = own_cols(cross_mixed_low)
    cross_out_grad = dot_tn(own_mixed, branch_low)
    grad_mixed_flat = low(dot_nt(branch_low, cross_out_w))
    grad_mixed = split_heads(grad_mixed_flat, captions)
    grad_chances = jnp.einsum("cqhd,ckhd->chqk", grad_mixed, image_values, preferred_element_type=F32)
    delta = flip(jnp.sum(grad_mixed.astype(F32) * cross_mixed, -1, keepdims=True))
    slope = cross_chances * (grad_chances - delta)
    query_part, key_part = attend_back(cross_queries, image_keys, image_values, cross_chances, slope)
    value_part = jnp.einsum("chqk,cqhd->ckhd", low(cross_chances), grad_mixed, preferred_element_type=F32)
    query_low = low(query_part.reshape(rows, width))
    grad_queries = low(query_low.astype(F32) + swap(query_low).astype(F32))
    grad_pairs = low(jnp.concatenate([key_part.reshape(-1, width), value_part.reshape(-1, width)], 1))
    image_grad = dot_nt(grad_pairs, cross_keys_w).reshape(captions, half_image, width)
    keys_grad = dot_tn(flat_image, grad_pairs)
    keys_cols = jnp.concatenate([keys_grad[:half], keys_grad[half:]], 1)
    query_grad = dot_tn(own_cols(cross_normed), grad_queries)
    step, cross_gain_grad, cross_shift_grad = norm_back(first_1, cross_gain_w, dot_nt(grad_queries, cross_query_w))
    grad_first_1 = step + grad_mid_1
    cross_vec = jnp.stack([own_cols(cross_gain_grad), own_cols(cross_shift_grad)], 1)
    cross_got = scatter(low(jnp.concatenate([query_grad, cross_out_grad, keys_cols, cross_vec], 1)))

    grad_hidden, into_grad_1, g_low_1, self_vec_1 = self_back(grad_first_1, hidden, saved_1, w1)
    into_got_1 = scatter(into_grad_1)
    grad_mid_0, feed_grad_0, feed_vec_0 = feed_back(grad_hidden, mid_0, feed_saved_0, w0)
    feed_got_0 = scatter(feed_grad_0)
    text_grad, into_grad_0, g_low_0, self_vec_0 = self_back(grad_mid_0, text32, saved_0, w0)
    out_grad = dot_tn(pick(section, saved_0[5], saved_1[5]), pick(section, g_low_0, g_low_1))
    own_vec = [pick(section, a, b) for a, b in zip(self_vec_0 + feed_vec_0[:3], self_vec_1 + feed_vec_1[:3])]
    bias_cols = [v[3].reshape(folds, width)[i] for v in (feed_vec_0, feed_vec_1) for i in range(folds)]
    last_got = scatter(low(jnp.concatenate([into_grad_0, out_grad, jnp.stack(own_vec + bias_cols, 1)], 1)))
    into_got_0 = last_got[:, : 3 * half]
    out_got = last_got[:, 3 * half : 3 * half + width]
    vec_got = last_got[:, 3 * half + width :]
    bias_got = [vec_got[:, 5 + folds * l : 5 + folds * (l + 1)] for l in range(2)]

    def from_both(first, later):
        got = swap(pick(section, later, first))
        own = pick(section, first, later)
        return pick(section, own, got).astype(F32), pick(section, got, own).astype(F32)

    into_parts = from_both(into_got_0, into_got_1)
    feed_parts = from_both(feed_got_0, feed_got_1)
    bias_parts = from_both(*bias_got)
    heads_in_grad = jnp.stack([v.reshape(piece, 3, half) for v in into_parts], 2).reshape(1, piece, 6 * half)
    up_parts = [v[:, :half_ff].reshape(piece, folds, count, piece).transpose(0, 2, 1, 3) for v in feed_parts]
    up_grad = jnp.stack(up_parts, 2).reshape(1, piece, 2 * half_ff)
    down_parts = [v[:, half_ff:].reshape(piece, folds, width).transpose(1, 0, 2) for v in feed_parts]
    down_grad = jnp.stack(down_parts, 0).reshape(1, 2 * folds * piece, width)
    up_bias_grad = jnp.stack([v.T for v in bias_parts], 0).reshape(1, 2 * folds * piece)
    vec32 = vec_got.astype(F32).T
    keys_got = cross_got[:, 2 * width : 6 * width]
    pair_width = 2 * width
    own_keys = pick(section, keys_got[:, :pair_width], keys_got[:, pair_width:])
    got_keys = swap(pick(section, keys_got[:, pair_width:], keys_got[:, :pair_width]))
    cross32 = cross_got.astype(F32)
    return (
        layer_out,
        own_cols(text_grad),
        image_grad,
        vec32[0][None],
        vec32[1][None],
        heads_in_grad,
        out_got.astype(F32)[None],
        vec32[2][None],
        vec32[3][None],
        up_grad,
        up_bias_grad,
        down_grad,
        vec32[4][None],
        cross32[:, 6 * width],
        cross32[:, 6 * width + 1],
        cross32[:, :width],
        own_keys.astype(F32) + got_keys.astype(F32),
        cross32[:, width : 2 * width],
    )


def solution(mesh):
    placed = (
        P("dp", "section"),
        P("dp", "section", None),
        P("dp"),
        P("section", "dp"),
        P("section", "dp"),
        P("section", "dp", None),
        P("section", "dp", None),
        P("section", "dp"),
        P("section", "dp"),
        P("section", "dp", None),
        P("section", "dp"),
        P("section", "dp", None),
        P("section", "dp"),
        P(("section", "dp")),
        P(("section", "dp")),
        P(("section", "dp"), None),
        P(("section", "dp"), None),
        P(("section", "dp"), None),
        P("dp", "section"),
    )
    return jax.shard_map(
        body,
        mesh=mesh,
        in_specs=placed,
        out_specs=(P("dp", "section"), P("dp", "section"), P("dp", "section", None)) + placed[3:18],
        check_vma=False,
    )
```

```python
import functools

import jax
import jax.numpy as jnp
from jax import lax
from jax.experimental import pallas as pl
from jax.experimental.pallas import tpu as pltpu
from jax.sharding import PartitionSpec as P

HEAD_DIM = 64
PAIR = 2 * HEAD_DIM
EPS = 1e-05
MASKED = -1000000000.0
SCALE = HEAD_DIM**-0.5
F32 = jnp.float32
BF16 = jnp.bfloat16
MIB = 1 << 20


def swap(value):
    return lax.ppermute(value, "section", [(0, 1), (1, 0)])


def pick(section, first, later):
    return jnp.where(section == 0, first, later)


def side(own, other, section, axis):
    return jnp.concatenate([pick(section, own, other), pick(section, other, own)], axis)


def low(values):
    return values.astype(BF16)


def ring_chip(place, chips):
    return jnp.where(place < chips // 2, 2 * place, 2 * (chips - 1 - place) + 1)


def ring_steps(shift):
    count = lax.axis_size("dp")
    chips = count // 2
    order = list(range(0, chips, 2)) + list(range(chips - 1, 0, -2))
    return [(2 * order[i] + core, 2 * order[(i + shift) % chips] + core) for i in range(chips) for core in range(2)]


def ring_move(value, shift):
    return lax.ppermute(value, "dp", ring_steps(shift))


def core_swap(value):
    return lax.ppermute(value, "dp", [(i, i ^ 1) for i in range(lax.axis_size("dp"))])


def my_place():
    chips = lax.axis_size("dp") // 2
    me = lax.axis_index("dp")
    chip, core = me // 2, me % 2
    return jnp.where(chip % 2 == 0, chip // 2, chips - 1 - chip // 2), core


def assemble_kernel(places, spots, *refs):
    *sources, out, sems = refs
    copies = []
    for i, (ref, index) in enumerate(places):
        source = sources[ref] if index is None else sources[ref].at[index]
        copies.append(pltpu.make_async_copy(source, out.at[spots[i]], sems.at[i]))
    for copy in copies:
        copy.start()
    for copy in copies:
        copy.wait()


def gather_kernel(chips, spots, *refs):
    assemble_kernel([(i, None) for i in range(chips)] + [(chips, i) for i in range(chips)], spots, *refs)


def ring_gather(shard):
    chips = lax.axis_size("dp") // 2
    half = chips // 2
    rows, width = shard.shape
    cut = rows // 2
    got = {0: shard}
    for step in range(1, half):
        got[-step] = ring_move(got[1 - step], 1)
        got[step] = ring_move(got[step - 1], -1)
    got[half] = jnp.concatenate([ring_move(got[1 - half][:cut], 1), ring_move(got[half - 1][cut:], -1)], 0)
    steps = list(range(1 - half, half + 1))
    mine = [got[step] for step in steps]
    other = core_swap(jnp.stack(mine))
    place, core = my_place()
    chip = [ring_chip((place + step + chips) % chips, chips) for step in steps]
    spots = jnp.stack([2 * c + core for c in chip] + [2 * c + 1 - core for c in chip]).astype(jnp.int32)
    out = pl.pallas_call(
        functools.partial(gather_kernel, chips),
        out_shape=jax.ShapeDtypeStruct((2 * chips, rows, width), shard.dtype),
        in_specs=[pl.BlockSpec(memory_space=pltpu.SMEM)] + [pl.BlockSpec(memory_space=pl.ANY)] * (chips + 1),
        out_specs=pl.BlockSpec(memory_space=pltpu.VMEM),
        scratch_shapes=[pltpu.SemaphoreType.DMA((2 * chips,))],
        compiler_params=pltpu.CompilerParams(vmem_limit_bytes=16 * MIB),
        cost_estimate=pl.CostEstimate(flops=0, bytes_accessed=4 * chips * rows * width * 2, transcendentals=0),
        name="assemble",
    )(spots, *mine, other)
    return out.reshape(2 * chips * rows, width)


def ring_scatter(value):
    chips = lax.axis_size("dp") // 2
    half = chips // 2
    total, width = value.shape
    rows = total // (2 * chips)
    cut = rows // 2
    parts = value.reshape(chips, 2, rows, width)
    place, core = my_place()
    mine = lax.dynamic_index_in_dim(parts, core, 1, False)
    got = core_swap(lax.dynamic_index_in_dim(parts, 1 - core, 1, False))

    def own(step, begin=0, end=rows):
        chip = ring_chip((place + step + chips) % chips, chips)
        cut_out = lambda v: lax.dynamic_index_in_dim(v, chip, 0, False)[begin:end].astype(F32)
        return cut_out(mine) + cut_out(got)

    up = ring_move(low(own(half, 0, cut)), 1)
    down = ring_move(low(own(-half, cut, rows)), -1)
    pad = jnp.zeros((cut, width), F32)
    up_all = jnp.concatenate([up.astype(F32), jnp.zeros((rows - cut, width), F32)], 0)
    down_all = jnp.concatenate([pad, down.astype(F32)], 0)
    for step in range(half - 1, 0, -1):
        up_all = ring_move(low(own(step) + up_all), 1).astype(F32)
        down_all = ring_move(low(own(-step) + down_all), -1).astype(F32)
    return own(0) + up_all + down_all


def norm_unit(values):
    centred = values - jnp.mean(values, -1, keepdims=True)
    scale = lax.rsqrt(jnp.mean(centred * centred, -1, keepdims=True) + EPS)
    return centred * scale, scale


def norm_back(values, gain, grad):
    unit, scale = norm_unit(values)
    wide = grad * gain
    inner = wide - jnp.mean(wide, -1, keepdims=True) - unit * jnp.mean(wide * unit, -1, keepdims=True)
    return inner * scale, jnp.sum(grad * unit, 0, keepdims=True), jnp.sum(grad, 0, keepdims=True)


def dot(left, right):
    return jnp.dot(left, right, preferred_element_type=F32)


def dot_tn(left, right):
    return lax.dot_general(left, right, (((0,), (0,)), ((), ())), preferred_element_type=F32)


def dot_nt(left, right):
    return lax.dot_general(left, right, (((1,), (1,)), ((), ())), preferred_element_type=F32)


def gelu(values):
    return 0.5 * values * (1.0 + lax.erf(values * 0.5**0.5))


def gelu_slope(values):
    return 0.5 * (1.0 + lax.erf(values * 0.5**0.5)) + values * jnp.exp(-0.5 * values * values) * 0.3989422804014327


def first_head(rows):
    return lax.broadcasted_iota(jnp.int32, (rows, PAIR), 1) < HEAD_DIM


def stacked(pair):
    mask = first_head(pair.shape[0])
    zero = jnp.zeros_like(pair)
    return jnp.concatenate([jnp.where(mask, pair, zero), jnp.where(mask, zero, pair)], 0)


def unstacked(rows):
    half = rows.shape[0] // 2
    return jnp.where(first_head(half), rows[:half], rows[half:])


def keep_mask(length, slots):
    query = lax.broadcasted_iota(jnp.int32, (2 * slots, slots), 0) % slots
    key = lax.broadcasted_iota(jnp.int32, (2 * slots, slots), 1)
    return (key <= query) & (key < length)


def self_chances(queries, keys, keep):
    scores = jnp.where(keep, dot_nt(queries, keys) * SCALE, MASKED)
    raised = jnp.exp(scores - jnp.max(scores, -1, keepdims=True))
    return raised / jnp.sum(raised, -1, keepdims=True)


def call(kernel, ins, outs, scratch=(), vmem=48, name=None, flops=0):
    specs, arrays = [], []
    for array, spec in ins:
        if spec is None:
            zeros = (0,) * array.ndim
            specs.append(pl.BlockSpec(array.shape, lambda i, z=zeros: z))
        elif spec == "s":
            specs.append(pl.BlockSpec(memory_space=pltpu.SMEM))
        else:
            block, index = spec
            specs.append(pl.BlockSpec(block, lambda i, z=index: z))
        arrays.append(array)
    shapes = [jax.ShapeDtypeStruct(*o) for o in outs]
    out_specs = [pl.BlockSpec(o.shape, lambda i, z=(0,) * len(o.shape): z) for o in shapes]
    moved = sum(a.size * a.dtype.itemsize for a in arrays) + sum(o.size * o.dtype.itemsize for o in shapes)
    return pl.pallas_call(
        kernel,
        grid=(1,),
        in_specs=specs,
        out_specs=out_specs,
        out_shape=shapes,
        scratch_shapes=list(scratch),
        compiler_params=pltpu.CompilerParams(vmem_limit_bytes=vmem * MIB),
        cost_estimate=pl.CostEstimate(flops=flops, bytes_accessed=moved, transcendentals=0),
        name=name,
    )(*arrays)


SELF_GAIN, SELF_SHIFT, FEED_GAIN, FEED_SHIFT, DOWN_BIAS, UP_BIAS = range(6)
LAYER_VECS = 7
CROSS_GAIN, CROSS_SHIFT = 14, 15


def vec(ref, row):
    return ref[row : row + 1, :]


def self_part(values, layer, lengths, vecs, wq, wk, wv, normed_ref, projected, mixed_ref):
    base = LAYER_VECS * layer
    unit, _ = norm_unit(values)
    normed = low(unit * vec(vecs, base + SELF_GAIN) + vec(vecs, base + SELF_SHIFT))
    normed_ref[...] = normed
    half = wq.shape[1]
    for i, weight in enumerate((wq, wk, wv)):
        projected[:, i * half : (i + 1) * half] = low(dot(normed, weight[...]))
    captions = lengths.shape[0]
    slots = values.shape[0] // captions
    for c in range(captions):
        keep = keep_mask(lengths[c], slots)
        here = slice(c * slots, (c + 1) * slots)
        for j in range(half // PAIR):
            q, k, v = (projected[here, i * half + j * PAIR : i * half + (j + 1) * PAIR] for i in range(3))
            chances = self_chances(stacked(q), k, keep)
            mixed_ref[here, j * PAIR : (j + 1) * PAIR] = low(unstacked(dot(low(chances), v)))


def self_first_kernel(lengths, text, vecs, wq, wk, wv, normed, projected, mixed):
    self_part(text[...].astype(F32), 0, lengths, vecs, wq, wk, wv, normed, projected, mixed)


def self_second_kernel(lengths, middle, own, other, vecs, wq, wk, wv, hidden, normed, projected, mixed):
    total = middle[...] + (own[...].astype(F32) + other[...].astype(F32)) + vec(vecs, DOWN_BIAS)
    hidden[...] = low(total)
    self_part(hidden[...].astype(F32), 1, lengths, vecs, wq, wk, wv, normed, projected, mixed)


def add_heads_out(values, section, own, other, out):
    half = own.shape[1]
    own_rows = pl.multiple_of(section * half, half)
    other_rows = pl.multiple_of((1 - section) * half, half)
    return values + (dot(own[...], out[pl.ds(own_rows, half), :]) + dot(other[...], out[pl.ds(other_rows, half), :]))


def feed_part(middle, layer, vecs, up, down, normed_ref, raised_ref, active_ref):
    base = LAYER_VECS * layer
    width = middle.shape[1]
    unit, _ = norm_unit(middle)
    normed = low(unit * vec(vecs, base + FEED_GAIN) + vec(vecs, base + FEED_SHIFT))
    normed_ref[...] = normed
    total = jnp.zeros_like(middle)
    for i in range(up.shape[1] // width):
        here = slice(i * width, (i + 1) * width)
        raised = dot(normed, up[:, here]) + vec(vecs, base + UP_BIAS + i)
        raised_ref[:, here] = raised
        active = low(gelu(raised))
        active_ref[:, here] = active
        total += dot(active, down[:, here])
    return low(total)


def feed_first_kernel(section, text, own, other, vecs, out, up, down, middle, normed, raised, active, part):
    values = add_heads_out(text[...].astype(F32), section[0], own, other, out)
    middle[...] = values
    part[...] = feed_part(values, 0, vecs, up, down, normed, raised, active)


def cross_kernel(section, hidden, own, other, vecs, out, query, pairs, first, normed_ref, queries, part, stats):
    values = add_heads_out(hidden[...].astype(F32), section[0], own, other, out)
    first[...] = values
    unit, _ = norm_unit(values)
    normed = low(unit * vec(vecs, CROSS_GAIN) + vec(vecs, CROSS_SHIFT))
    normed_ref[...] = normed
    queries[...] = low(dot(normed, query[...]))
    rows, width = values.shape
    captions = pairs.shape[0]
    slots = rows // captions
    lane = lax.broadcasted_iota(jnp.int32, (slots, PAIR), 1)

    def one(c, carry):
        here = pl.ds(pl.multiple_of(c * slots, slots), slots)
        record = jnp.zeros((slots, PAIR), F32)
        for j in range(width // PAIR):
            cols = slice(j * PAIR, (j + 1) * PAIR)
            k = pairs[c, :, cols]
            v = pairs[c, :, width + j * PAIR : width + (j + 1) * PAIR]
            scores = dot_nt(stacked(queries[here, cols]), k) * SCALE
            top = jnp.max(scores, -1, keepdims=True)
            raised = jnp.exp(scores - top)
            total = jnp.sum(raised, -1, keepdims=True)
            part[here, cols] = low(unstacked(dot(low(raised), v)))
            for i in range(2):
                block = slice(i * slots, (i + 1) * slots)
                record = jnp.where(lane == 2 * j + i, top[block], record)
                record = jnp.where(lane == HEAD_DIM + 2 * j + i, total[block], record)
        stats[here, :] = record
        return carry

    lax.fori_loop(0, captions, one, 0)


def feed_second_kernel(first, own, other, own_stats, other_stats, vecs, out, up, down, middle, mixed, factor, normed, raised, active, part):
    top, top_other = own_stats[...], other_stats[...]
    total, total_other = pltpu.roll(top, HEAD_DIM, 1), pltpu.roll(top_other, HEAD_DIM, 1)
    best = jnp.maximum(top, top_other)
    own_weight, other_weight = jnp.exp(top - best), jnp.exp(top_other - best)
    inverse = 1.0 / (total * own_weight + total_other * other_weight)
    own_factor, other_factor = own_weight * inverse, other_weight * inverse
    factor[...] = own_factor
    rows, width = first.shape
    mask = first_head(rows)
    for j in range(width // PAIR):
        cols = slice(j * PAIR, (j + 1) * PAIR)
        spread = lambda f: jnp.where(mask, f[:, 2 * j : 2 * j + 1], f[:, 2 * j + 1 : 2 * j + 2])
        mixed[:, cols] = low(spread(own_factor) * own[:, cols].astype(F32) + spread(other_factor) * other[:, cols].astype(F32))
    values = first[...] + dot(mixed[...], out[...])
    middle[...] = values
    part[...] = feed_part(values, 1, vecs, up, down, normed, raised, active)


def feed_back(grad, layer, vecs, up, down, raised, bias_grad, down_bias_grad, slope_ref, part):
    width = grad.shape[1]
    grad_low = low(grad)
    down_bias_grad[...] = jnp.sum(grad, 0, keepdims=True)
    total = jnp.zeros(grad.shape, F32)
    for i in range(up.shape[1] // width):
        here = slice(i * width, (i + 1) * width)
        grad_raised = low(dot_nt(grad_low, down[:, here]) * gelu_slope(raised[:, here]))
        slope_ref[:, here] = grad_raised
        bias_grad[i : i + 1, :] = jnp.sum(grad_raised.astype(F32), 0, keepdims=True)
        total += dot_nt(grad_raised, up[:, here])
    part[...] = low(total)


def feed_back_last_kernel(cot, vecs, up, down, raised, bias_grad, down_bias_grad, slope, part):
    feed_back(cot[...].astype(F32), 1, vecs, up, down, raised, bias_grad, down_bias_grad, slope, part)


def cross_back_kernel(cot, own, other, middle, vecs, out, queries, pairs, stats, factor, mixed, grad_ref, low_ref, vec_grad, query_part, grad_pairs, grad_mixed):
    base = LAYER_VECS
    inner = own[...].astype(F32) + other[...].astype(F32)
    step, gain_grad, shift_grad = norm_back(middle[...], vec(vecs, base + FEED_GAIN), inner)
    vec_grad[0:1, :] = gain_grad
    vec_grad[1:2, :] = shift_grad
    grad = step + cot[...].astype(F32)
    grad_ref[...] = grad
    low_ref[...] = low(grad)
    grad_mixed[...] = low(dot_nt(low_ref[...], out[...]))
    rows, width = grad.shape
    captions = pairs.shape[0]
    slots = rows // captions
    mask = first_head(slots)

    def one(c, carry):
        here = pl.ds(pl.multiple_of(c * slots, slots), slots)
        tops, factors = stats[here, :], factor[here, :]
        for j in range(width // PAIR):
            cols = slice(j * PAIR, (j + 1) * PAIR)
            later = slice(width + j * PAIR, width + (j + 1) * PAIR)
            k, v = pairs[c, :, cols], pairs[c, :, later]
            two = lambda a: jnp.concatenate([a[:, 2 * j : 2 * j + 1], a[:, 2 * j + 1 : 2 * j + 2]], 0)
            q = stacked(queries[here, cols])
            grad_pair = grad_mixed[here, cols]
            both = grad_pair.astype(F32) * mixed[here, cols].astype(F32)
            delta = jnp.concatenate([jnp.sum(jnp.where(mask, both, 0.0), -1, keepdims=True), jnp.sum(jnp.where(mask, 0.0, both), -1, keepdims=True)], 0)
            chances = jnp.exp(dot_nt(q, k) * SCALE - two(tops)) * two(factors)
            grads = stacked(grad_pair)
            slope = low(chances * (dot_nt(grads, v) - delta))
            query_part[here, cols] = low(unstacked(dot(slope, k)) * SCALE)
            grad_pairs[c, :, cols] = low(dot_tn(slope, q) * SCALE)
            grad_pairs[c, :, later] = low(dot_tn(low(chances), grads))
        return carry

    lax.fori_loop(0, captions, one, 0)


def self_back(grad, section, lengths, out, wq, wk, wv, projected, low_ref, grad_projected, grad_mixed):
    half = wq.shape[1]
    low_ref[...] = low(grad)
    rows = pl.multiple_of(section * half, half)
    grad_mixed[...] = low(dot_nt(low_ref[...], out[pl.ds(rows, half), :]))
    captions = lengths.shape[0]
    slots = grad.shape[0] // captions
    for c in range(captions):
        keep = keep_mask(lengths[c], slots)
        here = slice(c * slots, (c + 1) * slots)
        for j in range(half // PAIR):
            cols = [slice(i * half + j * PAIR, i * half + (j + 1) * PAIR) for i in range(3)]
            q, k, v = (projected[here, cols[i]] for i in range(3))
            q = stacked(q)
            chances = self_chances(q, k, keep)
            grads = stacked(grad_mixed[here, cols[0]])
            grad_chances = dot_nt(grads, v)
            slope = low(chances * (grad_chances - jnp.sum(grad_chances * chances, -1, keepdims=True)))
            grad_projected[here, cols[0]] = low(unstacked(dot(slope, k)) * SCALE)
            grad_projected[here, cols[1]] = low(dot_tn(slope, q) * SCALE)
            grad_projected[here, cols[2]] = low(dot_tn(low(chances), grads))
    total = jnp.zeros(grad.shape, F32)
    for i, weight in enumerate((wq, wk, wv)):
        total += dot_nt(grad_projected[:, i * half : (i + 1) * half], weight[...])
    return total


def self_back_second_kernel(section, lengths, grad_middle, own, other, first, vecs, query, out, wq, wk, wv, projected, grad_ref, low_ref, grad_queries, grad_projected, part, vec_grad, grad_mixed):
    grad_queries[...] = low(own[...].astype(F32) + other[...].astype(F32))
    inner = dot_nt(grad_queries[...], query[...])
    step, gain_grad, shift_grad = norm_back(first[...], vec(vecs, CROSS_GAIN), inner)
    vec_grad[0:1, :] = gain_grad
    vec_grad[1:2, :] = shift_grad
    grad = step + grad_middle[...]
    grad_ref[...] = grad
    part[...] = low(self_back(grad, section[0], lengths, out, wq, wk, wv, projected, low_ref, grad_projected, grad_mixed))


def feed_back_first_kernel(grad_first, own, other, hidden, vecs, up, down, raised, grad_ref, vec_grad, bias_grad, down_bias_grad, slope, part):
    inner = own[...].astype(F32) + other[...].astype(F32)
    step, gain_grad, shift_grad = norm_back(hidden[...].astype(F32), vec(vecs, LAYER_VECS + SELF_GAIN), inner)
    vec_grad[0:1, :] = gain_grad
    vec_grad[1:2, :] = shift_grad
    grad = low(step + grad_first[...]).astype(F32)
    grad_ref[...] = grad
    feed_back(grad, 0, vecs, up, down, raised, bias_grad, down_bias_grad, slope, part)


def self_back_first_kernel(section, lengths, grad_hidden, own, other, middle, text, vecs, out, wq, wk, wv, projected, grad_ref, low_ref, grad_projected, part, vec_grad, grad_mixed):
    inner = own[...].astype(F32) + other[...].astype(F32)
    step, gain_grad, shift_grad = norm_back(middle[...], vec(vecs, FEED_GAIN), inner)
    vec_grad[0:1, :] = gain_grad
    vec_grad[1:2, :] = shift_grad
    grad = step + grad_hidden[...]
    grad_ref[...] = grad
    total = self_back(grad, section[0], lengths, out, wq, wk, wv, projected, low_ref, grad_projected, grad_mixed)
    part[...] = low(total)
    unit, _ = norm_unit(text[...].astype(F32))
    vec_grad[2:3, :] = jnp.sum(total * unit, 0, keepdims=True)
    vec_grad[3:4, :] = jnp.sum(total, 0, keepdims=True)


def text_grad_kernel(section, grad_middle, own, other, text, vecs, out):
    inner = own[...].astype(F32) + other[...].astype(F32)
    step, _, _ = norm_back(text[...].astype(F32), vec(vecs, SELF_GAIN), inner)
    total = step + grad_middle[...]
    half = out.shape[1]
    out[...] = jnp.where(section[0] == 0, total[:, :half], total[:, half:])


def products_kernel(pieces, *refs):
    out = refs[-1]
    offset = 0
    for left, right, swapped in pieces:
        lhs, rhs = refs[left], refs[right]
        block = 384
        if swapped:
            rows = out.shape[0]
            for i in range(lhs.shape[1] // rows):
                for j in range(rhs.shape[1] // block):
                    out[:, offset : offset + block] = low(dot_tn(lhs[:, i * rows : (i + 1) * rows], rhs[:, j * block : (j + 1) * block]))
                    offset += block
        else:
            for j in range(rhs.shape[1] // block):
                out[:, offset : offset + block] = low(dot_tn(lhs[...], rhs[:, j * block : (j + 1) * block]))
                offset += block


def products(pieces, arrays, name):
    rows = min(arrays[left].shape[1] for left, _, _ in pieces)
    width = sum(arrays[left].shape[1] // rows * arrays[right].shape[1] for left, right, _ in pieces)
    flops = 2 * arrays[0].shape[0] * rows * width
    return call(functools.partial(products_kernel, pieces), [(a, None) for a in arrays], [((rows, width), BF16)], name=name, flops=flops)[0]


def body(
    text,
    image,
    lengths,
    self_gain,
    self_shift,
    heads_in,
    heads_out,
    feed_gain,
    feed_shift,
    up_weight,
    up_bias,
    down_weight,
    down_bias,
    cross_gain,
    cross_shift,
    cross_query,
    cross_keys,
    cross_out,
    cotangent,
):
    section = lax.axis_index("section")
    section_ref = section.astype(jnp.int32).reshape(1)
    count = lax.axis_size("dp")
    captions, half_image, width = image.shape
    rows = text.shape[0]
    piece = heads_in.shape[1]
    cross_piece = cross_query.shape[0]
    half = width // 2
    folds = down_weight.shape[1] // (2 * piece)
    half_ff = folds * width

    def attn_rows(index):
        return heads_in[0].reshape(piece, 3, 2, half)[:, :, index].reshape(piece, 3 * half)

    def feed_rows(index):
        up = up_weight[0].reshape(piece, count, 2, folds, piece)[:, :, index]
        up = up.transpose(0, 2, 1, 3).reshape(piece, half_ff)
        down = down_weight[0].reshape(2, folds, piece, width)[index]
        return jnp.concatenate([up] + [down[i] for i in range(folds)], 1)

    def vec_rows(index):
        bias = up_bias[0].reshape(2, folds, piece)[index]
        return jnp.stack([self_gain[0], self_shift[0], feed_gain[0], feed_shift[0], down_bias[0]] + [bias[i] for i in range(folds)], 1)

    def both_layers(make):
        first, later = make(0), make(1)
        own, got = pick(section, first, later), swap(pick(section, later, first))
        return pick(section, own, got), pick(section, got, own)

    pad = jnp.zeros((piece, 128 - 2 * LAYER_VECS), BF16)
    attn_0, attn_1 = both_layers(lambda i: jnp.concatenate([heads_out[0], attn_rows(i), vec_rows(i)], 1))
    text_all = side(text, swap(text), section, 1)
    feed_0, feed_1 = both_layers(feed_rows)
    cot_all = side(cotangent, swap(cotangent), section, 1)
    core_cols = width + 3 * half
    vec_cols = jnp.concatenate([attn_0[:, core_cols:], attn_1[:, core_cols:], pad], 1)

    cross_own = jnp.concatenate([cross_keys, cross_query, cross_out], 1)
    cross_vec = jnp.stack([cross_gain, cross_shift], 1)
    cross_wide = jnp.concatenate([cross_own, cross_vec, jnp.zeros((cross_piece, 126), BF16)], 1)
    own_cross = ring_gather(cross_wide)
    piece_a = ring_gather(jnp.concatenate([attn_0[:, :core_cols], vec_cols], 1))
    other_cross = swap(own_cross)
    cross_full = side(own_cross, other_cross, section, 0)
    piece_f0 = ring_gather(feed_0)
    piece_d = ring_gather(attn_1[:, :core_cols])
    piece_f1 = ring_gather(feed_1)
    vecs = jnp.concatenate([piece_a[:, core_cols : core_cols + 2 * LAYER_VECS], cross_full[:, 4 * width : 4 * width + 2]], 1).astype(F32).T
    keys_w = cross_full[:, : 2 * width]

    def attn_specs(array):
        return [(array, ((width, half), (0, 2 + i))) for i in range(3)]

    def out_spec(array):
        return (array, ((width, width), (0, 0)))

    def feed_specs(array):
        return [(array, ((width, half_ff), (0, 0))), (array, ((width, half_ff), (0, 1)))]

    query_spec = (cross_full, ((width, width), (0, 2)))
    cross_out_spec = (cross_full, ((width, width), (0, 3)))

    shape_f = ((rows, width), F32)
    shape_b = ((rows, width), BF16)
    shape_half = ((rows, half), BF16)
    shape_qkv = ((rows, 3 * half), BF16)
    shape_raised = ((rows, half_ff), F32)
    shape_active = ((rows, half_ff), BF16)
    lens = (lengths, "s")
    sec = (section_ref, "s")
    whole = lambda a: (a, None)

    pairs = low(dot(image.reshape(captions * half_image, width), keys_w)).reshape(captions, half_image, 2 * width)
    normed_a0, qkv_0, mixed_0 = call(
        self_first_kernel, [lens, whole(text_all), whole(vecs)] + attn_specs(piece_a), [shape_b, shape_qkv, shape_half], name="self_0", flops=2 * rows * width * 3 * half
    )
    other_0 = swap(mixed_0)
    middle_0, normed_f0, raised_0, active_0, part_0 = call(
        feed_first_kernel,
        [sec, whole(text_all), whole(mixed_0), whole(other_0), whole(vecs), out_spec(piece_a)] + feed_specs(piece_f0),
        [shape_f, shape_b, shape_raised, shape_active, shape_b],
        name="feed_0", flops=4 * rows * width * half_ff,
    )
    part_0_other = swap(part_0)
    hidden, normed_a1, qkv_1, mixed_1 = call(
        self_second_kernel,
        [lens, whole(middle_0), whole(part_0), whole(part_0_other), whole(vecs)] + attn_specs(piece_d),
        [shape_b, shape_b, shape_qkv, shape_half],
        name="self_1", flops=2 * rows * width * 3 * half,
    )
    other_1 = swap(mixed_1)
    first_1, normed_c, queries, cross_part, stats = call(
        cross_kernel,
        [sec, whole(hidden), whole(mixed_1), whole(other_1), whole(vecs), out_spec(piece_d), query_spec, whole(pairs)],
        [shape_f, shape_b, shape_b, shape_b, ((rows, 128), F32)],
        name="cross_1", flops=4 * rows * width * width,
    )
    cross_part_other, stats_other = swap(cross_part), swap(stats)
    middle_1, cross_mixed, factor, normed_f1, raised_1, active_1, part_1 = call(
        feed_second_kernel,
        [whole(first_1), whole(cross_part), whole(cross_part_other), whole(stats), whole(stats_other), whole(vecs), cross_out_spec] + feed_specs(piece_f1),
        [shape_f, shape_b, ((rows, 128), F32), shape_b, shape_raised, shape_active, shape_b],
        name="feed_1", flops=4 * rows * width * half_ff,
    )
    own_cols = lambda v: pick(section, v[..., :half], v[..., half:])
    got_part = swap(pick(section, part_1[:, half:], part_1[:, :half]))
    layer_out = own_cols(middle_1) + (own_cols(part_1).astype(F32) + got_part.astype(F32)) + own_cols(vecs[LAYER_VECS + DOWN_BIAS])

    shape_vec = ((8, width), F32)
    shape_bias = ((folds, width), F32)
    shape_one = ((1, width), F32)
    scratch_half = [pltpu.VMEM((rows, half), BF16)]
    bias_grad_1, down_bias_grad_1, slope_1, back_1 = call(
        feed_back_last_kernel, [whole(cot_all), whole(vecs)] + feed_specs(piece_f1) + [whole(raised_1)], [shape_bias, shape_one, shape_active, shape_b], name="feed_back_1", flops=4 * rows * width * half_ff
    )
    back_1_other = swap(back_1)
    feed_grad_1 = products([(0, 1, False), (2, 3, True)], [normed_f1, slope_1, active_1, cot_all], "feed_grads_1")
    feed_got_1 = ring_scatter(feed_grad_1)
    grad_middle_1, grad_low_1, feed_vec_1, query_part, grad_pairs = call(
        cross_back_kernel,
        [whole(cot_all), whole(back_1), whole(back_1_other), whole(middle_1), whole(vecs), cross_out_spec, whole(queries), whole(pairs), whole(stats), whole(factor), whole(cross_mixed)],
        [shape_f, shape_b, shape_vec, shape_b, ((captions, half_image, 2 * width), BF16)],
        scratch=[pltpu.VMEM((rows, width), BF16)],
        name="cross_back", flops=4 * rows * width * width,
    )
    query_part_other = swap(query_part)
    flat_pairs = grad_pairs.reshape(captions * half_image, 2 * width)
    flat_image = image.reshape(captions * half_image, width)
    image_grad = dot_nt(flat_pairs, keys_w).reshape(captions, half_image, width)
    keys_grad = low(dot_tn(flat_image, flat_pairs))
    grad_first_1, head_low_1, grad_queries, grad_qkv_1, self_back_1, cross_vec_1 = call(
        self_back_second_kernel,
        [sec, lens, whole(grad_middle_1), whole(query_part), whole(query_part_other), whole(first_1), whole(vecs), query_spec, out_spec(piece_d)]
        + attn_specs(piece_d) + [whole(qkv_1)],
        [shape_f, shape_b, shape_b, shape_qkv, shape_b, shape_vec],
        scratch=scratch_half, name="self_back_1", flops=4 * rows * width * 3 * half,
    )
    self_back_1_other = swap(self_back_1)
    cross_grad = products([(0, 1, False), (2, 3, False)], [own_cols(normed_c), grad_queries, own_cols(cross_mixed), grad_low_1], "cross_grads")
    cross_vec_cols = jnp.stack([own_cols(cross_vec_1[0]), own_cols(cross_vec_1[1])], 1)
    cross_pack = jnp.concatenate([cross_grad, keys_grad[:half], keys_grad[half:], low(cross_vec_cols), jnp.zeros((half, 126), BF16)], 1)
    cross_got = ring_scatter(cross_pack)
    into_grad_1 = products([(0, 1, False)], [normed_a1, grad_qkv_1], "into_grads_1")
    into_got_1 = ring_scatter(into_grad_1)
    grad_hidden, self_vec_1, bias_grad_0, down_bias_grad_0, slope_0, back_0 = call(
        feed_back_first_kernel,
        [whole(grad_first_1), whole(self_back_1), whole(self_back_1_other), whole(hidden), whole(vecs)] + feed_specs(piece_f0) + [whole(raised_0)],
        [shape_f, shape_vec, shape_bias, shape_one, shape_active, shape_b],
        name="feed_back_0", flops=4 * rows * width * half_ff,
    )
    back_0_other = swap(back_0)
    feed_grad_0 = products([(0, 1, False), (2, 3, True)], [normed_f0, slope_0, active_0, low(grad_hidden)], "feed_grads_0")
    feed_got_0 = ring_scatter(feed_grad_0)
    grad_middle_0, head_low_0, grad_qkv_0, self_back_0, feed_vec_0 = call(
        self_back_first_kernel,
        [sec, lens, whole(grad_hidden), whole(back_0), whole(back_0_other), whole(middle_0), whole(text_all), whole(vecs), out_spec(piece_a)]
        + attn_specs(piece_a) + [whole(qkv_0)],
        [shape_f, shape_b, shape_qkv, shape_b, shape_vec],
        scratch=scratch_half, name="self_back_0", flops=4 * rows * width * 3 * half,
    )
    self_back_0_other = swap(self_back_0)
    mixed_all = pick(section, side(mixed_0, other_0, section, 1), side(mixed_1, other_1, section, 1))
    head_low = pick(section, head_low_0, head_low_1)
    last_grad = products([(0, 1, False), (2, 3, False)], [normed_a0, grad_qkv_0, mixed_all, head_low], "last_grads")
    (text_grad,) = call(
        text_grad_kernel, [sec, whole(grad_middle_0), whole(self_back_0), whole(self_back_0_other), whole(text_all), whole(vecs)], [((rows, half), F32)], name="text_grad"
    )
    vec_rows_out = jnp.concatenate(
        [
            feed_vec_0[2:4],
            jnp.where(section == 0, 0.0, self_vec_1[:2]),
            pick(section, feed_vec_0[:2], feed_vec_1[:2]),
            pick(section, down_bias_grad_0, down_bias_grad_1),
            bias_grad_0,
            bias_grad_1,
        ],
        0,
    )
    vec_grads = jnp.concatenate([low(vec_rows_out).T, jnp.zeros((width, 128 - vec_rows_out.shape[0]), BF16)], 1)
    last_got = ring_scatter(jnp.concatenate([last_grad, vec_grads], 1))
    into_got_0 = last_got[:, : 3 * half]
    out_got = last_got[:, 3 * half : 3 * half + width]
    vec_got = last_got[:, 3 * half + width :]

    def from_both(first, later):
        own, got = pick(section, first, later), swap(low(pick(section, later, first))).astype(F32)
        return pick(section, own, got), pick(section, got, own)

    into_parts = from_both(into_got_0, into_got_1)
    feed_parts = from_both(feed_got_0, feed_got_1)
    zeros_2 = jnp.zeros((piece, 2), F32)
    vec_first = jnp.concatenate([vec_got[:, 0:2], vec_got[:, 7 : 7 + folds]], 1)
    vec_later = jnp.concatenate([vec_got[:, 2:4], vec_got[:, 7 + folds : 7 + 2 * folds]], 1)
    vec_parts = from_both(vec_first, vec_later)
    self_vec = vec_parts[0][:, :2] + vec_parts[1][:, :2]
    heads_in_grad = jnp.stack([v.reshape(piece, 3, half) for v in into_parts], 2).reshape(1, piece, 6 * half)
    up_parts = [v[:, :half_ff].reshape(piece, folds, count, piece).transpose(0, 2, 1, 3) for v in feed_parts]
    up_grad = jnp.stack(up_parts, 2).reshape(1, piece, 2 * half_ff)
    down_parts = [v[:, half_ff:].reshape(piece, folds, width).transpose(1, 0, 2) for v in feed_parts]
    down_grad = jnp.stack(down_parts, 0).reshape(1, 2 * folds * piece, width)
    up_bias_grad = jnp.stack([v[:, 2:].T for v in vec_parts], 0).reshape(1, 2 * folds * piece)
    keys_got = cross_got[:, 2 * width : 6 * width]
    own_keys = pick(section, keys_got[:, : 2 * width], keys_got[:, 2 * width :])
    got_keys = swap(low(pick(section, keys_got[:, 2 * width :], keys_got[:, : 2 * width])))
    return (
        layer_out,
        text_grad,
        image_grad,
        self_vec[:, 0][None],
        self_vec[:, 1][None],
        heads_in_grad,
        out_got[None],
        vec_got[:, 4][None],
        vec_got[:, 5][None],
        up_grad,
        up_bias_grad,
        down_grad,
        vec_got[:, 6][None],
        cross_got[:, 6 * width],
        cross_got[:, 6 * width + 1],
        cross_got[:, :width],
        own_keys + got_keys.astype(F32),
        cross_got[:, width : 2 * width],
    )


def solution(mesh):
    placed = (
        P("dp", "section"),
        P("dp", "section", None),
        P("dp"),
        P("section", "dp"),
        P("section", "dp"),
        P("section", "dp", None),
        P("section", "dp", None),
        P("section", "dp"),
        P("section", "dp"),
        P("section", "dp", None),
        P("section", "dp"),
        P("section", "dp", None),
        P("section", "dp"),
        P(("section", "dp")),
        P(("section", "dp")),
        P(("section", "dp"), None),
        P(("section", "dp"), None),
        P(("section", "dp"), None),
        P("dp", "section"),
    )
    return jax.shard_map(
        body,
        mesh=mesh,
        in_specs=placed,
        out_specs=(P("dp", "section"), P("dp", "section"), P("dp", "section", None)) + placed[3:18],
        check_vma=False,
    )
```

```python
import functools

import jax
import jax.numpy as jnp
from jax import lax
from jax.experimental import pallas as pl
from jax.experimental.pallas import tpu as pltpu
from jax.sharding import PartitionSpec as P

HEAD_DIM = 64
PAIR = 2 * HEAD_DIM
QUAD = 4 * HEAD_DIM
EPS = 1e-05
MASKED = -1000000000.0
SCALE = HEAD_DIM**-0.5
F32 = jnp.float32
BF16 = jnp.bfloat16
MIB = 1 << 20


def swap(value):
    return lax.ppermute(value, "section", [(0, 1), (1, 0)])


def pick(section, first, later):
    return jnp.where(section == 0, first, later)


def side(own, other, section, axis):
    return jnp.concatenate([pick(section, own, other), pick(section, other, own)], axis)


def low(values):
    return values.astype(BF16)


def ring_chip(place, chips):
    return jnp.where(place < chips // 2, 2 * place, 2 * (chips - 1 - place) + 1)


def ring_order():
    chips = lax.axis_size("dp") // 2
    return list(range(0, chips, 2)) + list(range(chips - 1, 0, -2))


def ring_steps(shift):
    order = ring_order()
    chips = len(order)
    return [(2 * order[i] + core, 2 * order[(i + shift) % chips] + core) for i in range(chips) for core in range(2)]


def ring_move(value, shift):
    return lax.ppermute(value, "dp", ring_steps(shift))


def core_swap(value):
    return lax.ppermute(value, "dp", [(i, i ^ 1) for i in range(lax.axis_size("dp"))])


def my_place():
    chips = lax.axis_size("dp") // 2
    me = lax.axis_index("dp")
    chip, core = me // 2, me % 2
    return jnp.where(chip % 2 == 0, chip // 2, chips - 1 - chip // 2), core


def pack_kernel(cut, spots, *refs):
    *sources, out = refs
    chips = out.shape[0]
    for i, source in enumerate(sources[: chips - 1]):
        out[spots[i]] = source[...]
    out[spots[chips - 1], :, :cut] = sources[chips - 1][...]
    out[spots[chips - 1], :, cut:] = sources[chips][...]


def join_kernel(place, mine, other, out):
    core = place[1]
    for chip in range(mine.shape[0]):
        out[2 * chip + core] = mine[chip]
        out[2 * chip + 1 - core] = other[chip]


def reorder_kernel(order, parts, place, source, *outs):
    rows = source.shape[0] // len(order)
    width = sum(out.shape[1] for out in outs)
    for part in range(parts):
        offset = part * width
        for out in outs:
            for i, spot in enumerate(order):
                begin = part * source.shape[0] + spot * rows
                out[begin : begin + rows, :] = source[i * rows : (i + 1) * rows, offset : offset + out.shape[1]]
            offset += out.shape[1]


class Gather:
    def __init__(self, shard):
        self.chips = lax.axis_size("dp") // 2
        self.steps = self.chips // 2
        self.rows, self.width = shard.shape
        self.cut = self.width // 256 * 128
        self.got = {0: shard}
        self.step = 0
        self.last = ()

    def front(self):
        return self.last or (self.got[-self.step], self.got[self.step])

    def put_front(self, values):
        if self.last:
            self.last = values
        else:
            self.got[-self.step], self.got[self.step] = values

    def move(self):
        self.step += 1
        up, down = self.got[1 - self.step], self.got[self.step - 1]
        if self.step < self.steps:
            self.got[-self.step], self.got[self.step] = ring_move(up, 1), ring_move(down, -1)
        else:
            self.last = (ring_move(up[:, : self.cut], 1), ring_move(down[:, self.cut :], -1))

    def pack(self):
        chips, half = self.chips, self.steps
        steps = list(range(1 - half, half + 1))
        place, _ = my_place()
        spots = jnp.stack([ring_chip((place + step + chips) % chips, chips) for step in steps]).astype(jnp.int32)
        (self.mine,) = call(
            functools.partial(pack_kernel, self.cut), spots, [self.got[step] for step in steps[:-1]] + list(self.last), [((chips, self.rows, self.width), BF16)], name="pack"
        )
        self.other = core_swap(self.mine)

    def result(self, place):
        rows = 2 * self.chips * self.rows
        if self.rows % 16 == 0:
            (full,) = call(join_kernel, place, [self.mine, self.other], [((2 * self.chips, self.rows, self.width), BF16)], name="join")
            return full.reshape(rows, self.width)
        first, later = pick(place[1], self.mine, self.other), pick(place[1], self.other, self.mine)
        return jnp.stack([first, later], 1).reshape(rows, self.width)


def together(*values):
    return lax.optimization_barrier(values)


def meet(rings, *values):
    fronts = [ring.front() for ring in rings]
    flat = together(*[v for front in fronts for v in front], *values)
    for i, ring in enumerate(rings):
        ring.put_front((flat[2 * i], flat[2 * i + 1]))
    return flat[2 * len(rings) :]


class Scatter:
    def __init__(self, mine, sent):
        self.mine, self.sent = mine, sent
        self.chips, self.rows, self.width = mine.shape
        self.steps = self.left = self.chips // 2
        self.cut = self.width // 256 * 128
        self.place, _ = my_place()

    def begin(self):
        self.got = core_swap(self.sent)

    def own(self, step, begin=0, end=None):
        chip = ring_chip((self.place + step + self.chips) % self.chips, self.chips)
        cut_out = lambda v: lax.dynamic_index_in_dim(v, chip, 0, False)[:, begin:end].astype(F32)
        return cut_out(self.mine) + cut_out(self.got)

    def front(self):
        return self.up, self.down

    def put_front(self, values):
        self.up, self.down = values

    def step(self, *pins):
        left, cut = self.left, self.cut
        if left == self.steps:
            up, down = self.own(left, 0, cut), self.own(-left, cut)
        else:
            up, down = self.added()
            up, down = self.own(left) + up, self.own(-left) + down
        up, down, *pins = together(low(up), low(down), *pins)
        self.up, self.down = ring_move(up, 1), ring_move(down, -1)
        self.left -= 1
        return pins

    def added(self):
        up, down = self.up.astype(F32), self.down.astype(F32)
        if self.left == self.steps - 1:
            up = jnp.concatenate([up, jnp.zeros((self.rows, self.width - self.cut), F32)], 1)
            down = jnp.concatenate([jnp.zeros((self.rows, self.cut), F32), down], 1)
        return up, down

    def after_here(self, *values):
        self.mine, self.got, *_ = together(self.mine, self.got, *values)

    def result(self):
        up, down = self.added()
        return self.own(0) + up + down


def norm_unit(values):
    centred = values - jnp.mean(values, -1, keepdims=True)
    scale = lax.rsqrt(jnp.mean(centred * centred, -1, keepdims=True) + EPS)
    return centred * scale, scale


def norm_back(values, gain, grad):
    unit, scale = norm_unit(values)
    wide = grad * gain
    inner = wide - jnp.mean(wide, -1, keepdims=True) - unit * jnp.mean(wide * unit, -1, keepdims=True)
    return inner * scale, jnp.sum(grad * unit, 0, keepdims=True), jnp.sum(grad, 0, keepdims=True)


def dot(left, right):
    return jnp.dot(left, right, preferred_element_type=F32)


def dot_tn(left, right):
    return lax.dot_general(left, right, (((0,), (0,)), ((), ())), preferred_element_type=F32)


def dot_nt(left, right):
    return lax.dot_general(left, right, (((1,), (1,)), ((), ())), preferred_element_type=F32)


def heads_of(shape):
    return lax.broadcasted_iota(jnp.int32, shape, 1) // HEAD_DIM


def stacked(block):
    head = heads_of(block.shape)
    zero = jnp.zeros_like(block)
    return jnp.concatenate([jnp.where(head == h, block, zero) for h in range(block.shape[1] // HEAD_DIM)], 0)


def unstacked(rows):
    heads = rows.shape[1] // HEAD_DIM
    slots = rows.shape[0] // heads
    head = heads_of((slots, rows.shape[1]))
    out = rows[:slots]
    for h in range(1, heads):
        out = jnp.where(head == h, rows[h * slots : (h + 1) * slots], out)
    return out


def row_sums(values):
    high = low(values)
    rest = low(values - high.astype(F32))
    ones = jnp.ones((8, values.shape[1]), BF16)
    return (dot_nt(ones, high) + dot_nt(ones, rest))[0:1]


def keep_mask(length, slots):
    query = lax.broadcasted_iota(jnp.int32, (2 * slots, slots), 0) % slots
    key = lax.broadcasted_iota(jnp.int32, (2 * slots, slots), 1)
    return (key <= query) & (key < length)


def self_chances(queries, keys, keep):
    scores = jnp.where(keep, dot_nt(queries, keys) * SCALE, MASKED)
    raised = jnp.exp(scores - jnp.max(scores, -1, keepdims=True))
    return raised / jnp.sum(raised, -1, keepdims=True)


def keep_mask_turned(length, slots):
    key = lax.broadcasted_iota(jnp.int32, (slots, 2 * slots), 0)
    query = lax.broadcasted_iota(jnp.int32, (slots, 2 * slots), 1) % slots
    return (key <= query) & (key < length)


def self_chances_turned(queries, keys, keep):
    scores = jnp.where(keep, dot_nt(keys, queries) * SCALE, MASKED)
    raised = jnp.exp(scores - jnp.max(scores, 0, keepdims=True))
    return raised / jnp.sum(raised, 0, keepdims=True)


class Late:
    def __init__(self, source, scratch, sems, blocks):
        self.scratch, self.shape = scratch, scratch.shape
        self.copies = {}
        for i, (begin, end) in enumerate(blocks or [(0, None)]):
            here = (slice(None), slice(begin, end)) if blocks else Ellipsis
            copy = pltpu.make_async_copy(source.at[here] if blocks else source, scratch.at[here] if blocks else scratch, sems.at[i])
            copy.start()
            self.copies[(begin, end)] = copy

    def __getitem__(self, index):
        wanted = index[-1] if isinstance(index, tuple) and len(self.shape) == 2 else slice(None)
        low_end, high_end = wanted.start or 0, wanted.stop or self.shape[-1]
        for block in list(self.copies):
            if block[0] < high_end and (block[1] is None or block[1] > low_end):
                self.copies.pop(block).wait()
        return self.scratch[index]


class Save:
    def __init__(self, buffer, target, sems):
        self.buffer, self.target, self.sems, self.shape = buffer, target, sems, buffer.shape
        self.copies, self.whole = [], False

    def __getitem__(self, index):
        return self.buffer[index]

    def __setitem__(self, index, value):
        self.buffer[index] = value

    def flush(self, cols=None):
        if self.whole:
            return
        self.whole = cols is None
        here = (slice(None),) * (len(self.shape) - 1) + (cols,)
        copy = pltpu.make_async_copy(self.buffer if cols is None else self.buffer.at[here], self.target if cols is None else self.target.at[here], self.sems.at[len(self.copies)])
        copy.start()
        self.copies.append(copy)


def flush(ref, cols=None):
    if isinstance(ref, Save):
        ref.flush(cols)


def late(array, *blocks):
    return (array, blocks)


def save(shape, dtype):
    return (shape, dtype, "save")


def both(shape, dtype):
    return (shape, dtype, "both")


FLUSHES = 10


def run_kernel(kernel, in_kinds, out_kinds, kept, n_results, *refs):
    n_ins = 1 + len(in_kinds)
    ins, results, scratch = refs[1:n_ins], list(refs[n_ins : n_ins + n_results]), list(refs[n_ins + n_results :])
    given = []
    for ref, blocks in zip(ins, in_kinds):
        given.append(ref if blocks is None else Late(ref, scratch.pop(0), scratch.pop(0), blocks))
    saves, outs = [], []
    for i in kept:
        saves.append(Save(ins[i], results.pop(), scratch.pop(0)))
        saves[-1].flush()
    for kind in out_kinds:
        if kind == "near":
            outs.append(results.pop(0))
            continue
        buffer = scratch.pop(0) if kind == "save" else results.pop(0)
        saves.append(Save(buffer, results.pop(0), scratch.pop(0)))
        outs.append(saves[-1])
    kernel(refs[0], *given, *outs, *scratch)
    for item in saves:
        if not item.copies:
            item.flush()
    for item in saves:
        for copy in item.copies:
            copy.wait()


def call(kernel, place, ins, outs, scratch=(), vmem=14, name=None, flops=0, keep=()):
    smem, near, far = pl.BlockSpec(memory_space=pltpu.SMEM), pl.BlockSpec(memory_space=pltpu.VMEM), pl.BlockSpec(memory_space=pl.ANY)
    in_specs, arrays, in_kinds, buffers = [smem], [place], [], []
    for entry in ins:
        if isinstance(entry, tuple):
            array, blocks = entry
            array = pltpu.with_memory_space_constraint(array, pltpu.HBM)
            in_specs.append(far)
            in_kinds.append(tuple(blocks))
            buffers += [pltpu.VMEM(array.shape, array.dtype), pltpu.SemaphoreType.DMA((max(1, len(blocks)),))]
        else:
            array = entry
            in_specs.append(smem if array.dtype == jnp.int32 else near)
            in_kinds.append(None)
        arrays.append(array)
    buffers += [pltpu.SemaphoreType.DMA((1,)) for _ in keep]
    out_specs, out_shapes, out_kinds = [], [], []
    for entry in outs:
        shape, dtype, kind = entry if len(entry) == 3 else entry + ("near",)
        out_kinds.append(kind)
        if kind != "save":
            out_specs.append(near)
            out_shapes.append(jax.ShapeDtypeStruct(shape, dtype))
        else:
            buffers.append(pltpu.VMEM(shape, dtype))
        if kind != "near":
            out_specs.append(far)
            out_shapes.append(pltpu.HBM(shape, dtype))
            buffers.append(pltpu.SemaphoreType.DMA((FLUSHES,)))
    for i in reversed(keep):
        out_specs.append(far)
        out_shapes.append(pltpu.HBM(ins[i].shape, ins[i].dtype))
    moved = sum(a.size * a.dtype.itemsize for a in arrays)
    return pl.pallas_call(
        functools.partial(run_kernel, kernel, tuple(in_kinds), tuple(out_kinds), tuple(keep), len(out_shapes)),
        in_specs=in_specs,
        out_specs=out_specs,
        out_shape=out_shapes,
        scratch_shapes=buffers + list(scratch),
        compiler_params=pltpu.CompilerParams(vmem_limit_bytes=vmem * MIB),
        cost_estimate=pl.CostEstimate(flops=flops, bytes_accessed=moved, transcendentals=0),
        name=name,
    )(*arrays)


SELF_GAIN, SELF_SHIFT, FEED_GAIN, FEED_SHIFT, DOWN_BIAS, UP_BIAS = range(6)
FOLDS = 2
LAYER_VECS = 5 + 2 * FOLDS
CROSS_GAIN, CROSS_SHIFT = 2 * LAYER_VECS, 2 * LAYER_VECS + 1
VECS = 24


def woven(first, later, blocks):
    parts = [v.reshape(blocks, v.shape[0] // blocks, v.shape[1]) for v in (first, later)]
    return jnp.concatenate(parts, 1).reshape(2 * first.shape[0], first.shape[1])


def unwoven(value, blocks):
    parts = value.reshape(blocks, value.shape[0] // blocks, value.shape[1])
    half = parts.shape[1] // 2
    return jnp.concatenate([parts[:, :half].reshape(-1, value.shape[1]), parts[:, half:].reshape(-1, value.shape[1])], 0)


def side_in(section, own, other):
    first = jnp.where(section == 0, own, other)
    return jnp.concatenate([first, jnp.where(section == 0, other, own)], 1)


def half_in(section, values):
    half = values.shape[1] // 2
    return jnp.where(section == 0, values[:, :half], values[:, half:])


def vec(ref, row):
    return ref[row : row + 1, :]


def up_bias_of(vecs, layer, section, fold):
    return vecs[pl.ds(LAYER_VECS * layer + UP_BIAS + FOLDS * section + fold, 1), :]


def self_part(values, layer, lengths, vecs, weights, normed_ref, projected, mixed_ref):
    base = LAYER_VECS * layer
    unit, _ = norm_unit(values)
    normed = low(unit * vec(vecs, base + SELF_GAIN) + vec(vecs, base + SELF_SHIFT))
    normed_ref[...] = normed
    flush(normed_ref)
    half = mixed_ref.shape[1]
    width = values.shape[1]
    projected[...] = low(dot(normed, weights[:, width : width + 3 * half]))
    flush(projected)
    captions = lengths.shape[0]
    slots = values.shape[0] // captions
    for c in range(captions):
        keep = keep_mask(lengths[c], slots)
        here = slice(c * slots, (c + 1) * slots)
        for j in range(half // PAIR):
            q, k, v = (projected[here, i * half + j * PAIR : i * half + (j + 1) * PAIR] for i in range(3))
            chances = self_chances(stacked(q), k, keep)
            mixed_ref[here, j * PAIR : (j + 1) * PAIR] = low(unstacked(dot(low(chances), v)))


def self_first_kernel(aligned, place, lengths, text, weights, vecs, normed, projected, mixed):
    columns = weights[:, weights.shape[1] - 128 :].astype(F32)
    if aligned:
        lane = lax.broadcasted_iota(jnp.int32, columns.shape, 1)
        columns = jnp.where(lane < CROSS_GAIN, columns, unwoven(columns, weights.shape[0] // 48))
    vecs[...] = columns.T[: vecs.shape[0]]
    flush(vecs)
    self_part(text[...].astype(F32), 0, lengths, vecs, weights, normed, projected, mixed)


def self_second_kernel(place, lengths, middle, own, other, vecs, weights, hidden, normed, projected, mixed):
    total = middle[...] + (own[...].astype(F32) + other[...].astype(F32)) + vec(vecs, DOWN_BIAS)
    hidden[...] = low(total)
    flush(hidden)
    self_part(hidden[...].astype(F32), 1, lengths, vecs, weights, normed, projected, mixed)


def heads_rows(weights, section):
    width = weights.shape[0]
    return weights[pl.ds(pl.multiple_of(section * (width // 2), width // 2), width // 2), :width]


def add_heads_out(values, mixed, weights):
    return values + dot(mixed[...], weights[:, : values.shape[1]])


def feed_part(middle, layer, section, vecs, feed, normed_ref, slope_ref, active_ref):
    base = LAYER_VECS * layer
    width = middle.shape[1]
    unit, _ = norm_unit(middle)
    normed = low(unit * vec(vecs, base + FEED_GAIN) + vec(vecs, base + FEED_SHIFT))
    normed_ref[...] = normed
    flush(normed_ref)
    total = jnp.zeros_like(middle)
    for i in range(FOLDS):
        here = slice(i * width, (i + 1) * width)
        raised = dot(normed, feed[:, here]) + up_bias_of(vecs, layer, section, i)
        chance = 0.5 * (1.0 + lax.erf(raised * 0.5**0.5))
        slope_ref[:, here] = low(chance + raised * jnp.exp(-0.5 * raised * raised) * 0.3989422804014327)
        active = low(raised * chance)
        active_ref[:, here] = active
        flush(slope_ref, here)
        flush(active_ref, here)
        total += dot(active, feed[:, (FOLDS + i) * width : (FOLDS + i + 1) * width])
    return low(total)


def feed_first_kernel(place, text, own, other, vecs, weights, feed, mixed_all, middle, normed, slope, active, part):
    mixed_all[...] = side_in(place[0], own[...], other[...])
    flush(mixed_all)
    values = add_heads_out(text[...].astype(F32), mixed_all, weights)
    middle[...] = values
    flush(middle)
    part[...] = feed_part(values, 0, place[0], vecs, feed, normed, slope, active)


def by_caption(kernel, array, weights, out, name, flops):
    block = lambda shape: pl.BlockSpec((1,) + shape[1:], lambda i: (i, 0, 0))
    moved = array.size * array.dtype.itemsize + out.size * out.dtype.itemsize
    return pl.pallas_call(
        kernel,
        grid=(array.shape[0],),
        in_specs=[block(array.shape), pl.BlockSpec(weights.shape, lambda i: (0, 0))],
        out_specs=block(out.shape),
        out_shape=pltpu.HBM(out.shape, out.dtype),
        compiler_params=pltpu.CompilerParams(vmem_limit_bytes=24 * MIB),
        cost_estimate=pl.CostEstimate(flops=flops, bytes_accessed=moved, transcendentals=0),
        name=name,
    )(array, weights)


def pairs_kernel(place, image, keys, pairs):
    for c in range(image.shape[0]):
        pairs[c] = low(dot(image[c], keys[...]))


def image_grad_kernel(grad_pairs, keys, grad):
    grad[0] = dot_nt(grad_pairs[0], keys[...])


def cross_kernel(place, hidden, own, other, vecs, weights, query, pairs, mixed_all, first, normed_ref, queries, part, stats):
    mixed_all[...] = side_in(place[0], own[...], other[...])
    flush(mixed_all)
    values = add_heads_out(hidden[...].astype(F32), mixed_all, weights)
    first[...] = values
    flush(first)
    unit, _ = norm_unit(values)
    normed = low(unit * vec(vecs, CROSS_GAIN) + vec(vecs, CROSS_SHIFT))
    normed_ref[...] = normed
    flush(normed_ref)
    rows, width = values.shape
    queries[...] = low(dot(normed, query[...]))
    flush(queries)
    captions = pairs.shape[0]
    slots = rows // captions
    quads = width // QUAD
    for c in range(captions):
        here = slice(c * slots, (c + 1) * slots)
        for j in range(quads):
            cols = slice(j * QUAD, (j + 1) * QUAD)
            k, v = pairs[c, :, cols], pairs[c, :, width + j * QUAD : width + (j + 1) * QUAD]
            scores = dot_nt(k, stacked(queries[here, cols])) * SCALE
            top = jnp.max(scores, 0, keepdims=True)
            raised = jnp.exp(scores - top)
            part[here, cols] = low(unstacked(dot_tn(low(raised), v)))
            row = c * quads + j
            stats[row : row + 1, :] = top
            stats[STATS + row : STATS + row + 1, :] = jnp.sum(raised, 0, keepdims=True)


STATS = 16


def feed_second_kernel(place, first, own, other, own_stats, other_stats, vecs, out, feed, middle, mixed, factor, normed, slope, active, part):
    rows, width = first.shape
    quads = width // QUAD
    top, top_other = own_stats[:STATS], other_stats[:STATS]
    best = jnp.maximum(top, top_other)
    own_weight, other_weight = jnp.exp(top - best), jnp.exp(top_other - best)
    inverse = 1.0 / (own_stats[STATS:] * own_weight + other_stats[STATS:] * other_weight)
    own_factor, other_factor = own_weight * inverse, other_weight * inverse
    factor[...] = own_factor
    flush(factor)
    columns = jnp.concatenate([own_factor, other_factor, jnp.zeros((PAIR - 2 * STATS, QUAD), F32)], 0).T
    slots = QUAD // 4
    head = heads_of((slots, QUAD))
    for c in range(rows // slots):
        here = slice(c * slots, (c + 1) * slots)
        for j in range(quads):
            cols = slice(j * QUAD, (j + 1) * QUAD)

            def spread(column):
                out = columns[:slots, column : column + 1]
                for h in range(1, 4):
                    out = jnp.where(head == h, columns[h * slots : (h + 1) * slots, column : column + 1], out)
                return out

            row = c * quads + j
            mixed[here, cols] = low(spread(row) * own[here, cols].astype(F32) + spread(STATS + row) * other[here, cols].astype(F32))
    flush(mixed)
    values = first[...] + dot(mixed[...], out[...])
    middle[...] = values
    flush(middle)
    part[...] = feed_part(values, 1, place[0], vecs, feed, normed, slope, active)


def feed_back(grad, vecs, feed, slope, bias_grad, down_bias_grad, slope_ref, part):
    width = grad.shape[1]
    grad_low = low(grad)
    down_bias_grad[...] = jnp.sum(grad, 0, keepdims=True)
    total = jnp.zeros(grad.shape, F32)
    for i in range(FOLDS):
        here = slice(i * width, (i + 1) * width)
        down = feed[:, (FOLDS + i) * width : (FOLDS + i + 1) * width]
        grad_raised = low(dot_nt(grad_low, down) * slope[:, here].astype(F32))
        slope_ref[:, here] = grad_raised
        bias_grad[i : i + 1, :] = jnp.sum(grad_raised.astype(F32), 0, keepdims=True)
        total += dot_nt(grad_raised, feed[:, here])
    part[...] = low(total)


def feed_back_last_kernel(place, cot, vecs, feed, slope, bias_grad, down_bias_grad, grad_raised, part):
    feed_back(cot[...].astype(F32), vecs, feed, slope, bias_grad, down_bias_grad, grad_raised, part)


def cross_back_kernel(place, cot, own, other, middle, vecs, out, queries, pairs, stats, factor, mixed, grad_ref, low_ref, vec_grad, query_part, grad_pairs, grad_mixed):
    rows, width = middle.shape
    inner = own[...].astype(F32) + other[...].astype(F32)
    step, gain_grad, shift_grad = norm_back(middle[...], vec(vecs, LAYER_VECS + FEED_GAIN), inner)
    vec_grad[0:1, :] = gain_grad
    vec_grad[1:2, :] = shift_grad
    grad = step + cot[...].astype(F32)
    grad_ref[...] = grad
    low_ref[...] = low(grad)
    grad_mixed[...] = low(dot_nt(low(grad), out[...]))
    captions = pairs.shape[0]
    slots = rows // captions
    quads = width // QUAD
    for c in range(captions):
        here = slice(c * slots, (c + 1) * slots)
        for j in range(quads):
            cols = slice(j * QUAD, (j + 1) * QUAD)
            later = slice(width + j * QUAD, width + (j + 1) * QUAD)
            row = slice(c * quads + j, c * quads + j + 1)
            k, v = pairs[c, :, cols], pairs[c, :, later]
            q = stacked(queries[here, cols])
            grad_block = grad_mixed[here, cols]
            grads = stacked(grad_block)
            delta = row_sums(stacked(grad_block.astype(F32) * mixed[here, cols].astype(F32)))
            chances = jnp.exp(dot_nt(k, q) * SCALE - stats[row, :]) * factor[row, :]
            slope = low(chances * (dot_nt(v, grads) - delta))
            query_part[here, cols] = low(unstacked(dot_tn(slope, k)) * SCALE)
            grad_pairs[c, :, cols] = low(dot(slope, q) * SCALE)
            grad_pairs[c, :, later] = low(dot(low(chances), grads))


def self_back(grad, section, lengths, weights, projected, low_ref, grad_projected, grad_mixed):
    half = grad_mixed.shape[1]
    low_ref[...] = low(grad)
    flush(low_ref)
    grad_mixed[...] = low(dot_nt(low(grad), heads_rows(weights, section)))
    captions = lengths.shape[0]
    slots = grad.shape[0] // captions
    for c in range(captions):
        keep = keep_mask_turned(lengths[c], slots)
        here = slice(c * slots, (c + 1) * slots)
        for j in range(half // PAIR):
            cols = [slice(i * half + j * PAIR, i * half + (j + 1) * PAIR) for i in range(3)]
            q, k, v = (projected[here, cols[i]] for i in range(3))
            q = stacked(q)
            chances = self_chances_turned(q, k, keep)
            grads = stacked(grad_mixed[here, cols[0]])
            grad_chances = dot_nt(v, grads)
            slope = low(chances * (grad_chances - jnp.sum(grad_chances * chances, 0, keepdims=True)))
            grad_projected[here, cols[0]] = low(unstacked(dot_tn(slope, k)) * SCALE)
            grad_projected[here, cols[1]] = low(dot(slope, q) * SCALE)
            grad_projected[here, cols[2]] = low(dot(low(chances), grads))
    width = grad.shape[1]
    return dot_nt(grad_projected[...], weights[:, width : width + 3 * half])


def self_back_second_kernel(place, lengths, grad_middle, own, other, first, vecs, query, weights, projected, grad_ref, low_ref, grad_queries, grad_projected, part, vec_grad, grad_mixed):
    total = low(own[...].astype(F32) + other[...].astype(F32))
    grad_queries[...] = total
    inner = dot_nt(total, query[...])
    step, gain_grad, shift_grad = norm_back(first[...], vec(vecs, CROSS_GAIN), inner)
    vec_grad[0:1, :] = gain_grad
    vec_grad[1:2, :] = shift_grad
    grad = step + grad_middle[...]
    grad_ref[...] = grad
    part[...] = low(self_back(grad, place[0], lengths, weights, projected, low_ref, grad_projected, grad_mixed))


def feed_back_first_kernel(place, grad_first, own, other, hidden, vecs, feed, slope, grad_ref, low_ref, vec_grad, bias_grad, down_bias_grad, grad_raised, part):
    inner = own[...].astype(F32) + other[...].astype(F32)
    step, gain_grad, shift_grad = norm_back(hidden[...].astype(F32), vec(vecs, LAYER_VECS + SELF_GAIN), inner)
    vec_grad[0:1, :] = gain_grad
    vec_grad[1:2, :] = shift_grad
    low_ref[...] = low(step + grad_first[...])
    grad = low_ref[...].astype(F32)
    grad_ref[...] = grad
    feed_back(grad, vecs, feed, slope, bias_grad, down_bias_grad, grad_raised, part)


def self_back_first_kernel(place, lengths, grad_hidden, own, other, middle, text, vecs, weights, projected, grad_ref, low_ref, grad_projected, part, vec_grad, grad_mixed):
    inner = own[...].astype(F32) + other[...].astype(F32)
    step, gain_grad, shift_grad = norm_back(middle[...], vec(vecs, FEED_GAIN), inner)
    vec_grad[0:1, :] = gain_grad
    vec_grad[1:2, :] = shift_grad
    grad = step + grad_hidden[...]
    grad_ref[...] = grad
    total = self_back(grad, place[0], lengths, weights, projected, low_ref, grad_projected, grad_mixed)
    part[...] = low(total)
    unit, _ = norm_unit(text[...].astype(F32))
    vec_grad[2:3, :] = jnp.sum(total * unit, 0, keepdims=True)
    vec_grad[3:4, :] = jnp.sum(total, 0, keepdims=True)


def text_grad_kernel(place, grad_middle, own, other, text, vecs, out):
    inner = own[...].astype(F32) + other[...].astype(F32)
    step, _, _ = norm_back(text[...].astype(F32), vec(vecs, SELF_GAIN), inner)
    total = step + grad_middle[...]
    half = out.shape[1]
    out[...] = jnp.where(place[0] == 0, total[:, :half], total[:, half:])


BLOCK = 384


def weight_grads(pieces, refs, put):
    offset = 0
    rows = min(refs[left].shape[1] for left, _ in pieces)
    for left, right in pieces:
        for i in range(refs[left].shape[1] // rows):
            for j in range(refs[right].shape[1] // BLOCK):
                put(offset, dot_tn(refs[left][:, i * rows : (i + 1) * rows], refs[right][:, j * BLOCK : (j + 1) * BLOCK]))
                offset += BLOCK
    return offset


def put_in_order(order, out, cols, value):
    rows = value.shape[0] // len(order)
    for i, device in enumerate(order):
        out[i * rows : (i + 1) * rows, cols] = low(value[device * rows : (device + 1) * rows])
    flush(out, cols)


def products_kernel(order, pieces, place, *refs):
    weight_grads(pieces, refs, lambda offset, value: put_in_order(order, refs[-1], slice(offset, offset + value.shape[1]), value))


def put_by_core(core, mine, sent):
    chips, rows, _ = mine.shape

    def put(offset, value):
        cols = slice(offset, offset + value.shape[1])
        for chip in range(chips):
            first = value[2 * chip * rows : (2 * chip + 1) * rows]
            later = value[(2 * chip + 1) * rows : (2 * chip + 2) * rows]
            mine[chip, :, cols] = low(jnp.where(core == 0, first, later))
            sent[chip, :, cols] = low(jnp.where(core == 0, later, first))
        flush(mine, cols)

    return put


def ring_products_kernel(pieces, place, *refs):
    weight_grads(pieces, refs, put_by_core(place[1], *refs[-2:]))


def last_products_kernel(
    blocks, place, normed, grad_projected, mixed_0, mixed_1, low_0, low_1, vecs_0, self_vecs_1, feed_vecs_1, cross_vecs, down_0, down_1, bias_0, bias_1, mine, sent
):
    section = place[0]
    put = put_by_core(place[1], mine, sent)
    width = normed.shape[1]
    offset = weight_grads(((0, 1),), (normed, grad_projected), put)
    mixed = jnp.where(section == 0, mixed_0[...], mixed_1[...])
    head_low = jnp.where(section == 0, low_0[...], low_1[...])
    for j in range(width // BLOCK):
        put(offset, dot_tn(mixed, head_low[:, j * BLOCK : (j + 1) * BLOCK]))
        offset += BLOCK
    rows = [
        vecs_0[2:4, :],
        jnp.where(section == 0, 0.0, self_vecs_1[0:2, :]),
        jnp.where(section == 0, vecs_0[0:2, :], feed_vecs_1[0:2, :]),
        jnp.where(section == 0, down_0[...], down_1[...]),
        bias_0[...],
        bias_1[...],
        cross_vecs[0:2, :],
    ]
    used = 7 + 2 * FOLDS
    columns = jnp.concatenate(rows + [jnp.zeros((128 - used - 2, width), F32)], 0).T
    if blocks:
        lane = lax.broadcasted_iota(jnp.int32, columns.shape, 1)
        columns = jnp.where(lane < used, columns, woven(columns[: width // 2], columns[width // 2 :], blocks))
    put(offset, columns)


def second_products_kernel(blocks, place, normed, grad_queries, mixed, grad_low, self_normed, grad_projected, image, grad_pairs, mine, sent):
    put = put_by_core(place[1], mine, sent)
    offset = weight_grads(((0, 1),), (self_normed, grad_projected), put)
    own_normed, own_mixed = half_in(place[0], normed[...]), half_in(place[0], mixed[...])
    half = own_normed.shape[1]
    for j in range(grad_queries.shape[1] // BLOCK):
        cols = slice(j * BLOCK, (j + 1) * BLOCK)
        put(offset, woven(dot_tn(own_normed, grad_queries[:, cols]), dot_tn(own_mixed, grad_low[:, cols]), blocks))
        offset += BLOCK
    for j in range(grad_pairs.shape[2] // BLOCK):
        value = sum(dot_tn(image[c], grad_pairs[c, :, j * BLOCK : (j + 1) * BLOCK]) for c in range(image.shape[0]))
        put(offset, woven(value[:half], value[half:], blocks))
        offset += BLOCK


def in_order(section, own, other):
    own, other = own.astype(F32), other.astype(F32)
    return jnp.where(section == 0, own, other), jnp.where(section == 0, other, own)


def finish_feed_kernel(count, place, own, other, up, down):
    rows, width = own.shape[0], down.shape[1]
    halves = in_order(place[0], own[...], other[...])
    parts = []
    for device in range(count):
        for half in halves:
            for fold in range(FOLDS):
                begin = fold * width + device * rows
                parts.append(half[:, begin : begin + rows])
    up[...] = jnp.concatenate(parts, 1)
    for i, half in enumerate(halves):
        for fold in range(FOLDS):
            begin = (i * FOLDS + fold) * rows
            down[begin : begin + rows, :] = half[:, (FOLDS + fold) * width : (FOLDS + fold + 1) * width]


def finish_cross_kernel(place, heads, keys, keys_other, query_grad, keys_grad, out_grad):
    rows = query_grad.shape[0]
    heads32, keys32 = heads[...].astype(F32), keys[...].astype(F32)
    query_grad[...] = heads32[:rows]
    out_grad[...] = heads32[rows:]
    keys_grad[...] = jnp.where(place[0] == 0, keys32[:rows], keys32[rows:]) + keys_other[...].astype(F32)


def finish_heads_kernel(cross_rows, place, sums, own, other, into, out, gain, shift, feed_gain, feed_shift, down_bias, cross_gain, cross_shift, up_bias):
    rows, width = out.shape
    half = width // 2
    section = place[0]
    halves = in_order(section, own[...], other[:, : 3 * half])
    for i in range(3):
        for j, part in enumerate(halves):
            into[:, (2 * i + j) * half : (2 * i + j + 1) * half] = part[:, i * half : (i + 1) * half]
    out[...] = sums[:, 3 * half : 3 * half + width]
    flipped = lambda v: jnp.concatenate([v.astype(F32), jnp.zeros((128 - rows, 128), F32)], 0).T[:, :rows]
    own_vec, other_vec = flipped(sums[:, 3 * half + width :]), flipped(other[:, 3 * half :])
    mine = lambda v, first, later: jnp.where(section == 0, v[first : first + 1], v[later : later + 1])
    gain[...] = mine(own_vec, 0, 2) + mine(other_vec, 0, 2)
    shift[...] = mine(own_vec, 1, 3) + mine(other_vec, 1, 3)
    feed_gain[...] = own_vec[4:5]
    feed_shift[...] = own_vec[5:6]
    down_bias[...] = own_vec[6:7]
    bias = [[mine(v, 7 + i, 7 + FOLDS + i) for i in range(FOLDS)] for v in (own_vec, other_vec)]
    ordered = [jnp.where(section == 0, a, b) for a, b in zip(*bias)] + [jnp.where(section == 0, b, a) for a, b in zip(*bias)]
    up_bias[...] = jnp.concatenate(ordered, 1)
    for i, ref in enumerate((cross_gain, cross_shift)):
        row = own_vec[7 + 2 * FOLDS + i : 8 + 2 * FOLDS + i]
        ref[...] = jnp.where(section == 0, row[:, :cross_rows], row[:, cross_rows:])


def body(
    text,
    image,
    lengths,
    self_gain,
    self_shift,
    heads_in,
    heads_out,
    feed_gain,
    feed_shift,
    up_weight,
    up_bias,
    down_weight,
    down_bias,
    cross_gain,
    cross_shift,
    cross_query,
    cross_keys,
    cross_out,
    cotangent,
):
    section = lax.axis_index("section")
    count = lax.axis_size("dp")
    core = lax.axis_index("dp") % 2
    place = jnp.stack([section, core]).astype(jnp.int32)
    captions, half_image, width = image.shape
    rows = text.shape[0]
    piece = heads_in.shape[1]
    cross_piece = cross_query.shape[0]
    half = width // 2
    half_ff = FOLDS * width
    aligned = piece % 16 == 0
    order = [2 * chip + i for chip in ring_order() for i in range(2)] if aligned else list(range(count))
    groups = [order]

    def both_layers(first, later):
        own, got = pick(section, first, later), swap(pick(section, later, first))
        return pick(section, own, got), pick(section, got, own)

    core_cols = width + 3 * half
    cross_own = jnp.concatenate([cross_keys, cross_query, cross_out], 1)
    cross_got = swap(cross_own)
    into = heads_in[0].reshape(piece, 3, 2, half)
    attn_0, attn_1 = both_layers(*[jnp.concatenate([heads_out[0], into[:, :, i].reshape(piece, 3 * half)], 1) for i in range(2)])
    own_vecs = jnp.concatenate([self_gain, self_shift, feed_gain, feed_shift, down_bias, up_bias.reshape(2 * FOLDS, piece)], 0)
    own_cross_vecs = jnp.concatenate([cross_gain[None], cross_shift[None]], 0)
    sent_vecs = jnp.concatenate([own_vecs, jnp.pad(own_cross_vecs, ((0, 0), (0, piece - cross_piece)))], 0)
    got_vecs = swap(sent_vecs)
    cross_vec_rows = side(own_cross_vecs, got_vecs[LAYER_VECS:, :cross_piece], section, 1)
    vec_cols = jnp.concatenate([pick(section, own_vecs, got_vecs[:LAYER_VECS]), pick(section, got_vecs[:LAYER_VECS], own_vecs), cross_vec_rows], 0)
    vec_cols = jnp.pad(vec_cols, ((0, 128 - vec_cols.shape[0]), (0, 0))).T
    up = up_weight[0].reshape(piece, count, 2, FOLDS, piece).transpose(2, 0, 3, 1, 4).reshape(2, piece, half_ff)
    down = down_weight[0].reshape(2, FOLDS, piece, width)
    feed_own = [jnp.concatenate([up[i]] + [down[i, j] for j in range(FOLDS)], 1) for i in range(2)]
    cross_got, attn_0, attn_1, vec_cols, first_own, later_own, text_own, cot_own = together(cross_got, attn_0, attn_1, vec_cols, *feed_own, text, cotangent)

    def gather(value):
        return lax.all_gather(value, "dp", axis=0, tiled=True, axis_index_groups=groups)

    def reordered(value, blocks, parts, widths):
        rows_out = value.shape[0] * parts
        if aligned:
            return call(functools.partial(reorder_kernel, blocks, parts), place, [value], [((rows_out, w), BF16) for w in widths], name="reorder")
        whole = value.reshape(value.shape[0], parts, sum(widths)).transpose(1, 0, 2).reshape(rows_out, sum(widths))
        ends = [sum(widths[: i + 1]) for i in range(len(widths))]
        return [whole[:, end - w : end] for end, w in zip(ends, widths)]

    attn_first = gather(jnp.concatenate([attn_0, vec_cols], 1))
    feed_0, feed_1 = both_layers(first_own, later_own)
    text_all = side(text, swap(text_own), section, 1)
    cross_all = gather(side(cross_own, cross_got, section, 1))
    feed_last = gather(feed_1)
    cot_all = side(cotangent, swap(cot_own), section, 1)
    ring_f, ring_d = Gather(feed_0), Gather(attn_1)
    ring_f.move()
    meet([ring_f])
    for _ in range(ring_f.steps - 2):
        ring_f.move()
        ring_d.move()
        meet([ring_f, ring_d])
    ring_f.move()
    ring_d.move()
    (weights_0,) = reordered(attn_first, order, 1, [core_cols + 128])

    shape_f = ((rows, width), F32)
    shape_b = ((rows, width), BF16)
    shape_half = ((rows, half), BF16)
    shape_qkv = ((rows, 3 * half), BF16)
    shape_active = ((rows, half_ff), BF16)
    shape_stats = ((2 * STATS, QUAD), F32)
    shape_factor = ((STATS, QUAD), F32)
    shape_pairs = ((captions, half_image, 2 * width), BF16)
    shape_vec = ((8, width), F32)
    shape_bias = ((FOLDS, width), F32)
    shape_one = ((1, width), F32)
    half_scratch = [pltpu.VMEM((rows, half), BF16)]
    self_flops, feed_flops, pair_flops = 6 * rows * width * half, 4 * rows * width * half_ff, 4 * captions * half_image * width * width
    feed_blocks = [(i * width, (i + 1) * width) for i in (2, 0, 3, 1)]
    attn_blocks = [(0, width), (width, core_cols)]

    vecs, vecs_far, normed_a0, qkv_0, mixed_0, weights_0_far = call(
        functools.partial(self_first_kernel, aligned),
        place,
        [lengths, text_all, weights_0],
        [both((VECS, width), F32), save(*shape_b), save(*shape_qkv), shape_half],
        name="self_0",
        flops=self_flops,
        keep=(2,),
    )
    if not aligned:
        straight = lambda v: jnp.concatenate([v[:CROSS_GAIN], v[CROSS_GAIN : CROSS_GAIN + 2].reshape(2, count, 2, cross_piece).transpose(0, 2, 1, 3).reshape(2, width), v[CROSS_GAIN + 2 :]], 0)
        vecs, vecs_far = straight(vecs), straight(vecs_far)
    other_0 = swap(mixed_0)
    (mixed_0,) = meet([ring_f, ring_d], mixed_0)
    ring_f.pack()
    while ring_d.step < ring_d.steps:
        ring_d.move()
    other_0, ring_f.other = together(other_0, ring_f.other)
    feed_w0 = ring_f.result(place)
    keys, query, cross_out_w = reordered(cross_all, ring_order() if aligned else [0], 2, [2 * width, width, width])
    mixed_all_0, middle_0, middle_0_far, normed_f0, slope_f0, active_0, part_0, feed_w0_far = call(
        feed_first_kernel,
        place,
        [text_all, mixed_0, other_0, vecs, weights_0, feed_w0],
        [save(*shape_b), both(*shape_f), save(*shape_b), save(*shape_active), save(*shape_active), shape_b],
        name="feed_0",
        flops=feed_flops,
        keep=(5,),
    )
    part_0_other = swap(part_0)
    (part_0,) = meet([ring_d], part_0)
    ring_d.pack()
    weights_1 = ring_d.result(place)
    hidden, hidden_far, normed_a1, qkv_1, mixed_1, weights_1_far = call(
        self_second_kernel,
        place,
        [lengths, middle_0, part_0, part_0_other, vecs, weights_1],
        [both(*shape_b), save(*shape_b), save(*shape_qkv), shape_half],
        name="self_1",
        flops=self_flops,
        keep=(5,),
    )
    other_1 = swap(mixed_1)
    pairs, keys_far = call(pairs_kernel, place, [late(image), keys], [shape_pairs], name="pairs", flops=pair_flops, keep=(1,))
    other_1, pairs = together(other_1, pairs)
    mixed_all_1, first_1, first_1_far, normed_c, queries, cross_part, stats, stats_far, query_far = call(
        cross_kernel,
        place,
        [hidden, mixed_1, other_1, vecs, weights_1, query, pairs],
        [save(*shape_b), both(*shape_f), save(*shape_b), save(*shape_b), shape_b, both(*shape_stats)],
        name="cross_1",
        flops=4 * rows * width * width,
        keep=(5,),
    )
    cross_part_other, stats_other = swap(cross_part), swap(stats)
    (feed_w1,) = reordered(feed_last, order, 1, [2 * half_ff])
    middle_1, middle_1_far, cross_mixed_far, factor, normed_f1, slope_f1, active_1, part_1, cross_out_far = call(
        feed_second_kernel,
        place,
        [first_1, cross_part, cross_part_other, stats, stats_other, vecs, cross_out_w, feed_w1],
        [both(*shape_f), save(*shape_b), save(*shape_factor), shape_b, shape_active, shape_active, shape_b],
        name="feed_1",
        flops=feed_flops,
        keep=(6,),
    )
    own_cols = lambda v: pick(section, v[..., :half], v[..., half:])

    def scatter(value):
        return lax.psum_scatter(value, "dp", scatter_dimension=0, tiled=True, axis_index_groups=groups)

    bias_grad_1, down_bias_grad_1, slope_1, back_1 = call(
        feed_back_last_kernel, place, [cot_all, vecs, feed_w1, slope_f1], [save(*shape_bias), save(*shape_one), shape_active, shape_b], name="feed_back_1", flops=feed_flops
    )
    back_1_other = swap(back_1)
    (feed_grad_1,) = call(
        functools.partial(products_kernel, order, ((0, 1), (2, 3))),
        place,
        [normed_f1, slope_1, active_1, cot_all],
        [save((width, 2 * half_ff), BF16)],
        name="feed_grads_1",
        flops=feed_flops,
    )
    back_1_other, feed_grad_1 = together(back_1_other, feed_grad_1)
    feed_got_1 = scatter(feed_grad_1)
    grad_middle_1, grad_low_1, feed_vec_1, query_part, grad_pairs = call(
        cross_back_kernel,
        place,
        [cot_all, back_1, back_1_other, late(middle_1_far), late(vecs_far), late(cross_out_far), late(queries), pairs, late(stats_far), late(factor), late(cross_mixed_far)],
        [shape_f, shape_b, save(*shape_vec), shape_b, shape_pairs],
        scratch=[pltpu.VMEM((rows, width), BF16)],
        name="cross_back",
        flops=4 * rows * width * width,
    )
    query_part_other = swap(query_part)
    grad_first_1, head_low_1, grad_queries, grad_qkv_1, self_back_1, cross_vec_1 = call(
        self_back_second_kernel,
        place,
        [lengths, grad_middle_1, query_part, query_part_other, late(first_1_far), late(vecs_far), late(query_far), late(weights_1_far, *attn_blocks), late(qkv_1)],
        [shape_f, save(*shape_b), shape_b, shape_qkv, shape_b, save(*shape_vec)],
        scratch=half_scratch,
        name="self_back_1",
        flops=2 * self_flops,
    )
    self_back_1_other = swap(self_back_1)
    ring_shape = lambda cols: ((count // 2, piece, cols), BF16)
    second_cols = 3 * half + 3 * width
    if aligned:
        second_grads = call(
            functools.partial(second_products_kernel, count),
            place,
            [late(normed_c), grad_queries, late(cross_mixed_far), grad_low_1, late(normed_a1), grad_qkv_1, late(image), grad_pairs],
            [save(*ring_shape(second_cols)), ring_shape(second_cols)],
            vmem=20,
            name="second_grads",
            flops=pair_flops,
        )
    else:
        pair_rows = lambda v: v.reshape(2, count, cross_piece, v.shape[1]).transpose(1, 0, 2, 3).reshape(width, v.shape[1])
        flat = lambda v: v.reshape(captions * half_image, v.shape[2])
        heads = pair_rows(jnp.concatenate([dot_tn(own_cols(normed_c), grad_queries), dot_tn(own_cols(cross_mixed_far), grad_low_1)], 0))
        second_grad = low(jnp.concatenate([dot_tn(normed_a1, grad_qkv_1), heads, pair_rows(dot_tn(flat(image), flat(grad_pairs)))], 1))
        parts = second_grad.reshape(count // 2, 2, piece, second_cols)
        second_grads = pick(core, parts[:, 0], parts[:, 1]), pick(core, parts[:, 1], parts[:, 0])
    self_back_1_other, *second_grads = together(self_back_1_other, *second_grads)
    ring_second = Scatter(*second_grads)
    ring_second.begin()
    grad_hidden, grad_hidden_low, self_vec_1, bias_grad_0, down_bias_grad_0, slope_0, back_0 = call(
        feed_back_first_kernel,
        place,
        [grad_first_1, self_back_1, self_back_1_other, late(hidden_far), late(vecs_far), late(feed_w0_far, *feed_blocks), late(slope_f0)],
        [shape_f, shape_b, save(*shape_vec), save(*shape_bias), save(*shape_one), shape_active, shape_b],
        name="feed_back_0",
        flops=feed_flops,
    )
    back_0_other = swap(back_0)
    ring_second.after_here(back_0)
    (slope_0,) = ring_second.step(slope_0)
    (feed_grad_0,) = call(
        functools.partial(products_kernel, order, ((0, 1), (2, 3))),
        place,
        [late(normed_f0), slope_0, late(active_0), grad_hidden_low],
        [save((width, 2 * half_ff), BF16)],
        name="feed_grads_0",
        flops=feed_flops,
    )
    back_0_other, feed_grad_0, up, down = together(back_0_other, feed_grad_0, *ring_second.front())
    ring_second.put_front((up, down))
    feed_got_0 = scatter(feed_grad_0)
    (back_0_other,) = ring_second.step(back_0_other)
    grad_middle_0, head_low_0, grad_qkv_0, self_back_0, vecs_grad_0 = call(
        self_back_first_kernel,
        place,
        [lengths, grad_hidden, back_0, back_0_other, late(middle_0_far), text_all, late(vecs_far), late(weights_0_far, *attn_blocks), late(qkv_0)],
        [shape_f, shape_b, shape_qkv, shape_b, shape_vec],
        scratch=half_scratch,
        name="self_back_0",
        flops=2 * self_flops,
    )
    self_back_0_other = swap(self_back_0)
    def meet_sums(rings, *values):
        flat = together(*[v for ring in rings for v in ring.front()], *values)
        for i, ring in enumerate(rings):
            ring.put_front(flat[2 * i : 2 * i + 2])
        return flat[2 * len(rings) :]

    grad_qkv_0, feed_got_1 = meet_sums([ring_second], grad_qkv_0, feed_got_1)
    (grad_qkv_0,) = ring_second.step(grad_qkv_0)
    cross_vec_woven = cross_vec_1
    if not aligned:
        cross_vec_woven = cross_vec_1.reshape(8, 2, count, cross_piece).transpose(0, 2, 1, 3).reshape(8, width)
    last_grads = call(
        functools.partial(last_products_kernel, count if aligned else 0),
        place,
        [late(normed_a0), grad_qkv_0, late(mixed_all_0), late(mixed_all_1), head_low_0, late(head_low_1), vecs_grad_0]
        + [late(v) for v in (self_vec_1, feed_vec_1, cross_vec_woven, down_bias_grad_0, down_bias_grad_1, bias_grad_0, bias_grad_1)],
        [save(*ring_shape(core_cols + 128)), ring_shape(core_cols + 128)],
        name="last_grads",
        flops=2 * rows * width * core_cols,
    )
    ring_last = Scatter(*last_grads)
    ring_last.begin()
    ring_last.mine, ring_last.got = meet_sums([ring_second], ring_last.mine, ring_last.got)
    ring_second.step()
    def other_half(first, later):
        return swap(pick(section, low(later), low(first)))

    (grad_pairs,) = ring_last.step(grad_pairs)
    image_grad = by_caption(image_grad_kernel, grad_pairs, keys_far, jax.ShapeDtypeStruct((captions, half_image, width), F32), "image_grad", pair_flops)
    (image_grad,) = meet_sums([ring_second, ring_last], image_grad)
    (grad_middle_0,) = ring_last.step(grad_middle_0)
    (text_grad,) = call(text_grad_kernel, place, [grad_middle_0, self_back_0, self_back_0_other, text_all, late(vecs_far)], [((rows, half), F32)], name="text_grad")
    second_got = low(ring_second.result())
    text_grad, second_got = meet_sums([ring_last], text_grad, second_got)
    (second_got,) = ring_last.step(second_got)
    (feed_got_0,) = meet_sums([ring_last], feed_got_0)
    feed_other = other_half(feed_got_0, feed_got_1)
    while ring_last.left:
        ring_last.step()
    got_part = swap(pick(section, part_1[:, half:], part_1[:, :half]))
    layer_out = own_cols(middle_1_far) + (own_cols(part_1).astype(F32) + got_part.astype(F32)) + own_cols(vecs_far[LAYER_VECS + DOWN_BIAS])
    cross_got = second_got[:, 3 * half : 3 * half + width]
    keys_got = second_got[:, 3 * half + width :]
    keys_other = swap(pick(section, keys_got[cross_piece:], keys_got[:cross_piece]))
    feed_own = pick(section, feed_got_0, feed_got_1)
    into_got_1 = second_got[:, : 3 * half]
    if aligned:
        up_grad, down_grad = call(
            functools.partial(finish_feed_kernel, count),
            place,
            [feed_own, feed_other],
            [((piece, 2 * half_ff), F32), ((2 * FOLDS * piece, width), F32)],
            name="finish_feed",
        )
        cross_query_grad, cross_keys_grad, cross_out_grad = call(
            finish_cross_kernel,
            place,
            [cross_got, keys_got, keys_other],
            [((cross_piece, width), F32), ((cross_piece, 2 * width), F32), ((cross_piece, width), F32)],
            name="finish_cross",
        )
        keys_other, cross_query_grad = together(keys_other, cross_query_grad)
    else:
        feed_parts = [v.astype(F32) for v in (pick(section, feed_own, feed_other), pick(section, feed_other, feed_own))]
        up_parts = [v[:, :half_ff].reshape(piece, FOLDS, count, piece).transpose(0, 2, 1, 3) for v in feed_parts]
        up_grad = jnp.stack(up_parts, 2).reshape(piece, 2 * half_ff)
        down_parts = [v[:, half_ff:].reshape(piece, FOLDS, width).transpose(1, 0, 2) for v in feed_parts]
        down_grad = jnp.stack(down_parts, 0).reshape(2 * FOLDS * piece, width)
        cross_query_grad, cross_out_grad = cross_got[:cross_piece].astype(F32), cross_got[cross_piece:].astype(F32)
        own_keys = pick(section, keys_got[:cross_piece], keys_got[cross_piece:])
        cross_keys_grad = own_keys.astype(F32) + keys_other.astype(F32)
    last_got = ring_last.result()
    vec_got = last_got[:, core_cols:]
    last_other = swap(low(jnp.concatenate([pick(section, into_got_1.astype(F32), last_got[:, : 3 * half]), vec_got], 1)))
    into_own = pick(section, last_got[:, : 3 * half], into_got_1.astype(F32))
    if aligned:
        shape_row = ((1, piece), F32)
        heads_in_grad, heads_out_grad, *rows_out, up_bias_grad = call(
            functools.partial(finish_heads_kernel, cross_piece),
            place,
            [last_got, into_own, last_other],
            [((piece, 6 * half), F32), ((piece, width), F32)] + [shape_row] * 5 + [((1, cross_piece), F32)] * 2 + [((1, 2 * FOLDS * piece), F32)],
            name="finish_heads",
        )
        cross_gain_grad, cross_shift_grad = rows_out[5][0], rows_out[6][0]
    else:
        into_other = last_other[:, : 3 * half].astype(F32)
        into_parts = pick(section, into_own, into_other), pick(section, into_other, into_own)
        heads_in_grad = jnp.stack([v.reshape(piece, 3, half) for v in into_parts], 2).reshape(piece, 6 * half)
        heads_out_grad = last_got[:, 3 * half : core_cols]
        own_vec, other_vec = vec_got.T, last_other[:, 3 * half :].astype(F32).T
        mine = lambda v, begin, size: pick(section, v[begin : begin + size], v[begin + size : begin + 2 * size])
        self_vec = mine(own_vec, 0, 2) + mine(other_vec, 0, 2)
        rows_out = [self_vec[0:1], self_vec[1:2], own_vec[4:5], own_vec[5:6], own_vec[6:7]]
        bias = mine(own_vec, 7, FOLDS), mine(other_vec, 7, FOLDS)
        up_bias_grad = jnp.concatenate([pick(section, *bias), pick(section, *bias[::-1])], 0).reshape(1, 2 * FOLDS * piece)
        cross_vec = pick(section, own_vec[7 + 2 * FOLDS : 9 + 2 * FOLDS, :cross_piece], own_vec[7 + 2 * FOLDS : 9 + 2 * FOLDS, cross_piece:])
        cross_gain_grad, cross_shift_grad = cross_vec[0], cross_vec[1]
    return (
        layer_out,
        text_grad,
        image_grad,
        rows_out[0],
        rows_out[1],
        heads_in_grad[None],
        heads_out_grad[None],
        rows_out[2],
        rows_out[3],
        up_grad[None],
        up_bias_grad,
        down_grad[None],
        rows_out[4],
        cross_gain_grad,
        cross_shift_grad,
        cross_query_grad,
        cross_keys_grad,
        cross_out_grad,
    )


def solution(mesh):
    placed = (
        P("dp", "section"),
        P("dp", "section", None),
        P("dp"),
        P("section", "dp"),
        P("section", "dp"),
        P("section", "dp", None),
        P("section", "dp", None),
        P("section", "dp"),
        P("section", "dp"),
        P("section", "dp", None),
        P("section", "dp"),
        P("section", "dp", None),
        P("section", "dp"),
        P(("section", "dp")),
        P(("section", "dp")),
        P(("section", "dp"), None),
        P(("section", "dp"), None),
        P(("section", "dp"), None),
        P("dp", "section"),
    )
    return jax.shard_map(
        body,
        mesh=mesh,
        in_specs=placed,
        out_specs=(P("dp", "section"), P("dp", "section"), P("dp", "section", None)) + placed[3:18],
        check_vma=False,
    )
```

```python
import functools

import jax
import jax.numpy as jnp
from jax import lax
from jax.experimental import pallas as pl
from jax.experimental.pallas import tpu as pltpu
from jax.sharding import PartitionSpec as P

HEAD_DIM = 64
PAIR = 2 * HEAD_DIM
QUAD = 4 * HEAD_DIM
EPS = 1e-05
MASKED = -1000000000.0
SCALE = HEAD_DIM**-0.5
F32 = jnp.float32
BF16 = jnp.bfloat16
MIB = 1 << 20


def swap(value):
    return lax.ppermute(value, "section", [(0, 1), (1, 0)])


def pick(section, first, later):
    return jnp.where(section == 0, first, later)


def side(own, other, section, axis):
    return jnp.concatenate([pick(section, own, other), pick(section, other, own)], axis)


def low(values):
    return values.astype(BF16)


def ring_chip(place, chips):
    return jnp.where(place < chips // 2, 2 * place, 2 * (chips - 1 - place) + 1)


def ring_order():
    chips = lax.axis_size("dp") // 2
    return list(range(0, chips, 2)) + list(range(chips - 1, 0, -2))


def ring_steps(shift):
    order = ring_order()
    chips = len(order)
    return [(2 * order[i] + core, 2 * order[(i + shift) % chips] + core) for i in range(chips) for core in range(2)]


def ring_move(value, shift):
    return lax.ppermute(value, "dp", ring_steps(shift))


def core_swap(value):
    return lax.ppermute(value, "dp", [(i, i ^ 1) for i in range(lax.axis_size("dp"))])


def my_place():
    chips = lax.axis_size("dp") // 2
    me = lax.axis_index("dp")
    chip, core = me // 2, me % 2
    return jnp.where(chip % 2 == 0, chip // 2, chips - 1 - chip // 2), core


def pack_kernel(cut, spots, *refs):
    *sources, out = refs
    chips = out.shape[0]
    for i, source in enumerate(sources[: chips - 1]):
        out[spots[i]] = source[...]
    out[spots[chips - 1], :, :cut] = sources[chips - 1][...]
    out[spots[chips - 1], :, cut:] = sources[chips][...]


def join_kernel(place, mine, other, out):
    core = place[1]
    for chip in range(mine.shape[0]):
        out[2 * chip + core] = mine[chip]
        out[2 * chip + 1 - core] = other[chip]


def reorder_kernel(order, parts, place, source, *outs):
    rows = source.shape[0] // len(order)
    width = sum(out.shape[1] for out in outs)
    for part in range(parts):
        offset = part * width
        for out in outs:
            for i, spot in enumerate(order):
                begin = part * source.shape[0] + spot * rows
                out[begin : begin + rows, :] = source[i * rows : (i + 1) * rows, offset : offset + out.shape[1]]
            offset += out.shape[1]


class Gather:
    def __init__(self, shard):
        self.chips = lax.axis_size("dp") // 2
        self.steps = self.chips // 2
        self.rows, self.width = shard.shape
        self.cut = self.width // 256 * 128
        self.got = {0: shard}
        self.step = 0
        self.last = ()

    def front(self):
        return self.last or (self.got[-self.step], self.got[self.step])

    def put_front(self, values):
        if self.last:
            self.last = values
        else:
            self.got[-self.step], self.got[self.step] = values

    def move(self):
        self.step += 1
        up, down = self.got[1 - self.step], self.got[self.step - 1]
        if self.step < self.steps:
            self.got[-self.step], self.got[self.step] = ring_move(up, 1), ring_move(down, -1)
        else:
            self.last = (ring_move(up[:, : self.cut], 1), ring_move(down[:, self.cut :], -1))

    def pack(self):
        chips, half = self.chips, self.steps
        steps = list(range(1 - half, half + 1))
        place, _ = my_place()
        spots = jnp.stack([ring_chip((place + step + chips) % chips, chips) for step in steps]).astype(jnp.int32)
        (self.mine,) = call(
            functools.partial(pack_kernel, self.cut), spots, [self.got[step] for step in steps[:-1]] + list(self.last), [((chips, self.rows, self.width), BF16)], name="pack"
        )
        self.other = core_swap(self.mine)

    def result(self, place):
        rows = 2 * self.chips * self.rows
        if self.rows % 16 == 0:
            (full,) = call(join_kernel, place, [self.mine, self.other], [((2 * self.chips, self.rows, self.width), BF16)], name="join")
            return full.reshape(rows, self.width)
        first, later = pick(place[1], self.mine, self.other), pick(place[1], self.other, self.mine)
        return jnp.stack([first, later], 1).reshape(rows, self.width)


def together(*values):
    return lax.optimization_barrier(values)


def meet(rings, *values):
    fronts = [ring.front() for ring in rings]
    flat = together(*[v for front in fronts for v in front], *values)
    for i, ring in enumerate(rings):
        ring.put_front((flat[2 * i], flat[2 * i + 1]))
    return flat[2 * len(rings) :]


class Scatter:
    def __init__(self, mine, sent):
        self.mine, self.sent = mine, sent
        self.chips, self.rows, self.width = mine.shape
        self.steps = self.left = self.chips // 2
        self.cut = self.width // 256 * 128
        self.place, _ = my_place()

    def begin(self):
        self.got = core_swap(self.sent)

    def own(self, step, begin=0, end=None):
        chip = ring_chip((self.place + step + self.chips) % self.chips, self.chips)
        cut_out = lambda v: lax.dynamic_index_in_dim(v, chip, 0, False)[:, begin:end].astype(F32)
        return cut_out(self.mine) + cut_out(self.got)

    def front(self):
        return self.up, self.down

    def put_front(self, values):
        self.up, self.down = values

    def step(self, *pins):
        left, cut = self.left, self.cut
        if left == self.steps:
            up, down = self.own(left, 0, cut), self.own(-left, cut)
        else:
            up, down = self.added()
            up, down = self.own(left) + up, self.own(-left) + down
        up, down, *pins = together(low(up), low(down), *pins)
        self.up, self.down = ring_move(up, 1), ring_move(down, -1)
        self.left -= 1
        return pins

    def added(self):
        up, down = self.up.astype(F32), self.down.astype(F32)
        if self.left == self.steps - 1:
            up = jnp.concatenate([up, jnp.zeros((self.rows, self.width - self.cut), F32)], 1)
            down = jnp.concatenate([jnp.zeros((self.rows, self.cut), F32), down], 1)
        return up, down

    def after_here(self, *values):
        self.mine, self.got, *_ = together(self.mine, self.got, *values)

    def result(self):
        up, down = self.added()
        return self.own(0) + up + down


def norm_unit(values):
    centred = values - jnp.mean(values, -1, keepdims=True)
    scale = lax.rsqrt(jnp.mean(centred * centred, -1, keepdims=True) + EPS)
    return centred * scale, scale


def norm_back(values, gain, grad):
    unit, scale = norm_unit(values)
    wide = grad * gain
    inner = wide - jnp.mean(wide, -1, keepdims=True) - unit * jnp.mean(wide * unit, -1, keepdims=True)
    return inner * scale, jnp.sum(grad * unit, 0, keepdims=True), jnp.sum(grad, 0, keepdims=True)


def dot(left, right):
    return jnp.dot(left, right, preferred_element_type=F32)


def dot_tn(left, right):
    return lax.dot_general(left, right, (((0,), (0,)), ((), ())), preferred_element_type=F32)


def dot_nt(left, right):
    return lax.dot_general(left, right, (((1,), (1,)), ((), ())), preferred_element_type=F32)


def heads_of(shape):
    return lax.broadcasted_iota(jnp.int32, shape, 1) // HEAD_DIM


def stacked(block):
    head = heads_of(block.shape)
    zero = jnp.zeros_like(block)
    return jnp.concatenate([jnp.where(head == h, block, zero) for h in range(block.shape[1] // HEAD_DIM)], 0)


def unstacked(rows):
    heads = rows.shape[1] // HEAD_DIM
    slots = rows.shape[0] // heads
    head = heads_of((slots, rows.shape[1]))
    out = rows[:slots]
    for h in range(1, heads):
        out = jnp.where(head == h, rows[h * slots : (h + 1) * slots], out)
    return out


def row_sums(values):
    high = low(values)
    rest = low(values - high.astype(F32))
    ones = jnp.ones((8, values.shape[1]), BF16)
    return (dot_nt(ones, high) + dot_nt(ones, rest))[0:1]


def keep_mask(length, slots):
    query = lax.broadcasted_iota(jnp.int32, (2 * slots, slots), 0) % slots
    key = lax.broadcasted_iota(jnp.int32, (2 * slots, slots), 1)
    return (key <= query) & (key < length)


def self_chances(queries, keys, keep):
    scores = jnp.where(keep, dot_nt(queries, keys) * SCALE, MASKED)
    raised = jnp.exp(scores - jnp.max(scores, -1, keepdims=True))
    return raised / jnp.sum(raised, -1, keepdims=True)


def keep_mask_turned(length, slots):
    key = lax.broadcasted_iota(jnp.int32, (slots, 2 * slots), 0)
    query = lax.broadcasted_iota(jnp.int32, (slots, 2 * slots), 1) % slots
    return (key <= query) & (key < length)


def self_chances_turned(queries, keys, keep):
    scores = jnp.where(keep, dot_nt(keys, queries) * SCALE, MASKED)
    raised = jnp.exp(scores - jnp.max(scores, 0, keepdims=True))
    return raised / jnp.sum(raised, 0, keepdims=True)


class Late:
    def __init__(self, source, scratch, sems, blocks):
        self.scratch, self.shape = scratch, scratch.shape
        self.copies = {}
        for i, (begin, end) in enumerate(blocks or [(0, None)]):
            here = (slice(None), slice(begin, end)) if blocks else Ellipsis
            copy = pltpu.make_async_copy(source.at[here] if blocks else source, scratch.at[here] if blocks else scratch, sems.at[i])
            copy.start()
            self.copies[(begin, end)] = copy

    def __getitem__(self, index):
        wanted = index[-1] if isinstance(index, tuple) and len(self.shape) == 2 else slice(None)
        low_end, high_end = wanted.start or 0, wanted.stop or self.shape[-1]
        for block in list(self.copies):
            if block[0] < high_end and (block[1] is None or block[1] > low_end):
                self.copies.pop(block).wait()
        return self.scratch[index]


class Save:
    def __init__(self, buffer, target, sems):
        self.buffer, self.target, self.sems, self.shape = buffer, target, sems, buffer.shape
        self.copies, self.whole = [], False

    def __getitem__(self, index):
        return self.buffer[index]

    def __setitem__(self, index, value):
        self.buffer[index] = value

    def flush(self, cols=None):
        if self.whole:
            return
        self.whole = cols is None
        here = (slice(None),) * (len(self.shape) - 1) + (cols,)
        copy = pltpu.make_async_copy(self.buffer if cols is None else self.buffer.at[here], self.target if cols is None else self.target.at[here], self.sems.at[len(self.copies)])
        copy.start()
        self.copies.append(copy)


def flush(ref, cols=None):
    if isinstance(ref, Save):
        ref.flush(cols)


def late(array, *blocks):
    return (array, blocks)


def save(shape, dtype):
    return (shape, dtype, "save")


def both(shape, dtype):
    return (shape, dtype, "both")


FLUSHES = 10


def run_kernel(kernel, in_kinds, out_kinds, kept, n_over, n_results, *refs):
    n_ins = 1 + len(in_kinds) + n_over
    ins, results, scratch = refs[1:n_ins], list(refs[n_ins : n_ins + n_results]), list(refs[n_ins + n_results :])
    given = []
    for ref, blocks in zip(ins, in_kinds):
        given.append(ref if blocks is None else Late(ref, scratch.pop(0), scratch.pop(0), blocks))
    saves, outs = [], []
    for i in kept:
        saves.append(Save(ins[i], results.pop(), scratch.pop(0)))
        saves[-1].flush()
    for kind in out_kinds:
        if kind == "near":
            outs.append(results.pop(0))
            continue
        buffer = scratch.pop(0) if kind == "save" else results.pop(0)
        saves.append(Save(buffer, results.pop(0), scratch.pop(0)))
        outs.append(saves[-1])
    kernel(refs[0], *given, *outs, *scratch)
    for item in saves:
        if not item.copies:
            item.flush()
    for item in saves:
        for copy in item.copies:
            copy.wait()


def call(kernel, place, ins, outs, scratch=(), vmem=14, name=None, flops=0, keep=(), over=()):
    smem, near, far = pl.BlockSpec(memory_space=pltpu.SMEM), pl.BlockSpec(memory_space=pltpu.VMEM), pl.BlockSpec(memory_space=pl.ANY)
    in_specs, arrays, in_kinds, buffers = [smem], [place], [], []
    for entry in ins:
        if isinstance(entry, tuple):
            array, blocks = entry
            array = pltpu.with_memory_space_constraint(array, pltpu.HBM)
            in_specs.append(far)
            in_kinds.append(tuple(blocks))
            buffers += [pltpu.VMEM(array.shape, array.dtype), pltpu.SemaphoreType.DMA((max(1, len(blocks)),))]
        else:
            array = entry
            in_specs.append(smem if array.dtype == jnp.int32 else near)
            in_kinds.append(None)
        arrays.append(array)
    for array in over:
        in_specs.append(far)
        arrays.append(pltpu.with_memory_space_constraint(array, pltpu.HBM))
    buffers += [pltpu.SemaphoreType.DMA((1,)) for _ in keep]
    out_specs, out_shapes, out_kinds = [], [], []
    for entry in outs:
        shape, dtype, kind = entry if len(entry) == 3 else entry + ("near",)
        out_kinds.append(kind)
        if kind != "save":
            out_specs.append(near)
            out_shapes.append(jax.ShapeDtypeStruct(shape, dtype))
        else:
            buffers.append(pltpu.VMEM(shape, dtype))
        if kind != "near":
            out_specs.append(far)
            out_shapes.append(pltpu.HBM(shape, dtype))
            buffers.append(pltpu.SemaphoreType.DMA((FLUSHES,)))
    for i in reversed(keep):
        out_specs.append(far)
        out_shapes.append(pltpu.HBM(ins[i].shape, ins[i].dtype))
    moved = sum(a.size * a.dtype.itemsize for a in arrays)
    return pl.pallas_call(
        functools.partial(run_kernel, kernel, tuple(in_kinds), tuple(out_kinds), tuple(keep), len(over), len(out_shapes)),
        in_specs=in_specs,
        out_specs=out_specs,
        out_shape=out_shapes,
        scratch_shapes=buffers + list(scratch),
        input_output_aliases={1 + len(ins) + i: i for i in range(len(over))},
        compiler_params=pltpu.CompilerParams(vmem_limit_bytes=vmem * MIB),
        cost_estimate=pl.CostEstimate(flops=flops, bytes_accessed=moved, transcendentals=0),
        name=name,
    )(*arrays)


SELF_GAIN, SELF_SHIFT, FEED_GAIN, FEED_SHIFT, DOWN_BIAS, UP_BIAS = range(6)
FOLDS = 2
LAYER_VECS = 5 + 2 * FOLDS
CROSS_GAIN, CROSS_SHIFT = 2 * LAYER_VECS, 2 * LAYER_VECS + 1
VECS = 24


def woven(first, later, blocks):
    parts = [v.reshape(blocks, v.shape[0] // blocks, v.shape[1]) for v in (first, later)]
    return jnp.concatenate(parts, 1).reshape(2 * first.shape[0], first.shape[1])


def unwoven(value, blocks):
    parts = value.reshape(blocks, value.shape[0] // blocks, value.shape[1])
    half = parts.shape[1] // 2
    return jnp.concatenate([parts[:, :half].reshape(-1, value.shape[1]), parts[:, half:].reshape(-1, value.shape[1])], 0)


def side_in(section, own, other):
    first = jnp.where(section == 0, own, other)
    return jnp.concatenate([first, jnp.where(section == 0, other, own)], 1)


def half_in(section, values):
    half = values.shape[1] // 2
    return jnp.where(section == 0, values[:, :half], values[:, half:])


def vec(ref, row):
    return ref[row : row + 1, :]


def up_bias_of(vecs, layer, section, fold):
    return vecs[pl.ds(LAYER_VECS * layer + UP_BIAS + FOLDS * section + fold, 1), :]


def self_part(values, layer, lengths, vecs, weights, normed_ref, projected, mixed_ref):
    base = LAYER_VECS * layer
    unit, _ = norm_unit(values)
    normed = low(unit * vec(vecs, base + SELF_GAIN) + vec(vecs, base + SELF_SHIFT))
    normed_ref[...] = normed
    flush(normed_ref)
    half = mixed_ref.shape[1]
    width = values.shape[1]
    projected[...] = low(dot(normed, weights[:, width : width + 3 * half]))
    flush(projected)
    captions = lengths.shape[0]
    slots = values.shape[0] // captions
    for c in range(captions):
        keep = keep_mask(lengths[c], slots)
        here = slice(c * slots, (c + 1) * slots)
        for j in range(half // PAIR):
            q, k, v = (projected[here, i * half + j * PAIR : i * half + (j + 1) * PAIR] for i in range(3))
            chances = self_chances(stacked(q), k, keep)
            mixed_ref[here, j * PAIR : (j + 1) * PAIR] = low(unstacked(dot(low(chances), v)))


def self_first_kernel(aligned, place, lengths, text, weights, vecs, normed, projected, mixed):
    columns = weights[:, weights.shape[1] - 128 :].astype(F32)
    if aligned:
        lane = lax.broadcasted_iota(jnp.int32, columns.shape, 1)
        columns = jnp.where(lane < CROSS_GAIN, columns, unwoven(columns, weights.shape[0] // 48))
    vecs[...] = columns.T[: vecs.shape[0]]
    flush(vecs)
    self_part(text[...].astype(F32), 0, lengths, vecs, weights, normed, projected, mixed)


def self_second_kernel(place, lengths, middle, own, other, vecs, weights, hidden, normed, projected, mixed):
    total = middle[...] + (own[...].astype(F32) + other[...].astype(F32)) + vec(vecs, DOWN_BIAS)
    hidden[...] = low(total)
    flush(hidden)
    self_part(hidden[...].astype(F32), 1, lengths, vecs, weights, normed, projected, mixed)


def heads_rows(weights, section):
    width = weights.shape[0]
    return weights[pl.ds(pl.multiple_of(section * (width // 2), width // 2), width // 2), :width]


def add_heads_out(values, mixed, weights):
    return values + dot(mixed[...], weights[:, : values.shape[1]])


def feed_part(middle, layer, section, vecs, feed, normed_ref, slope_ref, active_ref):
    base = LAYER_VECS * layer
    width = middle.shape[1]
    unit, _ = norm_unit(middle)
    normed = low(unit * vec(vecs, base + FEED_GAIN) + vec(vecs, base + FEED_SHIFT))
    normed_ref[...] = normed
    flush(normed_ref)
    total = jnp.zeros_like(middle)
    for i in range(FOLDS):
        here = slice(i * width, (i + 1) * width)
        raised = dot(normed, feed[:, here]) + up_bias_of(vecs, layer, section, i)
        chance = 0.5 * (1.0 + lax.erf(raised * 0.5**0.5))
        slope_ref[:, here] = low(chance + raised * jnp.exp(-0.5 * raised * raised) * 0.3989422804014327)
        active = low(raised * chance)
        active_ref[:, here] = active
        flush(slope_ref, here)
        flush(active_ref, here)
        total += dot(active, feed[:, (FOLDS + i) * width : (FOLDS + i + 1) * width])
    return low(total)


def feed_first_kernel(place, text, own, other, vecs, weights, feed, mixed_all, middle, normed, slope, active, part):
    mixed_all[...] = side_in(place[0], own[...], other[...])
    flush(mixed_all)
    values = add_heads_out(text[...].astype(F32), mixed_all, weights)
    middle[...] = values
    flush(middle)
    part[...] = feed_part(values, 0, place[0], vecs, feed, normed, slope, active)


def by_caption(kernel, array, weights, out, name, flops):
    block = lambda shape: pl.BlockSpec((1,) + shape[1:], lambda i: (i, 0, 0))
    moved = array.size * array.dtype.itemsize + out.size * out.dtype.itemsize
    return pl.pallas_call(
        kernel,
        grid=(array.shape[0],),
        in_specs=[block(array.shape), pl.BlockSpec(weights.shape, lambda i: (0, 0))],
        out_specs=block(out.shape),
        out_shape=pltpu.HBM(out.shape, out.dtype),
        compiler_params=pltpu.CompilerParams(vmem_limit_bytes=24 * MIB),
        cost_estimate=pl.CostEstimate(flops=flops, bytes_accessed=moved, transcendentals=0),
        name=name,
    )(array, weights)


def pairs_kernel(place, image, keys, pairs):
    for c in range(image.shape[0]):
        pairs[c] = low(dot(image[c], keys[...]))


def image_grad_kernel(grad_pairs, keys, grad):
    grad[0] = dot_nt(grad_pairs[0], keys[...])


def cross_kernel(place, hidden, own, other, vecs, weights, query, pairs, mixed_all, first, normed_ref, queries, part, stats):
    mixed_all[...] = side_in(place[0], own[...], other[...])
    flush(mixed_all)
    values = add_heads_out(hidden[...].astype(F32), mixed_all, weights)
    first[...] = values
    flush(first)
    unit, _ = norm_unit(values)
    normed = low(unit * vec(vecs, CROSS_GAIN) + vec(vecs, CROSS_SHIFT))
    normed_ref[...] = normed
    flush(normed_ref)
    rows, width = values.shape
    queries[...] = low(dot(normed, query[...]))
    flush(queries)
    captions = pairs.shape[0]
    slots = rows // captions
    quads = width // QUAD
    for c in range(captions):
        here = slice(c * slots, (c + 1) * slots)
        for j in range(quads):
            cols = slice(j * QUAD, (j + 1) * QUAD)
            k, v = pairs[c, :, cols], pairs[c, :, width + j * QUAD : width + (j + 1) * QUAD]
            scores = dot_nt(k, stacked(queries[here, cols])) * SCALE
            top = jnp.max(scores, 0, keepdims=True)
            raised = jnp.exp(scores - top)
            part[here, cols] = low(unstacked(dot_tn(low(raised), v)))
            row = c * quads + j
            stats[row : row + 1, :] = top
            stats[STATS + row : STATS + row + 1, :] = jnp.sum(raised, 0, keepdims=True)


STATS = 16


def feed_second_kernel(place, first, own, other, own_stats, other_stats, vecs, out, feed, middle, mixed, factor, normed, slope, active, part):
    rows, width = first.shape
    quads = width // QUAD
    top, top_other = own_stats[:STATS], other_stats[:STATS]
    best = jnp.maximum(top, top_other)
    own_weight, other_weight = jnp.exp(top - best), jnp.exp(top_other - best)
    inverse = 1.0 / (own_stats[STATS:] * own_weight + other_stats[STATS:] * other_weight)
    own_factor, other_factor = own_weight * inverse, other_weight * inverse
    factor[...] = own_factor
    flush(factor)
    columns = jnp.concatenate([own_factor, other_factor, jnp.zeros((PAIR - 2 * STATS, QUAD), F32)], 0).T
    slots = QUAD // 4
    head = heads_of((slots, QUAD))
    for c in range(rows // slots):
        here = slice(c * slots, (c + 1) * slots)
        for j in range(quads):
            cols = slice(j * QUAD, (j + 1) * QUAD)

            def spread(column):
                out = columns[:slots, column : column + 1]
                for h in range(1, 4):
                    out = jnp.where(head == h, columns[h * slots : (h + 1) * slots, column : column + 1], out)
                return out

            row = c * quads + j
            mixed[here, cols] = low(spread(row) * own[here, cols].astype(F32) + spread(STATS + row) * other[here, cols].astype(F32))
    flush(mixed)
    values = first[...] + dot(mixed[...], out[...])
    middle[...] = values
    flush(middle)
    part[...] = feed_part(values, 1, place[0], vecs, feed, normed, slope, active)


def feed_back(grad, vecs, feed, slope, bias_grad, down_bias_grad, slope_ref, part):
    width = grad.shape[1]
    grad_low = low(grad)
    down_bias_grad[...] = jnp.sum(grad, 0, keepdims=True)
    total = jnp.zeros(grad.shape, F32)
    for i in range(FOLDS):
        here = slice(i * width, (i + 1) * width)
        down = feed[:, (FOLDS + i) * width : (FOLDS + i + 1) * width]
        grad_raised = low(dot_nt(grad_low, down) * slope[:, here].astype(F32))
        slope_ref[:, here] = grad_raised
        bias_grad[i : i + 1, :] = jnp.sum(grad_raised.astype(F32), 0, keepdims=True)
        total += dot_nt(grad_raised, feed[:, here])
    part[...] = low(total)


def feed_back_last_kernel(place, cot, vecs, feed, slope, bias_grad, down_bias_grad, grad_raised, part):
    feed_back(cot[...].astype(F32), vecs, feed, slope, bias_grad, down_bias_grad, grad_raised, part)


def cross_back_kernel(place, cot, own, other, middle, vecs, out, queries, pairs, stats, factor, mixed, grad_ref, low_ref, vec_grad, query_part, grad_pairs, grad_mixed):
    rows, width = middle.shape
    inner = own[...].astype(F32) + other[...].astype(F32)
    step, gain_grad, shift_grad = norm_back(middle[...], vec(vecs, LAYER_VECS + FEED_GAIN), inner)
    vec_grad[0:1, :] = gain_grad
    vec_grad[1:2, :] = shift_grad
    grad = step + cot[...].astype(F32)
    grad_ref[...] = grad
    low_ref[...] = low(grad)
    grad_mixed[...] = low(dot_nt(low(grad), out[...]))
    captions = pairs.shape[0]
    slots = rows // captions
    quads = width // QUAD
    for c in range(captions):
        here = slice(c * slots, (c + 1) * slots)
        for j in range(quads):
            cols = slice(j * QUAD, (j + 1) * QUAD)
            later = slice(width + j * QUAD, width + (j + 1) * QUAD)
            row = slice(c * quads + j, c * quads + j + 1)
            k, v = pairs[c, :, cols], pairs[c, :, later]
            q = stacked(queries[here, cols])
            grad_block = grad_mixed[here, cols]
            grads = stacked(grad_block)
            delta = row_sums(stacked(grad_block.astype(F32) * mixed[here, cols].astype(F32)))
            chances = jnp.exp(dot_nt(k, q) * SCALE - stats[row, :]) * factor[row, :]
            slope = low(chances * (dot_nt(v, grads) - delta))
            query_part[here, cols] = low(unstacked(dot_tn(slope, k)) * SCALE)
            grad_pairs[c, :, cols] = low(dot(slope, q) * SCALE)
            grad_pairs[c, :, later] = low(dot(low(chances), grads))


def self_back(grad, section, lengths, weights, projected, low_ref, grad_projected, grad_mixed):
    half = grad_mixed.shape[1]
    low_ref[...] = low(grad)
    flush(low_ref)
    grad_mixed[...] = low(dot_nt(low(grad), heads_rows(weights, section)))
    captions = lengths.shape[0]
    slots = grad.shape[0] // captions
    for c in range(captions):
        keep = keep_mask_turned(lengths[c], slots)
        here = slice(c * slots, (c + 1) * slots)
        for j in range(half // PAIR):
            cols = [slice(i * half + j * PAIR, i * half + (j + 1) * PAIR) for i in range(3)]
            q, k, v = (projected[here, cols[i]] for i in range(3))
            q = stacked(q)
            chances = self_chances_turned(q, k, keep)
            grads = stacked(grad_mixed[here, cols[0]])
            grad_chances = dot_nt(v, grads)
            slope = low(chances * (grad_chances - jnp.sum(grad_chances * chances, 0, keepdims=True)))
            grad_projected[here, cols[0]] = low(unstacked(dot_tn(slope, k)) * SCALE)
            grad_projected[here, cols[1]] = low(dot(slope, q) * SCALE)
            grad_projected[here, cols[2]] = low(dot(low(chances), grads))
    width = grad.shape[1]
    return dot_nt(grad_projected[...], weights[:, width : width + 3 * half])


def self_back_second_kernel(place, lengths, grad_middle, own, other, first, vecs, query, weights, projected, grad_ref, low_ref, grad_queries, grad_projected, part, vec_grad, grad_mixed):
    total = low(own[...].astype(F32) + other[...].astype(F32))
    grad_queries[...] = total
    inner = dot_nt(total, query[...])
    step, gain_grad, shift_grad = norm_back(first[...], vec(vecs, CROSS_GAIN), inner)
    vec_grad[0:1, :] = gain_grad
    vec_grad[1:2, :] = shift_grad
    grad = step + grad_middle[...]
    grad_ref[...] = grad
    part[...] = low(self_back(grad, place[0], lengths, weights, projected, low_ref, grad_projected, grad_mixed))


def feed_back_first_kernel(place, grad_first, own, other, hidden, vecs, feed, slope, grad_ref, low_ref, vec_grad, bias_grad, down_bias_grad, grad_raised, part):
    inner = own[...].astype(F32) + other[...].astype(F32)
    step, gain_grad, shift_grad = norm_back(hidden[...].astype(F32), vec(vecs, LAYER_VECS + SELF_GAIN), inner)
    vec_grad[0:1, :] = gain_grad
    vec_grad[1:2, :] = shift_grad
    low_ref[...] = low(step + grad_first[...])
    grad = low_ref[...].astype(F32)
    grad_ref[...] = grad
    feed_back(grad, vecs, feed, slope, bias_grad, down_bias_grad, grad_raised, part)


def self_back_first_kernel(place, lengths, grad_hidden, own, other, middle, text, vecs, weights, projected, grad_ref, low_ref, grad_projected, part, vec_grad, grad_mixed):
    inner = own[...].astype(F32) + other[...].astype(F32)
    step, gain_grad, shift_grad = norm_back(middle[...], vec(vecs, FEED_GAIN), inner)
    vec_grad[0:1, :] = gain_grad
    vec_grad[1:2, :] = shift_grad
    grad = step + grad_hidden[...]
    grad_ref[...] = grad
    total = self_back(grad, place[0], lengths, weights, projected, low_ref, grad_projected, grad_mixed)
    part[...] = low(total)
    unit, _ = norm_unit(text[...].astype(F32))
    vec_grad[2:3, :] = jnp.sum(total * unit, 0, keepdims=True)
    vec_grad[3:4, :] = jnp.sum(total, 0, keepdims=True)


def text_grad_kernel(place, grad_middle, own, other, text, vecs, out):
    inner = own[...].astype(F32) + other[...].astype(F32)
    step, _, _ = norm_back(text[...].astype(F32), vec(vecs, SELF_GAIN), inner)
    total = step + grad_middle[...]
    half = out.shape[1]
    out[...] = jnp.where(place[0] == 0, total[:, :half], total[:, half:])


BLOCK = 384


def weight_grads(pieces, refs, put):
    offset = 0
    rows = min(refs[left].shape[1] for left, _ in pieces)
    for left, right in pieces:
        for i in range(refs[left].shape[1] // rows):
            for j in range(refs[right].shape[1] // BLOCK):
                put(offset, dot_tn(refs[left][:, i * rows : (i + 1) * rows], refs[right][:, j * BLOCK : (j + 1) * BLOCK]))
                offset += BLOCK
    return offset


def put_in_order(order, out, cols, value):
    rows = value.shape[0] // len(order)
    for i, device in enumerate(order):
        out[i * rows : (i + 1) * rows, cols] = low(value[device * rows : (device + 1) * rows])
    flush(out, cols)


def products_kernel(order, pieces, place, *refs):
    weight_grads(pieces, refs, lambda offset, value: put_in_order(order, refs[-1], slice(offset, offset + value.shape[1]), value))


def put_by_core(core, mine, sent):
    chips, rows, _ = mine.shape

    def put(offset, value):
        cols = slice(offset, offset + value.shape[1])
        for chip in range(chips):
            first = value[2 * chip * rows : (2 * chip + 1) * rows]
            later = value[(2 * chip + 1) * rows : (2 * chip + 2) * rows]
            mine[chip, :, cols] = low(jnp.where(core == 0, first, later))
            sent[chip, :, cols] = low(jnp.where(core == 0, later, first))
        flush(mine, cols)
        flush(sent, cols)

    return put


def ring_products_kernel(pieces, place, *refs):
    weight_grads(pieces, refs, put_by_core(place[1], *refs[-2:]))


def last_products_kernel(
    blocks, place, normed, grad_projected, mixed_0, mixed_1, low_0, low_1, vecs_0, self_vecs_1, feed_vecs_1, cross_vecs, down_0, down_1, bias_0, bias_1, mine, sent
):
    section = place[0]
    put = put_by_core(place[1], mine, sent)
    width = normed.shape[1]
    offset = weight_grads(((0, 1),), (normed, grad_projected), put)
    mixed = jnp.where(section == 0, mixed_0[...], mixed_1[...])
    head_low = jnp.where(section == 0, low_0[...], low_1[...])
    for j in range(width // BLOCK):
        put(offset, dot_tn(mixed, head_low[:, j * BLOCK : (j + 1) * BLOCK]))
        offset += BLOCK
    rows = [
        vecs_0[2:4, :],
        jnp.where(section == 0, 0.0, self_vecs_1[0:2, :]),
        jnp.where(section == 0, vecs_0[0:2, :], feed_vecs_1[0:2, :]),
        jnp.where(section == 0, down_0[...], down_1[...]),
        bias_0[...],
        bias_1[...],
        cross_vecs[0:2, :],
    ]
    used = 7 + 2 * FOLDS
    columns = jnp.concatenate(rows + [jnp.zeros((128 - used - 2, width), F32)], 0).T
    if blocks:
        lane = lax.broadcasted_iota(jnp.int32, columns.shape, 1)
        columns = jnp.where(lane < used, columns, woven(columns[: width // 2], columns[width // 2 :], blocks))
    put(offset, columns)


def keys_products_kernel(blocks, offset, place, image, grad_pairs, mine, sent):
    put = put_by_core(place[1], mine, sent)
    half = image.shape[2] // 2
    for j in range(grad_pairs.shape[2] // BLOCK):
        value = sum(dot_tn(image[c], grad_pairs[c, :, j * BLOCK : (j + 1) * BLOCK]) for c in range(image.shape[0]))
        put(offset + j * BLOCK, woven(value[:half], value[half:], blocks))


def second_products_kernel(blocks, place, normed, grad_queries, mixed, grad_low, self_normed, grad_projected, mine, sent):
    put = put_by_core(place[1], mine, sent)
    offset = weight_grads(((0, 1),), (self_normed, grad_projected), put)
    own_normed, own_mixed = half_in(place[0], normed[...]), half_in(place[0], mixed[...])
    for j in range(grad_queries.shape[1] // BLOCK):
        cols = slice(j * BLOCK, (j + 1) * BLOCK)
        put(offset, woven(dot_tn(own_normed, grad_queries[:, cols]), dot_tn(own_mixed, grad_low[:, cols]), blocks))
        offset += BLOCK


def in_order(section, own, other):
    own, other = own.astype(F32), other.astype(F32)
    return jnp.where(section == 0, own, other), jnp.where(section == 0, other, own)


def finish_feed_kernel(count, place, own, other, up, down):
    rows, width = own.shape[0], down.shape[1]
    halves = in_order(place[0], own[...], other[...])
    parts = []
    for device in range(count):
        for half in halves:
            for fold in range(FOLDS):
                begin = fold * width + device * rows
                parts.append(half[:, begin : begin + rows])
    up[...] = jnp.concatenate(parts, 1)
    for i, half in enumerate(halves):
        for fold in range(FOLDS):
            begin = (i * FOLDS + fold) * rows
            down[begin : begin + rows, :] = half[:, (FOLDS + fold) * width : (FOLDS + fold + 1) * width]


def finish_cross_kernel(place, heads, keys, keys_other, query_grad, keys_grad, out_grad):
    rows = query_grad.shape[0]
    heads32, keys32 = heads[...].astype(F32), keys[...].astype(F32)
    query_grad[...] = heads32[:rows]
    out_grad[...] = heads32[rows:]
    keys_grad[...] = jnp.where(place[0] == 0, keys32[:rows], keys32[rows:]) + keys_other[...].astype(F32)


def finish_heads_kernel(cross_rows, place, sums, own, other, into, out, gain, shift, feed_gain, feed_shift, down_bias, cross_gain, cross_shift, up_bias):
    rows, width = out.shape
    half = width // 2
    section = place[0]
    halves = in_order(section, own[...], other[:, : 3 * half])
    for i in range(3):
        for j, part in enumerate(halves):
            into[:, (2 * i + j) * half : (2 * i + j + 1) * half] = part[:, i * half : (i + 1) * half]
    out[...] = sums[:, 3 * half : 3 * half + width]
    flipped = lambda v: jnp.concatenate([v.astype(F32), jnp.zeros((128 - rows, 128), F32)], 0).T[:, :rows]
    own_vec, other_vec = flipped(sums[:, 3 * half + width :]), flipped(other[:, 3 * half :])
    mine = lambda v, first, later: jnp.where(section == 0, v[first : first + 1], v[later : later + 1])
    gain[...] = mine(own_vec, 0, 2) + mine(other_vec, 0, 2)
    shift[...] = mine(own_vec, 1, 3) + mine(other_vec, 1, 3)
    feed_gain[...] = own_vec[4:5]
    feed_shift[...] = own_vec[5:6]
    down_bias[...] = own_vec[6:7]
    bias = [[mine(v, 7 + i, 7 + FOLDS + i) for i in range(FOLDS)] for v in (own_vec, other_vec)]
    ordered = [jnp.where(section == 0, a, b) for a, b in zip(*bias)] + [jnp.where(section == 0, b, a) for a, b in zip(*bias)]
    up_bias[...] = jnp.concatenate(ordered, 1)
    for i, ref in enumerate((cross_gain, cross_shift)):
        row = own_vec[7 + 2 * FOLDS + i : 8 + 2 * FOLDS + i]
        ref[...] = jnp.where(section == 0, row[:, :cross_rows], row[:, cross_rows:])


def body(
    text,
    image,
    lengths,
    self_gain,
    self_shift,
    heads_in,
    heads_out,
    feed_gain,
    feed_shift,
    up_weight,
    up_bias,
    down_weight,
    down_bias,
    cross_gain,
    cross_shift,
    cross_query,
    cross_keys,
    cross_out,
    cotangent,
):
    section = lax.axis_index("section")
    count = lax.axis_size("dp")
    core = lax.axis_index("dp") % 2
    place = jnp.stack([section, core]).astype(jnp.int32)
    captions, half_image, width = image.shape
    rows = text.shape[0]
    piece = heads_in.shape[1]
    cross_piece = cross_query.shape[0]
    half = width // 2
    half_ff = FOLDS * width
    aligned = piece % 16 == 0
    order = [2 * chip + i for chip in ring_order() for i in range(2)] if aligned else list(range(count))
    groups = [order]

    def both_layers(first, later):
        own, got = pick(section, first, later), swap(pick(section, later, first))
        return pick(section, own, got), pick(section, got, own)

    core_cols = width + 3 * half
    up = up_weight[0].reshape(piece, count, 2, FOLDS, piece).transpose(2, 0, 3, 1, 4).reshape(2, piece, half_ff)
    down = down_weight[0].reshape(2, FOLDS, piece, width)
    feed_own = [jnp.concatenate([up[i]] + [down[i, j] for j in range(FOLDS)], 1) for i in range(2)]
    into = heads_in[0].reshape(piece, 3, 2, half)
    attn_own = [jnp.concatenate([heads_out[0], into[:, :, i].reshape(piece, 3 * half)], 1) for i in range(2)]
    own_vecs = jnp.concatenate([self_gain, self_shift, feed_gain, feed_shift, down_bias, up_bias.reshape(2 * FOLDS, piece)], 0)
    own_cross_vecs = jnp.concatenate([cross_gain[None], cross_shift[None]], 0)
    sent_vecs = jnp.concatenate([own_vecs, jnp.pad(own_cross_vecs, ((0, 0), (0, piece - cross_piece)))], 0)
    cross_own = jnp.concatenate([cross_keys, cross_query, cross_out], 1)
    feed_0, feed_1 = both_layers(*feed_own)
    feed_0, feed_1, sent_vecs, *attn_own = together(feed_0, feed_1, sent_vecs, *attn_own)
    ring_f = Gather(feed_0)
    ring_f.move()
    attn_0, attn_1 = both_layers(*attn_own)
    got_vecs = swap(sent_vecs)
    cross_vec_rows = side(own_cross_vecs, got_vecs[LAYER_VECS:, :cross_piece], section, 1)
    vec_cols = jnp.concatenate([pick(section, own_vecs, got_vecs[:LAYER_VECS]), pick(section, got_vecs[:LAYER_VECS], own_vecs), cross_vec_rows], 0)
    vec_cols = jnp.pad(vec_cols, ((0, 128 - vec_cols.shape[0]), (0, 0))).T
    def gather(value):
        return lax.all_gather(value, "dp", axis=0, tiled=True, axis_index_groups=groups)

    def reordered(value, blocks, parts, widths):
        rows_out = value.shape[0] * parts
        if aligned:
            return call(functools.partial(reorder_kernel, blocks, parts), place, [value], [((rows_out, w), BF16) for w in widths], name="reorder")
        whole = value.reshape(value.shape[0], parts, sum(widths)).transpose(1, 0, 2).reshape(rows_out, sum(widths))
        ends = [sum(widths[: i + 1]) for i in range(len(widths))]
        return [whole[:, end - w : end] for end, w in zip(ends, widths)]

    attn_first = gather(jnp.concatenate([attn_0, vec_cols], 1))
    attn_1, feed_1, cross_own, text_own, cot_own = meet([ring_f], attn_1, feed_1, cross_own, text, cotangent)
    cross_all = gather(side(cross_own, swap(cross_own), section, 1))
    text_all = side(text, swap(text_own), section, 1)
    feed_last = gather(feed_1)
    cot_all = side(cotangent, swap(cot_own), section, 1)
    ring_d = Gather(attn_1)
    for i in range(ring_f.steps - 2):
        ring_f.move()
        ring_d.move()
        if i < ring_f.steps - 3:
            meet([ring_f, ring_d])
    (attn_first,) = meet([ring_f, ring_d], attn_first)
    ring_f.move()
    ring_d.move()
    (weights_0,) = reordered(attn_first, order, 1, [core_cols + 128])

    shape_f = ((rows, width), F32)
    shape_b = ((rows, width), BF16)
    shape_half = ((rows, half), BF16)
    shape_qkv = ((rows, 3 * half), BF16)
    shape_active = ((rows, half_ff), BF16)
    shape_stats = ((2 * STATS, QUAD), F32)
    shape_factor = ((STATS, QUAD), F32)
    shape_pairs = ((captions, half_image, 2 * width), BF16)
    shape_vec = ((8, width), F32)
    shape_bias = ((FOLDS, width), F32)
    shape_one = ((1, width), F32)
    half_scratch = [pltpu.VMEM((rows, half), BF16)]
    self_flops, feed_flops, pair_flops = 6 * rows * width * half, 4 * rows * width * half_ff, 4 * captions * half_image * width * width
    feed_blocks = [(i * width, (i + 1) * width) for i in (2, 0, 3, 1)]
    attn_blocks = [(0, width), (width, core_cols)]

    vecs, vecs_far, normed_a0, qkv_0, mixed_0, weights_0_far = call(
        functools.partial(self_first_kernel, aligned),
        place,
        [lengths, text_all, weights_0],
        [both((VECS, width), F32), save(*shape_b), save(*shape_qkv), shape_half],
        name="self_0",
        flops=self_flops,
        keep=(2,),
    )
    if not aligned:
        straight = lambda v: jnp.concatenate([v[:CROSS_GAIN], v[CROSS_GAIN : CROSS_GAIN + 2].reshape(2, count, 2, cross_piece).transpose(0, 2, 1, 3).reshape(2, width), v[CROSS_GAIN + 2 :]], 0)
        vecs, vecs_far = straight(vecs), straight(vecs_far)
    other_0 = swap(mixed_0)
    (mixed_0,) = meet([ring_f, ring_d], mixed_0)
    ring_f.pack()
    while ring_d.step < ring_d.steps:
        ring_d.move()
    other_0, ring_f.other = together(other_0, ring_f.other)
    feed_w0 = ring_f.result(place)
    keys, query, cross_out_w = reordered(cross_all, ring_order() if aligned else [0], 2, [2 * width, width, width])
    mixed_all_0, middle_0, normed_f0, slope_f0, active_0, part_0, feed_w0_far = call(
        feed_first_kernel,
        place,
        [text_all, mixed_0, other_0, vecs, weights_0, feed_w0],
        [save(*shape_b), save(*shape_f), save(*shape_b), save(*shape_active), save(*shape_active), shape_b],
        name="feed_0",
        flops=feed_flops,
        keep=(5,),
    )
    part_0_other = swap(part_0)
    (part_0,) = meet([ring_d], part_0)
    ring_d.pack()
    weights_1 = ring_d.result(place)
    hidden, hidden_far, normed_a1, qkv_1, mixed_1, weights_1_far = call(
        self_second_kernel,
        place,
        [lengths, late(middle_0), part_0, part_0_other, vecs, weights_1],
        [both(*shape_b), save(*shape_b), save(*shape_qkv), shape_half],
        name="self_1",
        flops=self_flops,
        keep=(5,),
    )
    other_1 = swap(mixed_1)
    pairs, keys_far = call(pairs_kernel, place, [late(image), keys], [shape_pairs], name="pairs", flops=pair_flops, keep=(1,))
    other_1, pairs = together(other_1, pairs)
    mixed_all_1, first_1, normed_c, queries, cross_part, stats, stats_far, query_far = call(
        cross_kernel,
        place,
        [hidden, mixed_1, other_1, vecs, weights_1, query, pairs],
        [save(*shape_b), save(*shape_f), save(*shape_b), save(*shape_b), shape_b, both(*shape_stats)],
        name="cross_1",
        flops=4 * rows * width * width,
        keep=(5,),
    )
    cross_part_other, stats_other = swap(cross_part), swap(stats)
    (feed_w1,) = reordered(feed_last, order, 1, [2 * half_ff])
    middle_1_far, cross_mixed_far, factor, normed_f1, slope_f1, active_1, part_1, cross_out_far = call(
        feed_second_kernel,
        place,
        [late(first_1), cross_part, cross_part_other, stats, stats_other, vecs, cross_out_w, feed_w1],
        [save(*shape_f), save(*shape_b), save(*shape_factor), shape_b, shape_active, shape_active, shape_b],
        name="feed_1",
        flops=feed_flops,
        keep=(6,),
    )
    own_cols = lambda v: pick(section, v[..., :half], v[..., half:])

    def meet_sums(rings, *values):
        flat = together(*[v for ring in rings for v in ring.front()], *values)
        for i, ring in enumerate(rings):
            ring.put_front(flat[2 * i : 2 * i + 2])
        return flat[2 * len(rings) :]

    def scatter(value):
        return lax.psum_scatter(value, "dp", scatter_dimension=0, tiled=True, axis_index_groups=groups)

    bias_grad_1, down_bias_grad_1, slope_1, back_1 = call(
        feed_back_last_kernel, place, [cot_all, vecs, feed_w1, slope_f1], [save(*shape_bias), save(*shape_one), shape_active, shape_b], name="feed_back_1", flops=feed_flops
    )
    back_1_other = swap(back_1)
    (feed_grad_1,) = call(
        functools.partial(products_kernel, order, ((0, 1), (2, 3))),
        place,
        [normed_f1, slope_1, active_1, cot_all],
        [save((width, 2 * half_ff), BF16)],
        name="feed_grads_1",
        flops=feed_flops,
    )
    back_1_other, feed_grad_1 = together(back_1_other, feed_grad_1)
    feed_got_1 = scatter(feed_grad_1)
    grad_middle_1, grad_low_1, feed_vec_1, query_part, grad_pairs = call(
        cross_back_kernel,
        place,
        [late(cot_all), back_1, back_1_other, late(middle_1_far), late(vecs_far), late(cross_out_far), late(queries), pairs, late(stats_far), late(factor), late(cross_mixed_far)],
        [shape_f, shape_b, save(*shape_vec), shape_b, shape_pairs],
        scratch=[pltpu.VMEM((rows, width), BF16)],
        name="cross_back",
        flops=4 * rows * width * width,
    )
    query_part_other = swap(query_part)
    ring_shape = lambda cols: ((count // 2, piece, cols), BF16)
    second_cols = 3 * half + 3 * width
    if aligned:
        keys_grads = call(
            functools.partial(keys_products_kernel, count, 3 * half + width),
            place,
            [late(image), grad_pairs],
            [save(*ring_shape(second_cols)), save(*ring_shape(second_cols))],
            vmem=20,
            name="keys_grads",
            flops=pair_flops,
        )
        query_part_other, *keys_grads = together(query_part_other, *keys_grads)
    grad_first_1, head_low_1, grad_queries, grad_qkv_1, self_back_1, cross_vec_1 = call(
        self_back_second_kernel,
        place,
        [lengths, grad_middle_1, query_part, query_part_other, late(first_1), late(vecs_far), late(query_far), late(weights_1_far, *attn_blocks), late(qkv_1)],
        [shape_f, save(*shape_b), shape_b, shape_qkv, shape_b, save(*shape_vec)],
        scratch=half_scratch,
        name="self_back_1",
        flops=2 * self_flops,
    )
    self_back_1_other = swap(self_back_1)
    if aligned:
        second_grads = call(
            functools.partial(second_products_kernel, count),
            place,
            [late(normed_c), grad_queries, late(cross_mixed_far), grad_low_1, late(normed_a1), grad_qkv_1],
            [save(*ring_shape(second_cols)), save(*ring_shape(second_cols))],
            vmem=20,
            name="second_grads",
            flops=2 * rows * width * (width + 3 * half),
            over=keys_grads,
        )
    else:
        pair_rows = lambda v: v.reshape(2, count, cross_piece, v.shape[1]).transpose(1, 0, 2, 3).reshape(width, v.shape[1])
        flat = lambda v: v.reshape(captions * half_image, v.shape[2])
        heads = pair_rows(jnp.concatenate([dot_tn(own_cols(normed_c), grad_queries), dot_tn(own_cols(cross_mixed_far), grad_low_1)], 0))
        second_grad = low(jnp.concatenate([dot_tn(normed_a1, grad_qkv_1), heads, pair_rows(dot_tn(flat(image), flat(grad_pairs)))], 1))
        parts = second_grad.reshape(count // 2, 2, piece, second_cols)
        second_grads = pick(core, parts[:, 0], parts[:, 1]), pick(core, parts[:, 1], parts[:, 0])
    self_back_1_other, *second_grads = together(self_back_1_other, *second_grads)
    ring_second = Scatter(*second_grads)
    ring_second.begin()
    (self_back_1_other,) = ring_second.step(self_back_1_other)
    grad_hidden, grad_hidden_low, self_vec_1, bias_grad_0, down_bias_grad_0, slope_0, back_0 = call(
        feed_back_first_kernel,
        place,
        [grad_first_1, self_back_1, self_back_1_other, late(hidden_far), late(vecs_far), late(feed_w0_far, *feed_blocks), late(slope_f0)],
        [shape_f, shape_b, save(*shape_vec), save(*shape_bias), save(*shape_one), shape_active, shape_b],
        name="feed_back_0",
        flops=feed_flops,
    )
    back_0_other = swap(back_0)
    (back_0,) = meet_sums([ring_second], back_0)
    (slope_0,) = ring_second.step(slope_0)
    (feed_grad_0,) = call(
        functools.partial(products_kernel, order, ((0, 1), (2, 3))),
        place,
        [late(normed_f0), slope_0, late(active_0), grad_hidden_low],
        [save((width, 2 * half_ff), BF16)],
        name="feed_grads_0",
        flops=feed_flops,
    )
    back_0_other, feed_grad_0, up, down = together(back_0_other, feed_grad_0, *ring_second.front())
    ring_second.put_front((up, down))
    feed_got_0 = scatter(feed_grad_0)
    (back_0_other,) = ring_second.step(back_0_other)
    grad_middle_0, head_low_0, grad_qkv_0, self_back_0, vecs_grad_0 = call(
        self_back_first_kernel,
        place,
        [lengths, grad_hidden, back_0, back_0_other, late(middle_0), text_all, late(vecs_far), late(weights_0_far, *attn_blocks), late(qkv_0)],
        [shape_f, shape_b, shape_qkv, shape_b, shape_vec],
        scratch=half_scratch,
        name="self_back_0",
        flops=2 * self_flops,
    )
    self_back_0_other = swap(self_back_0)
    (grad_qkv_0,) = meet_sums([ring_second], grad_qkv_0)
    (grad_qkv_0,) = ring_second.step(grad_qkv_0)
    cross_vec_woven = cross_vec_1
    if not aligned:
        cross_vec_woven = cross_vec_1.reshape(8, 2, count, cross_piece).transpose(0, 2, 1, 3).reshape(8, width)
    last_grads = call(
        functools.partial(last_products_kernel, count if aligned else 0),
        place,
        [late(normed_a0), grad_qkv_0, late(mixed_all_0), late(mixed_all_1), head_low_0, late(head_low_1), vecs_grad_0]
        + [late(v) for v in (self_vec_1, feed_vec_1, cross_vec_woven, down_bias_grad_0, down_bias_grad_1, bias_grad_0, bias_grad_1)],
        [save(*ring_shape(core_cols + 128)), ring_shape(core_cols + 128)],
        name="last_grads",
        flops=2 * rows * width * core_cols,
    )
    *last_grads, feed_got_1, self_back_0_other = meet_sums([ring_second], *last_grads, feed_got_1, self_back_0_other)
    ring_last = Scatter(*last_grads)
    ring_last.begin()
    (grad_middle_0,) = ring_last.step(grad_middle_0)
    second_got = low(ring_second.result())
    (text_grad,) = call(text_grad_kernel, place, [grad_middle_0, self_back_0, self_back_0_other, text_all, late(vecs_far)], [((rows, half), F32)], name="text_grad")
    text_grad, second_got = meet_sums([ring_last], text_grad, second_got)
    (grad_pairs,) = ring_last.step(grad_pairs)
    image_grad = by_caption(image_grad_kernel, grad_pairs, keys_far, jax.ShapeDtypeStruct((captions, half_image, width), F32), "image_grad", pair_flops)
    (image_grad,) = meet_sums([ring_last], image_grad)
    ring_last.step()

    def other_half(first, later):
        return swap(pick(section, low(later), low(first)))

    (feed_got_0,) = meet_sums([ring_last], feed_got_0)
    feed_other = other_half(feed_got_0, feed_got_1)
    ring_last.step()
    got_part = swap(pick(section, part_1[:, half:], part_1[:, :half]))
    layer_out = own_cols(middle_1_far) + (own_cols(part_1).astype(F32) + got_part.astype(F32)) + own_cols(vecs_far[LAYER_VECS + DOWN_BIAS])
    cross_got = second_got[:, 3 * half : 3 * half + width]
    keys_got = second_got[:, 3 * half + width :]
    keys_other = swap(pick(section, keys_got[cross_piece:], keys_got[:cross_piece]))
    feed_own = pick(section, feed_got_0, feed_got_1)
    into_got_1 = second_got[:, : 3 * half]
    if aligned:
        up_grad, down_grad = call(
            functools.partial(finish_feed_kernel, count),
            place,
            [feed_own, feed_other],
            [((piece, 2 * half_ff), F32), ((2 * FOLDS * piece, width), F32)],
            name="finish_feed",
        )
        cross_query_grad, cross_keys_grad, cross_out_grad = call(
            finish_cross_kernel,
            place,
            [cross_got, keys_got, keys_other],
            [((cross_piece, width), F32), ((cross_piece, 2 * width), F32), ((cross_piece, width), F32)],
            name="finish_cross",
        )
        keys_other, cross_query_grad = together(keys_other, cross_query_grad)
    else:
        feed_parts = [v.astype(F32) for v in (pick(section, feed_own, feed_other), pick(section, feed_other, feed_own))]
        up_parts = [v[:, :half_ff].reshape(piece, FOLDS, count, piece).transpose(0, 2, 1, 3) for v in feed_parts]
        up_grad = jnp.stack(up_parts, 2).reshape(piece, 2 * half_ff)
        down_parts = [v[:, half_ff:].reshape(piece, FOLDS, width).transpose(1, 0, 2) for v in feed_parts]
        down_grad = jnp.stack(down_parts, 0).reshape(2 * FOLDS * piece, width)
        cross_query_grad, cross_out_grad = cross_got[:cross_piece].astype(F32), cross_got[cross_piece:].astype(F32)
        own_keys = pick(section, keys_got[:cross_piece], keys_got[cross_piece:])
        cross_keys_grad = own_keys.astype(F32) + keys_other.astype(F32)
    last_got = ring_last.result()
    vec_got = last_got[:, core_cols:]
    last_other = swap(low(jnp.concatenate([pick(section, into_got_1.astype(F32), last_got[:, : 3 * half]), vec_got], 1)))
    into_own = pick(section, last_got[:, : 3 * half], into_got_1.astype(F32))
    if aligned:
        shape_row = ((1, piece), F32)
        heads_in_grad, heads_out_grad, *rows_out, up_bias_grad = call(
            functools.partial(finish_heads_kernel, cross_piece),
            place,
            [last_got, into_own, last_other],
            [((piece, 6 * half), F32), ((piece, width), F32)] + [shape_row] * 5 + [((1, cross_piece), F32)] * 2 + [((1, 2 * FOLDS * piece), F32)],
            name="finish_heads",
        )
        cross_gain_grad, cross_shift_grad = rows_out[5][0], rows_out[6][0]
    else:
        into_other = last_other[:, : 3 * half].astype(F32)
        into_parts = pick(section, into_own, into_other), pick(section, into_other, into_own)
        heads_in_grad = jnp.stack([v.reshape(piece, 3, half) for v in into_parts], 2).reshape(piece, 6 * half)
        heads_out_grad = last_got[:, 3 * half : core_cols]
        own_vec, other_vec = vec_got.T, last_other[:, 3 * half :].astype(F32).T
        mine = lambda v, begin, size: pick(section, v[begin : begin + size], v[begin + size : begin + 2 * size])
        self_vec = mine(own_vec, 0, 2) + mine(other_vec, 0, 2)
        rows_out = [self_vec[0:1], self_vec[1:2], own_vec[4:5], own_vec[5:6], own_vec[6:7]]
        bias = mine(own_vec, 7, FOLDS), mine(other_vec, 7, FOLDS)
        up_bias_grad = jnp.concatenate([pick(section, *bias), pick(section, *bias[::-1])], 0).reshape(1, 2 * FOLDS * piece)
        cross_vec = pick(section, own_vec[7 + 2 * FOLDS : 9 + 2 * FOLDS, :cross_piece], own_vec[7 + 2 * FOLDS : 9 + 2 * FOLDS, cross_piece:])
        cross_gain_grad, cross_shift_grad = cross_vec[0], cross_vec[1]
    return (
        layer_out,
        text_grad,
        image_grad,
        rows_out[0],
        rows_out[1],
        heads_in_grad[None],
        heads_out_grad[None],
        rows_out[2],
        rows_out[3],
        up_grad[None],
        up_bias_grad,
        down_grad[None],
        rows_out[4],
        cross_gain_grad,
        cross_shift_grad,
        cross_query_grad,
        cross_keys_grad,
        cross_out_grad,
    )


def solution(mesh):
    placed = (
        P("dp", "section"),
        P("dp", "section", None),
        P("dp"),
        P("section", "dp"),
        P("section", "dp"),
        P("section", "dp", None),
        P("section", "dp", None),
        P("section", "dp"),
        P("section", "dp"),
        P("section", "dp", None),
        P("section", "dp"),
        P("section", "dp", None),
        P("section", "dp"),
        P(("section", "dp")),
        P(("section", "dp")),
        P(("section", "dp"), None),
        P(("section", "dp"), None),
        P(("section", "dp"), None),
        P("dp", "section"),
    )
    return jax.shard_map(
        body,
        mesh=mesh,
        in_specs=placed,
        out_specs=(P("dp", "section"), P("dp", "section"), P("dp", "section", None)) + placed[3:18],
        check_vma=False,
    )
```

```python
import functools

import jax
import jax.numpy as jnp
from jax import lax
from jax.experimental import pallas as pl
from jax.experimental.pallas import tpu as pltpu
from jax.sharding import PartitionSpec as P

HEAD_DIM = 64
PAIR = 2 * HEAD_DIM
QUAD = 4 * HEAD_DIM
EPS = 1e-05
MASKED = -1000000000.0
SCALE = HEAD_DIM**-0.5
F32 = jnp.float32
BF16 = jnp.bfloat16
MIB = 1 << 20


def swap(value):
    return lax.ppermute(value, "section", [(0, 1), (1, 0)])


def pick(section, first, later):
    return jnp.where(section == 0, first, later)


def side(own, other, section, axis):
    return jnp.concatenate([pick(section, own, other), pick(section, other, own)], axis)


def low(values):
    return values.astype(BF16)


def ring_chip(place, chips):
    return jnp.where(place < chips // 2, 2 * place, 2 * (chips - 1 - place) + 1)


def ring_order():
    chips = lax.axis_size("dp") // 2
    return list(range(0, chips, 2)) + list(range(chips - 1, 0, -2))


def ring_steps(shift):
    order = ring_order()
    chips = len(order)
    return [(2 * order[i] + core, 2 * order[(i + shift) % chips] + core) for i in range(chips) for core in range(2)]


def ring_move(value, shift):
    return lax.ppermute(value, "dp", ring_steps(shift))


def core_swap(value):
    return lax.ppermute(value, "dp", [(i, i ^ 1) for i in range(lax.axis_size("dp"))])


def my_place():
    chips = lax.axis_size("dp") // 2
    me = lax.axis_index("dp")
    chip, core = me // 2, me % 2
    return jnp.where(chip % 2 == 0, chip // 2, chips - 1 - chip // 2), core


def pack_kernel(cut, spots, *refs):
    *sources, out = refs
    chips = out.shape[0]
    for i, source in enumerate(sources[: chips - 1]):
        out[spots[i]] = source[...]
    out[spots[chips - 1], :, :cut] = sources[chips - 1][...]
    out[spots[chips - 1], :, cut:] = sources[chips][...]


def join_kernel(place, mine, other, out):
    core = place[1]
    for chip in range(mine.shape[0]):
        out[2 * chip + core] = mine[chip]
        out[2 * chip + 1 - core] = other[chip]


def reorder_kernel(order, parts, place, source, *outs):
    rows = source.shape[0] // len(order)
    width = sum(out.shape[1] for out in outs)
    for part in range(parts):
        offset = part * width
        for out in outs:
            for i, spot in enumerate(order):
                begin = part * source.shape[0] + spot * rows
                out[begin : begin + rows, :] = source[i * rows : (i + 1) * rows, offset : offset + out.shape[1]]
            offset += out.shape[1]


class Gather:
    def __init__(self, shard):
        self.chips = lax.axis_size("dp") // 2
        self.steps = self.chips // 2
        self.rows, self.width = shard.shape
        self.cut = self.width // 256 * 128
        self.got = {0: shard}
        self.step = 0
        self.last = ()

    def front(self):
        return self.last or (self.got[-self.step], self.got[self.step])

    def put_front(self, values):
        if self.last:
            self.last = values
        else:
            self.got[-self.step], self.got[self.step] = values

    def move(self):
        self.step += 1
        up, down = self.got[1 - self.step], self.got[self.step - 1]
        if self.step < self.steps:
            self.got[-self.step], self.got[self.step] = ring_move(up, 1), ring_move(down, -1)
        else:
            self.last = (ring_move(up[:, : self.cut], 1), ring_move(down[:, self.cut :], -1))

    def pack(self):
        chips, half = self.chips, self.steps
        steps = list(range(1 - half, half + 1))
        place, _ = my_place()
        spots = jnp.stack([ring_chip((place + step + chips) % chips, chips) for step in steps]).astype(jnp.int32)
        (self.mine,) = call(
            functools.partial(pack_kernel, self.cut), spots, [self.got[step] for step in steps[:-1]] + list(self.last), [((chips, self.rows, self.width), BF16)], name="pack"
        )
        self.other = core_swap(self.mine)

    def result(self, place):
        rows = 2 * self.chips * self.rows
        if self.rows % 16 == 0:
            (full,) = call(join_kernel, place, [self.mine, self.other], [((2 * self.chips, self.rows, self.width), BF16)], name="join")
            return full.reshape(rows, self.width)
        first, later = pick(place[1], self.mine, self.other), pick(place[1], self.other, self.mine)
        return jnp.stack([first, later], 1).reshape(rows, self.width)


def together(*values):
    return lax.optimization_barrier(values)


def meet(rings, *values):
    fronts = [ring.front() for ring in rings]
    flat = together(*[v for front in fronts for v in front], *values)
    for i, ring in enumerate(rings):
        ring.put_front((flat[2 * i], flat[2 * i + 1]))
    return flat[2 * len(rings) :]


class Scatter:
    def __init__(self, mine, sent):
        self.mine, self.sent = mine, sent
        self.chips, self.rows, self.width = mine.shape
        self.steps = self.left = self.chips // 2
        self.cut = self.width // 256 * 128
        self.place, _ = my_place()

    def begin(self):
        self.got = core_swap(self.sent)

    def own(self, step, begin=0, end=None):
        chip = ring_chip((self.place + step + self.chips) % self.chips, self.chips)
        cut_out = lambda v: lax.dynamic_index_in_dim(v, chip, 0, False)[:, begin:end].astype(F32)
        return cut_out(self.mine) + cut_out(self.got)

    def front(self):
        return self.up, self.down

    def put_front(self, values):
        self.up, self.down = values

    def step(self, *pins):
        left, cut = self.left, self.cut
        if left == self.steps:
            up, down = self.own(left, 0, cut), self.own(-left, cut)
        else:
            up, down = self.added()
            up, down = self.own(left) + up, self.own(-left) + down
        up, down, *pins = together(low(up), low(down), *pins)
        self.up, self.down = ring_move(up, 1), ring_move(down, -1)
        self.left -= 1
        return pins

    def added(self):
        up, down = self.up.astype(F32), self.down.astype(F32)
        if self.left == self.steps - 1:
            up = jnp.concatenate([up, jnp.zeros((self.rows, self.width - self.cut), F32)], 1)
            down = jnp.concatenate([jnp.zeros((self.rows, self.cut), F32), down], 1)
        return up, down

    def after_here(self, *values):
        self.mine, self.got, *_ = together(self.mine, self.got, *values)

    def result(self):
        up, down = self.added()
        return self.own(0) + up + down


def norm_unit(values):
    centred = values - jnp.mean(values, -1, keepdims=True)
    scale = lax.rsqrt(jnp.mean(centred * centred, -1, keepdims=True) + EPS)
    return centred * scale, scale


def norm_back(values, gain, grad):
    unit, scale = norm_unit(values)
    wide = grad * gain
    inner = wide - jnp.mean(wide, -1, keepdims=True) - unit * jnp.mean(wide * unit, -1, keepdims=True)
    return inner * scale, jnp.sum(grad * unit, 0, keepdims=True), jnp.sum(grad, 0, keepdims=True)


def dot(left, right):
    return jnp.dot(left, right, preferred_element_type=F32)


def dot_tn(left, right):
    return lax.dot_general(left, right, (((0,), (0,)), ((), ())), preferred_element_type=F32)


def dot_nt(left, right):
    return lax.dot_general(left, right, (((1,), (1,)), ((), ())), preferred_element_type=F32)


def heads_of(shape):
    return lax.broadcasted_iota(jnp.int32, shape, 1) // HEAD_DIM


def stacked(block):
    head = heads_of(block.shape)
    zero = jnp.zeros_like(block)
    return jnp.concatenate([jnp.where(head == h, block, zero) for h in range(block.shape[1] // HEAD_DIM)], 0)


def unstacked(rows):
    heads = rows.shape[1] // HEAD_DIM
    slots = rows.shape[0] // heads
    head = heads_of((slots, rows.shape[1]))
    out = rows[:slots]
    for h in range(1, heads):
        out = jnp.where(head == h, rows[h * slots : (h + 1) * slots], out)
    return out


def row_sums(values):
    high = low(values)
    rest = low(values - high.astype(F32))
    ones = jnp.ones((8, values.shape[1]), BF16)
    return (dot_nt(ones, high) + dot_nt(ones, rest))[0:1]


def keep_mask(length, slots):
    query = lax.broadcasted_iota(jnp.int32, (2 * slots, slots), 0) % slots
    key = lax.broadcasted_iota(jnp.int32, (2 * slots, slots), 1)
    return (key <= query) & (key < length)


def self_chances(queries, keys, keep):
    scores = jnp.where(keep, dot_nt(queries, keys) * SCALE, MASKED)
    raised = jnp.exp(scores - jnp.max(scores, -1, keepdims=True))
    return raised / jnp.sum(raised, -1, keepdims=True)


def keep_mask_turned(length, slots):
    key = lax.broadcasted_iota(jnp.int32, (slots, 2 * slots), 0)
    query = lax.broadcasted_iota(jnp.int32, (slots, 2 * slots), 1) % slots
    return (key <= query) & (key < length)


def self_chances_turned(queries, keys, keep):
    scores = jnp.where(keep, dot_nt(keys, queries) * SCALE, MASKED)
    raised = jnp.exp(scores - jnp.max(scores, 0, keepdims=True))
    return raised / jnp.sum(raised, 0, keepdims=True)


class Late:
    def __init__(self, source, scratch, sems, blocks):
        self.scratch, self.shape = scratch, scratch.shape
        self.copies = {}
        for i, (begin, end) in enumerate(blocks or [(0, None)]):
            here = (slice(None), slice(begin, end)) if blocks else Ellipsis
            copy = pltpu.make_async_copy(source.at[here] if blocks else source, scratch.at[here] if blocks else scratch, sems.at[i])
            copy.start()
            self.copies[(begin, end)] = copy

    def __getitem__(self, index):
        wanted = index[-1] if isinstance(index, tuple) and len(self.shape) == 2 else slice(None)
        low_end, high_end = wanted.start or 0, wanted.stop or self.shape[-1]
        for block in list(self.copies):
            if block[0] < high_end and (block[1] is None or block[1] > low_end):
                self.copies.pop(block).wait()
        return self.scratch[index]


class Save:
    def __init__(self, buffer, target, sems):
        self.buffer, self.target, self.sems, self.shape = buffer, target, sems, buffer.shape
        self.copies, self.whole = [], False

    def __getitem__(self, index):
        return self.buffer[index]

    def __setitem__(self, index, value):
        self.buffer[index] = value

    def flush(self, cols=None):
        if self.whole:
            return
        self.whole = cols is None
        here = (slice(None),) * (len(self.shape) - 1) + (cols,)
        copy = pltpu.make_async_copy(self.buffer if cols is None else self.buffer.at[here], self.target if cols is None else self.target.at[here], self.sems.at[len(self.copies)])
        copy.start()
        self.copies.append(copy)


def flush(ref, cols=None):
    if isinstance(ref, Save):
        ref.flush(cols)


def late(array, *blocks):
    return (array, blocks)


def save(shape, dtype):
    return (shape, dtype, "save")


def both(shape, dtype):
    return (shape, dtype, "both")


FLUSHES = 10


def run_kernel(kernel, in_kinds, out_kinds, kept, n_over, n_fetch, n_results, *refs):
    n_ins = 1 + len(in_kinds) + n_over + n_fetch
    ins, results, scratch = refs[1:n_ins], list(refs[n_ins : n_ins + n_results]), list(refs[n_ins + n_results :])
    given = []
    for ref, blocks in zip(ins, in_kinds):
        given.append(ref if blocks is None else Late(ref, scratch.pop(0), scratch.pop(0), blocks))
    saves, outs = [], []
    for i in kept:
        saves.append(Save(ins[i], results.pop(), scratch.pop(0)))
        saves[-1].flush()
    fetches = []
    for i in range(n_fetch):
        copy = pltpu.make_async_copy(refs[n_ins - n_fetch + i], results[len(results) - n_fetch + i], scratch.pop(0).at[0])
        copy.start()
        fetches.append(copy)
    results = results[: len(results) - n_fetch]
    for kind in out_kinds:
        if kind == "near":
            outs.append(results.pop(0))
            continue
        buffer = scratch.pop(0) if kind == "save" else results.pop(0)
        saves.append(Save(buffer, results.pop(0), scratch.pop(0)))
        outs.append(saves[-1])
    kernel(refs[0], *given, *outs, *scratch)
    for item in saves:
        if not item.copies:
            item.flush()
    for item in saves:
        for copy in item.copies:
            copy.wait()
    for copy in fetches:
        copy.wait()


def call(kernel, place, ins, outs, scratch=(), vmem=14, name=None, flops=0, keep=(), over=(), fetch=()):
    smem, near, far = pl.BlockSpec(memory_space=pltpu.SMEM), pl.BlockSpec(memory_space=pltpu.VMEM), pl.BlockSpec(memory_space=pl.ANY)
    in_specs, arrays, in_kinds, buffers = [smem], [place], [], []
    for entry in ins:
        if isinstance(entry, tuple):
            array, blocks = entry
            array = pltpu.with_memory_space_constraint(array, pltpu.HBM)
            in_specs.append(far)
            in_kinds.append(tuple(blocks))
            buffers += [pltpu.VMEM(array.shape, array.dtype), pltpu.SemaphoreType.DMA((max(1, len(blocks)),))]
        else:
            array = entry
            in_specs.append(smem if array.dtype == jnp.int32 else near)
            in_kinds.append(None)
        arrays.append(array)
    for array in over:
        in_specs.append(far)
        arrays.append(pltpu.with_memory_space_constraint(array, pltpu.HBM))
    for array in fetch:
        in_specs.append(far)
        arrays.append(pltpu.with_memory_space_constraint(array, pltpu.HBM))
    buffers += [pltpu.SemaphoreType.DMA((1,)) for _ in list(keep) + list(fetch)]
    out_specs, out_shapes, out_kinds = [], [], []
    for entry in outs:
        shape, dtype, kind = entry if len(entry) == 3 else entry + ("near",)
        out_kinds.append(kind)
        if kind != "save":
            out_specs.append(near)
            out_shapes.append(jax.ShapeDtypeStruct(shape, dtype))
        else:
            buffers.append(pltpu.VMEM(shape, dtype))
        if kind != "near":
            out_specs.append(far)
            out_shapes.append(pltpu.HBM(shape, dtype))
            buffers.append(pltpu.SemaphoreType.DMA((FLUSHES,)))
    for array in fetch:
        out_specs.append(near)
        out_shapes.append(jax.ShapeDtypeStruct(array.shape, array.dtype))
    for i in reversed(keep):
        out_specs.append(far)
        out_shapes.append(pltpu.HBM(ins[i].shape, ins[i].dtype))
    moved = sum(a.size * a.dtype.itemsize for a in arrays)
    return pl.pallas_call(
        functools.partial(run_kernel, kernel, tuple(in_kinds), tuple(out_kinds), tuple(keep), len(over), len(fetch), len(out_shapes)),
        in_specs=in_specs,
        out_specs=out_specs,
        out_shape=out_shapes,
        scratch_shapes=buffers + list(scratch),
        input_output_aliases={1 + len(ins) + i: i for i in range(len(over))},
        compiler_params=pltpu.CompilerParams(vmem_limit_bytes=vmem * MIB),
        cost_estimate=pl.CostEstimate(flops=flops, bytes_accessed=moved, transcendentals=0),
        name=name,
    )(*arrays)


def prepare_kernel(count, place, into, out, up, down, vectors, up_bias, cross_gain, cross_shift, sent, own_attn, own_feed, own_vecs):
    rows, width = out.shape
    half = width // 2
    section = place[0]

    def choose(make):
        first, later = make(0), make(1)
        return jnp.where(section == 0, first, later), jnp.where(section == 0, later, first)

    def feed_of(side_index):
        parts = []
        for fold in range(FOLDS):
            for device in range(count):
                begin = ((device * 2 + side_index) * FOLDS + fold) * rows
                parts.append(up[:, begin : begin + rows])
        parts += [down[(side_index * FOLDS + fold) * rows : (side_index * FOLDS + fold + 1) * rows, :] for fold in range(FOLDS)]
        return jnp.concatenate(parts, 1)

    attn, attn_other = choose(lambda i: jnp.concatenate([into[:, (2 * j + i) * half : (2 * j + i + 1) * half] for j in range(3)], 1))
    feed, feed_other = choose(feed_of)
    wide = lambda v: jnp.concatenate([v, jnp.zeros((v.shape[0], 128 - v.shape[1]), F32)], 1)
    lines = [wide(vectors[...].astype(F32))] + [wide(up_bias[:, i * rows : (i + 1) * rows].astype(F32)) for i in range(2 * FOLDS)]
    lines += [wide(cross_gain[...].astype(F32)), wide(cross_shift[...].astype(F32))]
    vecs = low(jnp.concatenate(lines + [jnp.zeros((128 - LAYER_VECS - 2, 128), F32)], 0).T[:rows])
    own_attn[:, :width] = out[...]
    own_attn[:, width:] = attn
    own_feed[...] = feed
    own_vecs[...] = vecs
    cols = width + 3 * half
    sent[:, :width] = out[...]
    sent[:, width:cols] = attn_other
    sent[:, cols : cols + 128] = vecs
    sent[:, cols + 128 :] = feed_other


def merge_kernel(place, got, own_attn, own_feed, own_vecs, attn_first, attn_last, feed_first, feed_last):
    section = place[0]
    cols = own_attn.shape[1]
    first, last = (lambda own, other: jnp.where(section == 0, own, other)), (lambda own, other: jnp.where(section == 0, other, own))
    attn, attn_other = own_attn[...], got[:, :cols]
    attn_first[:, :cols] = first(attn, attn_other)
    attn_last[...] = last(attn, attn_other)
    feed, feed_other = own_feed[...], got[:, cols + 128 :]
    feed_first[...] = first(feed, feed_other)
    feed_last[...] = last(feed, feed_other)
    vecs, vecs_other = own_vecs[...].astype(F32), got[:, cols : cols + 128].astype(F32)
    vecs_0, vecs_1 = first(vecs, vecs_other), last(vecs, vecs_other)
    half = vecs.shape[0] // 2
    cross = jnp.concatenate([vecs_0[:half], vecs_1[:half]], 0)
    lane = lax.broadcasted_iota(jnp.int32, vecs.shape, 1)
    turned = lambda v: pltpu.roll(v, LAYER_VECS, 1)
    attn_first[:, cols:] = low(jnp.where(lane < LAYER_VECS, vecs_0, jnp.where(lane < 2 * LAYER_VECS, turned(vecs_1), turned(cross))))


SELF_GAIN, SELF_SHIFT, FEED_GAIN, FEED_SHIFT, DOWN_BIAS, UP_BIAS = range(6)
FOLDS = 2
LAYER_VECS = 5 + 2 * FOLDS
CROSS_GAIN, CROSS_SHIFT = 2 * LAYER_VECS, 2 * LAYER_VECS + 1
VECS = 24


def woven(first, later, blocks):
    parts = [v.reshape(blocks, v.shape[0] // blocks, v.shape[1]) for v in (first, later)]
    return jnp.concatenate(parts, 1).reshape(2 * first.shape[0], first.shape[1])


def unwoven(value, blocks):
    parts = value.reshape(blocks, value.shape[0] // blocks, value.shape[1])
    half = parts.shape[1] // 2
    return jnp.concatenate([parts[:, :half].reshape(-1, value.shape[1]), parts[:, half:].reshape(-1, value.shape[1])], 0)


def side_in(section, own, other):
    first = jnp.where(section == 0, own, other)
    return jnp.concatenate([first, jnp.where(section == 0, other, own)], 1)


def half_in(section, values):
    half = values.shape[1] // 2
    return jnp.where(section == 0, values[:, :half], values[:, half:])


def vec(ref, row):
    return ref[row : row + 1, :]


def up_bias_of(vecs, layer, section, fold):
    return vecs[pl.ds(LAYER_VECS * layer + UP_BIAS + FOLDS * section + fold, 1), :]


def self_part(values, layer, lengths, vecs, weights, normed_ref, projected, mixed_ref):
    base = LAYER_VECS * layer
    unit, _ = norm_unit(values)
    normed = low(unit * vec(vecs, base + SELF_GAIN) + vec(vecs, base + SELF_SHIFT))
    normed_ref[...] = normed
    flush(normed_ref)
    half = mixed_ref.shape[1]
    width = values.shape[1]
    projected[...] = low(dot(normed, weights[:, width : width + 3 * half]))
    flush(projected)
    captions = lengths.shape[0]
    slots = values.shape[0] // captions
    for c in range(captions):
        keep = keep_mask(lengths[c], slots)
        here = slice(c * slots, (c + 1) * slots)
        for j in range(half // PAIR):
            q, k, v = (projected[here, i * half + j * PAIR : i * half + (j + 1) * PAIR] for i in range(3))
            chances = self_chances(stacked(q), k, keep)
            mixed_ref[here, j * PAIR : (j + 1) * PAIR] = low(unstacked(dot(low(chances), v)))


def self_first_kernel(aligned, place, lengths, text, weights, vecs, normed, projected, mixed):
    columns = weights[:, weights.shape[1] - 128 :].astype(F32)
    if aligned:
        lane = lax.broadcasted_iota(jnp.int32, columns.shape, 1)
        columns = jnp.where(lane < CROSS_GAIN, columns, unwoven(columns, weights.shape[0] // 48))
    vecs[...] = columns.T[: vecs.shape[0]]
    flush(vecs)
    self_part(text[...].astype(F32), 0, lengths, vecs, weights, normed, projected, mixed)


def self_second_kernel(place, lengths, middle, own, other, vecs, weights, hidden, normed, projected, mixed):
    total = middle[...] + (own[...].astype(F32) + other[...].astype(F32)) + vec(vecs, DOWN_BIAS)
    hidden[...] = low(total)
    flush(hidden)
    self_part(hidden[...].astype(F32), 1, lengths, vecs, weights, normed, projected, mixed)


def heads_rows(weights, section):
    width = weights.shape[0]
    return weights[pl.ds(pl.multiple_of(section * (width // 2), width // 2), width // 2), :width]


def add_heads_out(values, mixed, weights):
    return values + dot(mixed[...], weights[:, : values.shape[1]])


def feed_part(middle, layer, section, vecs, feed, normed_ref, slope_ref, active_ref):
    base = LAYER_VECS * layer
    width = middle.shape[1]
    unit, _ = norm_unit(middle)
    normed = low(unit * vec(vecs, base + FEED_GAIN) + vec(vecs, base + FEED_SHIFT))
    normed_ref[...] = normed
    flush(normed_ref)
    total = jnp.zeros_like(middle)
    for i in range(FOLDS):
        here = slice(i * width, (i + 1) * width)
        raised = dot(normed, feed[:, here]) + up_bias_of(vecs, layer, section, i)
        chance = 0.5 * (1.0 + lax.erf(raised * 0.5**0.5))
        slope_ref[:, here] = low(chance + raised * jnp.exp(-0.5 * raised * raised) * 0.3989422804014327)
        active = low(raised * chance)
        active_ref[:, here] = active
        flush(slope_ref, here)
        flush(active_ref, here)
        total += dot(active, feed[:, (FOLDS + i) * width : (FOLDS + i + 1) * width])
    return low(total)


def feed_first_kernel(place, text, own, other, vecs, weights, feed, mixed_all, middle, normed, slope, active, part):
    mixed_all[...] = side_in(place[0], own[...], other[...])
    flush(mixed_all)
    values = add_heads_out(text[...].astype(F32), mixed_all, weights)
    middle[...] = values
    flush(middle)
    part[...] = feed_part(values, 0, place[0], vecs, feed, normed, slope, active)


def by_caption(kernel, array, weights, out, name, flops):
    block = lambda shape: pl.BlockSpec((1,) + shape[1:], lambda i: (i, 0, 0))
    moved = array.size * array.dtype.itemsize + out.size * out.dtype.itemsize
    return pl.pallas_call(
        kernel,
        grid=(array.shape[0],),
        in_specs=[block(array.shape), pl.BlockSpec(weights.shape, lambda i: (0, 0))],
        out_specs=block(out.shape),
        out_shape=pltpu.HBM(out.shape, out.dtype),
        compiler_params=pltpu.CompilerParams(vmem_limit_bytes=24 * MIB),
        cost_estimate=pl.CostEstimate(flops=flops, bytes_accessed=moved, transcendentals=0),
        name=name,
    )(array, weights)


def pairs_kernel(place, image, keys, pairs):
    for c in range(image.shape[0]):
        pairs[c] = low(dot(image[c], keys[...]))


def image_grad_kernel(grad_pairs, keys, grad):
    grad[0] = dot_nt(grad_pairs[0], keys[...])


def cross_kernel(place, hidden, own, other, vecs, weights, query, pairs, mixed_all, first, normed_ref, queries, part, stats):
    mixed_all[...] = side_in(place[0], own[...], other[...])
    flush(mixed_all)
    values = add_heads_out(hidden[...].astype(F32), mixed_all, weights)
    first[...] = values
    flush(first)
    unit, _ = norm_unit(values)
    normed = low(unit * vec(vecs, CROSS_GAIN) + vec(vecs, CROSS_SHIFT))
    normed_ref[...] = normed
    flush(normed_ref)
    rows, width = values.shape
    queries[...] = low(dot(normed, query[...]))
    flush(queries)
    captions = pairs.shape[0]
    slots = rows // captions
    quads = width // QUAD
    for c in range(captions):
        here = slice(c * slots, (c + 1) * slots)
        for j in range(quads):
            cols = slice(j * QUAD, (j + 1) * QUAD)
            k, v = pairs[c, :, cols], pairs[c, :, width + j * QUAD : width + (j + 1) * QUAD]
            scores = dot_nt(k, stacked(queries[here, cols])) * SCALE
            top = jnp.max(scores, 0, keepdims=True)
            raised = jnp.exp(scores - top)
            part[here, cols] = low(unstacked(dot_tn(low(raised), v)))
            row = c * quads + j
            stats[row : row + 1, :] = top
            stats[STATS + row : STATS + row + 1, :] = jnp.sum(raised, 0, keepdims=True)


STATS = 16


def feed_second_kernel(place, first, own, other, own_stats, other_stats, vecs, out, feed, middle, mixed, factor, normed, slope, active, part):
    rows, width = first.shape
    quads = width // QUAD
    top, top_other = own_stats[:STATS], other_stats[:STATS]
    best = jnp.maximum(top, top_other)
    own_weight, other_weight = jnp.exp(top - best), jnp.exp(top_other - best)
    inverse = 1.0 / (own_stats[STATS:] * own_weight + other_stats[STATS:] * other_weight)
    own_factor, other_factor = own_weight * inverse, other_weight * inverse
    factor[...] = own_factor
    flush(factor)
    columns = jnp.concatenate([own_factor, other_factor, jnp.zeros((PAIR - 2 * STATS, QUAD), F32)], 0).T
    slots = QUAD // 4
    head = heads_of((slots, QUAD))
    for c in range(rows // slots):
        here = slice(c * slots, (c + 1) * slots)
        for j in range(quads):
            cols = slice(j * QUAD, (j + 1) * QUAD)

            def spread(column):
                out = columns[:slots, column : column + 1]
                for h in range(1, 4):
                    out = jnp.where(head == h, columns[h * slots : (h + 1) * slots, column : column + 1], out)
                return out

            row = c * quads + j
            mixed[here, cols] = low(spread(row) * own[here, cols].astype(F32) + spread(STATS + row) * other[here, cols].astype(F32))
    flush(mixed)
    values = first[...] + dot(mixed[...], out[...])
    middle[...] = values
    flush(middle)
    part[...] = feed_part(values, 1, place[0], vecs, feed, normed, slope, active)


def feed_back(grad, vecs, feed, slope, bias_grad, down_bias_grad, slope_ref, part):
    width = grad.shape[1]
    grad_low = low(grad)
    down_bias_grad[...] = jnp.sum(grad, 0, keepdims=True)
    total = jnp.zeros(grad.shape, F32)
    for i in range(FOLDS):
        here = slice(i * width, (i + 1) * width)
        down = feed[:, (FOLDS + i) * width : (FOLDS + i + 1) * width]
        grad_raised = low(dot_nt(grad_low, down) * slope[:, here].astype(F32))
        slope_ref[:, here] = grad_raised
        bias_grad[i : i + 1, :] = jnp.sum(grad_raised.astype(F32), 0, keepdims=True)
        total += dot_nt(grad_raised, feed[:, here])
    part[...] = low(total)


def feed_back_last_kernel(place, cot, vecs, feed, slope, bias_grad, down_bias_grad, grad_raised, part):
    feed_back(cot[...].astype(F32), vecs, feed, slope, bias_grad, down_bias_grad, grad_raised, part)


def cross_back_kernel(place, cot, own, other, middle, vecs, out, queries, pairs, stats, factor, mixed, grad_ref, low_ref, vec_grad, query_part, grad_pairs, grad_mixed):
    rows, width = middle.shape
    inner = own[...].astype(F32) + other[...].astype(F32)
    step, gain_grad, shift_grad = norm_back(middle[...], vec(vecs, LAYER_VECS + FEED_GAIN), inner)
    vec_grad[0:1, :] = gain_grad
    vec_grad[1:2, :] = shift_grad
    grad = step + cot[...].astype(F32)
    grad_ref[...] = grad
    low_ref[...] = low(grad)
    grad_mixed[...] = low(dot_nt(low(grad), out[...]))
    captions = pairs.shape[0]
    slots = rows // captions
    quads = width // QUAD
    for c in range(captions):
        here = slice(c * slots, (c + 1) * slots)
        for j in range(quads):
            cols = slice(j * QUAD, (j + 1) * QUAD)
            later = slice(width + j * QUAD, width + (j + 1) * QUAD)
            row = slice(c * quads + j, c * quads + j + 1)
            k, v = pairs[c, :, cols], pairs[c, :, later]
            q = stacked(queries[here, cols])
            grad_block = grad_mixed[here, cols]
            grads = stacked(grad_block)
            delta = row_sums(stacked(grad_block.astype(F32) * mixed[here, cols].astype(F32)))
            chances = jnp.exp(dot_nt(k, q) * SCALE - stats[row, :]) * factor[row, :]
            slope = low(chances * (dot_nt(v, grads) - delta))
            query_part[here, cols] = low(unstacked(dot_tn(slope, k)) * SCALE)
            grad_pairs[c, :, cols] = low(dot(slope, q) * SCALE)
            grad_pairs[c, :, later] = low(dot(low(chances), grads))


def self_back(grad, section, lengths, weights, projected, low_ref, grad_projected, grad_mixed):
    half = grad_mixed.shape[1]
    low_ref[...] = low(grad)
    flush(low_ref)
    grad_mixed[...] = low(dot_nt(low(grad), heads_rows(weights, section)))
    captions = lengths.shape[0]
    slots = grad.shape[0] // captions
    for c in range(captions):
        keep = keep_mask_turned(lengths[c], slots)
        here = slice(c * slots, (c + 1) * slots)
        for j in range(half // PAIR):
            cols = [slice(i * half + j * PAIR, i * half + (j + 1) * PAIR) for i in range(3)]
            q, k, v = (projected[here, cols[i]] for i in range(3))
            q = stacked(q)
            chances = self_chances_turned(q, k, keep)
            grads = stacked(grad_mixed[here, cols[0]])
            grad_chances = dot_nt(v, grads)
            slope = low(chances * (grad_chances - jnp.sum(grad_chances * chances, 0, keepdims=True)))
            grad_projected[here, cols[0]] = low(unstacked(dot_tn(slope, k)) * SCALE)
            grad_projected[here, cols[1]] = low(dot(slope, q) * SCALE)
            grad_projected[here, cols[2]] = low(dot(low(chances), grads))
    width = grad.shape[1]
    return dot_nt(grad_projected[...], weights[:, width : width + 3 * half])


def self_back_second_kernel(place, lengths, grad_middle, own, other, first, vecs, query, weights, projected, grad_ref, low_ref, grad_queries, grad_projected, part, vec_grad, grad_mixed):
    total = low(own[...].astype(F32) + other[...].astype(F32))
    grad_queries[...] = total
    inner = dot_nt(total, query[...])
    step, gain_grad, shift_grad = norm_back(first[...], vec(vecs, CROSS_GAIN), inner)
    vec_grad[0:1, :] = gain_grad
    vec_grad[1:2, :] = shift_grad
    grad = step + grad_middle[...]
    grad_ref[...] = grad
    part[...] = low(self_back(grad, place[0], lengths, weights, projected, low_ref, grad_projected, grad_mixed))


def feed_back_first_kernel(place, grad_first, own, other, hidden, vecs, feed, slope, grad_ref, low_ref, vec_grad, bias_grad, down_bias_grad, grad_raised, part):
    inner = own[...].astype(F32) + other[...].astype(F32)
    step, gain_grad, shift_grad = norm_back(hidden[...].astype(F32), vec(vecs, LAYER_VECS + SELF_GAIN), inner)
    vec_grad[0:1, :] = gain_grad
    vec_grad[1:2, :] = shift_grad
    low_ref[...] = low(step + grad_first[...])
    grad = low_ref[...].astype(F32)
    grad_ref[...] = grad
    feed_back(grad, vecs, feed, slope, bias_grad, down_bias_grad, grad_raised, part)


def self_back_first_kernel(place, lengths, grad_hidden, own, other, middle, text, vecs, weights, projected, grad_ref, low_ref, grad_projected, part, vec_grad, grad_mixed):
    inner = own[...].astype(F32) + other[...].astype(F32)
    step, gain_grad, shift_grad = norm_back(middle[...], vec(vecs, FEED_GAIN), inner)
    vec_grad[0:1, :] = gain_grad
    vec_grad[1:2, :] = shift_grad
    grad = step + grad_hidden[...]
    grad_ref[...] = grad
    total = self_back(grad, place[0], lengths, weights, projected, low_ref, grad_projected, grad_mixed)
    part[...] = low(total)
    unit, _ = norm_unit(text[...].astype(F32))
    vec_grad[2:3, :] = jnp.sum(total * unit, 0, keepdims=True)
    vec_grad[3:4, :] = jnp.sum(total, 0, keepdims=True)


def text_grad_kernel(place, grad_middle, own, other, text, vecs, out):
    inner = own[...].astype(F32) + other[...].astype(F32)
    step, _, _ = norm_back(text[...].astype(F32), vec(vecs, SELF_GAIN), inner)
    total = step + grad_middle[...]
    half = out.shape[1]
    out[...] = jnp.where(place[0] == 0, total[:, :half], total[:, half:])


BLOCK = 384


def weight_grads(pieces, refs, put):
    offset = 0
    rows = min(refs[left].shape[1] for left, _ in pieces)
    for left, right in pieces:
        for i in range(refs[left].shape[1] // rows):
            for j in range(refs[right].shape[1] // BLOCK):
                put(offset, dot_tn(refs[left][:, i * rows : (i + 1) * rows], refs[right][:, j * BLOCK : (j + 1) * BLOCK]))
                offset += BLOCK
    return offset


def put_in_order(order, out, cols, value):
    rows = value.shape[0] // len(order)
    for i, device in enumerate(order):
        out[i * rows : (i + 1) * rows, cols] = low(value[device * rows : (device + 1) * rows])
    flush(out, cols)


def products_kernel(order, pieces, place, *refs):
    weight_grads(pieces, refs, lambda offset, value: put_in_order(order, refs[-1], slice(offset, offset + value.shape[1]), value))


def put_by_core(core, mine, sent):
    chips, rows, _ = mine.shape

    def put(offset, value):
        cols = slice(offset, offset + value.shape[1])
        for chip in range(chips):
            first = value[2 * chip * rows : (2 * chip + 1) * rows]
            later = value[(2 * chip + 1) * rows : (2 * chip + 2) * rows]
            mine[chip, :, cols] = low(jnp.where(core == 0, first, later))
            sent[chip, :, cols] = low(jnp.where(core == 0, later, first))
        flush(mine, cols)
        flush(sent, cols)

    return put


def ring_products_kernel(pieces, place, *refs):
    weight_grads(pieces, refs, put_by_core(place[1], *refs[-2:]))


def last_products_kernel(
    blocks, place, normed, grad_projected, mixed_0, mixed_1, low_0, low_1, vecs_0, self_vecs_1, feed_vecs_1, cross_vecs, down_0, down_1, bias_0, bias_1, mine, sent
):
    section = place[0]
    put = put_by_core(place[1], mine, sent)
    width = normed.shape[1]
    offset = weight_grads(((0, 1),), (normed, grad_projected), put)
    mixed = jnp.where(section == 0, mixed_0[...], mixed_1[...])
    head_low = jnp.where(section == 0, low_0[...], low_1[...])
    for j in range(width // BLOCK):
        put(offset, dot_tn(mixed, head_low[:, j * BLOCK : (j + 1) * BLOCK]))
        offset += BLOCK
    rows = [
        vecs_0[2:4, :],
        jnp.where(section == 0, 0.0, self_vecs_1[0:2, :]),
        jnp.where(section == 0, vecs_0[0:2, :], feed_vecs_1[0:2, :]),
        jnp.where(section == 0, down_0[...], down_1[...]),
        bias_0[...],
        bias_1[...],
        cross_vecs[0:2, :],
    ]
    used = 7 + 2 * FOLDS
    columns = jnp.concatenate(rows + [jnp.zeros((128 - used - 2, width), F32)], 0).T
    if blocks:
        lane = lax.broadcasted_iota(jnp.int32, columns.shape, 1)
        columns = jnp.where(lane < used, columns, woven(columns[: width // 2], columns[width // 2 :], blocks))
    put(offset, columns)


def keys_products_kernel(blocks, offset, place, image, grad_pairs, mine, sent):
    put = put_by_core(place[1], mine, sent)
    half = image.shape[2] // 2
    for j in range(grad_pairs.shape[2] // BLOCK):
        value = sum(dot_tn(image[c], grad_pairs[c, :, j * BLOCK : (j + 1) * BLOCK]) for c in range(image.shape[0]))
        put(offset + j * BLOCK, woven(value[:half], value[half:], blocks))


def second_products_kernel(blocks, place, normed, grad_queries, mixed, grad_low, self_normed, grad_projected, mine, sent):
    put = put_by_core(place[1], mine, sent)
    offset = weight_grads(((0, 1),), (self_normed, grad_projected), put)
    own_normed, own_mixed = half_in(place[0], normed[...]), half_in(place[0], mixed[...])
    for j in range(grad_queries.shape[1] // BLOCK):
        cols = slice(j * BLOCK, (j + 1) * BLOCK)
        put(offset, woven(dot_tn(own_normed, grad_queries[:, cols]), dot_tn(own_mixed, grad_low[:, cols]), blocks))
        offset += BLOCK


def in_order(section, own, other):
    own, other = own.astype(F32), other.astype(F32)
    return jnp.where(section == 0, own, other), jnp.where(section == 0, other, own)


def finish_feed_kernel(count, place, own, other, up, down):
    rows, width = own.shape[0], down.shape[1]
    halves = in_order(place[0], own[...], other[...])
    parts = []
    for device in range(count):
        for half in halves:
            for fold in range(FOLDS):
                begin = fold * width + device * rows
                parts.append(half[:, begin : begin + rows])
    up[...] = jnp.concatenate(parts, 1)
    for i, half in enumerate(halves):
        for fold in range(FOLDS):
            begin = (i * FOLDS + fold) * rows
            down[begin : begin + rows, :] = half[:, (FOLDS + fold) * width : (FOLDS + fold + 1) * width]


def finish_cross_kernel(place, heads, keys, keys_other, query_grad, keys_grad, out_grad):
    rows = query_grad.shape[0]
    heads32, keys32 = heads[...].astype(F32), keys[...].astype(F32)
    query_grad[...] = heads32[:rows]
    out_grad[...] = heads32[rows:]
    keys_grad[...] = jnp.where(place[0] == 0, keys32[:rows], keys32[rows:]) + keys_other[...].astype(F32)


def finish_heads_kernel(cross_rows, place, sums, own, other, into, out, gain, shift, feed_gain, feed_shift, down_bias, cross_gain, cross_shift, up_bias):
    rows, width = out.shape
    half = width // 2
    section = place[0]
    halves = in_order(section, own[...], other[:, : 3 * half])
    for i in range(3):
        for j, part in enumerate(halves):
            into[:, (2 * i + j) * half : (2 * i + j + 1) * half] = part[:, i * half : (i + 1) * half]
    out[...] = sums[:, 3 * half : 3 * half + width]
    flipped = lambda v: jnp.concatenate([v.astype(F32), jnp.zeros((128 - rows, 128), F32)], 0).T[:, :rows]
    own_vec, other_vec = flipped(sums[:, 3 * half + width :]), flipped(other[:, 3 * half :])
    mine = lambda v, first, later: jnp.where(section == 0, v[first : first + 1], v[later : later + 1])
    gain[...] = mine(own_vec, 0, 2) + mine(other_vec, 0, 2)
    shift[...] = mine(own_vec, 1, 3) + mine(other_vec, 1, 3)
    feed_gain[...] = own_vec[4:5]
    feed_shift[...] = own_vec[5:6]
    down_bias[...] = own_vec[6:7]
    bias = [[mine(v, 7 + i, 7 + FOLDS + i) for i in range(FOLDS)] for v in (own_vec, other_vec)]
    ordered = [jnp.where(section == 0, a, b) for a, b in zip(*bias)] + [jnp.where(section == 0, b, a) for a, b in zip(*bias)]
    up_bias[...] = jnp.concatenate(ordered, 1)
    for i, ref in enumerate((cross_gain, cross_shift)):
        row = own_vec[7 + 2 * FOLDS + i : 8 + 2 * FOLDS + i]
        ref[...] = jnp.where(section == 0, row[:, :cross_rows], row[:, cross_rows:])


def body(
    text,
    image,
    lengths,
    self_gain,
    self_shift,
    heads_in,
    heads_out,
    feed_gain,
    feed_shift,
    up_weight,
    up_bias,
    down_weight,
    down_bias,
    cross_gain,
    cross_shift,
    cross_query,
    cross_keys,
    cross_out,
    cotangent,
):
    section = lax.axis_index("section")
    count = lax.axis_size("dp")
    core = lax.axis_index("dp") % 2
    place = jnp.stack([section, core]).astype(jnp.int32)
    captions, half_image, width = image.shape
    rows = text.shape[0]
    piece = heads_in.shape[1]
    cross_piece = cross_query.shape[0]
    half = width // 2
    half_ff = FOLDS * width
    aligned = piece % 16 == 0
    order = [2 * chip + i for chip in ring_order() for i in range(2)] if aligned else list(range(count))
    groups = [order]

    def both_layers(first, later):
        own, got = pick(section, first, later), swap(pick(section, later, first))
        return pick(section, own, got), pick(section, got, own)

    core_cols = width + 3 * half
    cross_own = jnp.concatenate([cross_keys, cross_query, cross_out], 1)
    if aligned:
        vectors = jnp.concatenate([self_gain, self_shift, feed_gain, feed_shift, down_bias], 0)
        sent, own_attn, own_feed, own_vecs = call(
            functools.partial(prepare_kernel, count),
            place,
            [late(v) for v in (heads_in[0], heads_out[0], up_weight[0], down_weight[0], vectors, up_bias, cross_gain[None], cross_shift[None])],
            [((piece, cols), BF16) for cols in (core_cols + 128 + 2 * half_ff, core_cols, 2 * half_ff, 128)],
            name="prepare",
        )
        attn_rows_0, attn_1, feed_0, feed_1 = call(
            merge_kernel, place, [swap(sent), own_attn, own_feed, own_vecs], [((piece, cols), BF16) for cols in (core_cols + 128, core_cols, 2 * half_ff, 2 * half_ff)], name="merge"
        )
    else:
        up = up_weight[0].reshape(piece, count, 2, FOLDS, piece).transpose(2, 0, 3, 1, 4).reshape(2, piece, half_ff)
        down = down_weight[0].reshape(2, FOLDS, piece, width)
        feed_own = [jnp.concatenate([up[i]] + [down[i, j] for j in range(FOLDS)], 1) for i in range(2)]
        into = heads_in[0].reshape(piece, 3, 2, half)
        attn_own = [jnp.concatenate([heads_out[0], into[:, :, i].reshape(piece, 3 * half)], 1) for i in range(2)]
        own_vecs = jnp.concatenate([self_gain, self_shift, feed_gain, feed_shift, down_bias, up_bias.reshape(2 * FOLDS, piece)], 0)
        own_cross_vecs = jnp.concatenate([cross_gain[None], cross_shift[None]], 0)
        sent_vecs = jnp.concatenate([own_vecs, jnp.pad(own_cross_vecs, ((0, 0), (0, piece - cross_piece)))], 0)
        feed_0, feed_1 = both_layers(*feed_own)
        feed_0, feed_1, sent_vecs, *attn_own = together(feed_0, feed_1, sent_vecs, *attn_own)
        attn_0, attn_1 = both_layers(*attn_own)
        got_vecs = swap(sent_vecs)
        cross_vec_rows = side(own_cross_vecs, got_vecs[LAYER_VECS:, :cross_piece], section, 1)
        vec_cols = jnp.concatenate([pick(section, own_vecs, got_vecs[:LAYER_VECS]), pick(section, got_vecs[:LAYER_VECS], own_vecs), cross_vec_rows], 0)
        vec_cols = jnp.pad(vec_cols, ((0, 128 - vec_cols.shape[0]), (0, 0))).T
        attn_rows_0 = jnp.concatenate([attn_0, vec_cols], 1)
    ring_f = Gather(feed_0)
    ring_f.move()

    def gather(value):
        return lax.all_gather(value, "dp", axis=0, tiled=True, axis_index_groups=groups)

    def reordered(value, blocks, parts, widths):
        rows_out = value.shape[0] * parts
        if aligned:
            return call(functools.partial(reorder_kernel, blocks, parts), place, [value], [((rows_out, w), BF16) for w in widths], name="reorder")
        whole = value.reshape(value.shape[0], parts, sum(widths)).transpose(1, 0, 2).reshape(rows_out, sum(widths))
        ends = [sum(widths[: i + 1]) for i in range(len(widths))]
        return [whole[:, end - w : end] for end, w in zip(ends, widths)]

    attn_first = gather(attn_rows_0)
    attn_1, feed_1, cross_own, text_own, cot_own = meet([ring_f], attn_1, feed_1, cross_own, text, cotangent)
    cross_all = gather(side(cross_own, swap(cross_own), section, 1))
    text_all = side(text, swap(text_own), section, 1)
    feed_last = gather(feed_1)
    cot_all = side(cotangent, swap(cot_own), section, 1)
    ring_d = Gather(attn_1)
    for i in range(ring_f.steps - 2):
        ring_f.move()
        ring_d.move()
        if i < ring_f.steps - 3:
            meet([ring_f, ring_d])
    (attn_first,) = meet([ring_f, ring_d], attn_first)
    ring_f.move()
    ring_d.move()
    (weights_0,) = reordered(attn_first, order, 1, [core_cols + 128])

    shape_f = ((rows, width), F32)
    shape_b = ((rows, width), BF16)
    shape_half = ((rows, half), BF16)
    shape_qkv = ((rows, 3 * half), BF16)
    shape_active = ((rows, half_ff), BF16)
    shape_stats = ((2 * STATS, QUAD), F32)
    shape_factor = ((STATS, QUAD), F32)
    shape_pairs = ((captions, half_image, 2 * width), BF16)
    shape_vec = ((8, width), F32)
    shape_bias = ((FOLDS, width), F32)
    shape_one = ((1, width), F32)
    half_scratch = [pltpu.VMEM((rows, half), BF16)]
    self_flops, feed_flops, pair_flops = 6 * rows * width * half, 4 * rows * width * half_ff, 4 * captions * half_image * width * width
    feed_blocks = [(i * width, (i + 1) * width) for i in (2, 0, 3, 1)]
    attn_blocks = [(0, width), (width, core_cols)]

    vecs, vecs_far, normed_a0, qkv_0, mixed_0, weights_0_far = call(
        functools.partial(self_first_kernel, aligned),
        place,
        [lengths, text_all, weights_0],
        [both((VECS, width), F32), save(*shape_b), save(*shape_qkv), shape_half],
        name="self_0",
        flops=self_flops,
        keep=(2,),
    )
    if not aligned:
        straight = lambda v: jnp.concatenate([v[:CROSS_GAIN], v[CROSS_GAIN : CROSS_GAIN + 2].reshape(2, count, 2, cross_piece).transpose(0, 2, 1, 3).reshape(2, width), v[CROSS_GAIN + 2 :]], 0)
        vecs, vecs_far = straight(vecs), straight(vecs_far)
    other_0 = swap(mixed_0)
    (mixed_0,) = meet([ring_f, ring_d], mixed_0)
    ring_f.pack()
    while ring_d.step < ring_d.steps:
        ring_d.move()
    other_0, ring_f.other = together(other_0, ring_f.other)
    feed_w0 = ring_f.result(place)
    keys, query, cross_out_w = reordered(cross_all, ring_order() if aligned else [0], 2, [2 * width, width, width])
    mixed_all_0, middle_0, normed_f0, slope_f0, active_0, part_0, feed_w0_far = call(
        feed_first_kernel,
        place,
        [text_all, mixed_0, other_0, vecs, weights_0, feed_w0],
        [save(*shape_b), save(*shape_f), save(*shape_b), save(*shape_active), save(*shape_active), shape_b],
        name="feed_0",
        flops=feed_flops,
        keep=(5,),
    )
    part_0_other = swap(part_0)
    (part_0,) = meet([ring_d], part_0)
    ring_d.pack()
    weights_1 = ring_d.result(place)
    hidden, hidden_far, normed_a1, qkv_1, mixed_1 = call(
        self_second_kernel,
        place,
        [lengths, late(middle_0), part_0, part_0_other, vecs, weights_1],
        [both(*shape_b), save(*shape_b), save(*shape_qkv), shape_half],
        name="self_1",
        flops=self_flops,
    )
    other_1 = swap(mixed_1)
    pairs, keys_far = call(pairs_kernel, place, [late(image), keys], [shape_pairs], name="pairs", flops=pair_flops, keep=(1,))
    other_1, pairs = together(other_1, pairs)
    mixed_all_1, first_1, normed_c, queries, cross_part, stats, stats_far, query_far, weights_1_far = call(
        cross_kernel,
        place,
        [hidden, mixed_1, other_1, vecs, weights_1, query, pairs],
        [save(*shape_b), save(*shape_f), save(*shape_b), save(*shape_b), shape_b, both(*shape_stats)],
        name="cross_1",
        flops=4 * rows * width * width,
        keep=(4, 5),
    )
    cross_part_other, stats_other = swap(cross_part), swap(stats)
    (feed_w1,) = reordered(feed_last, order, 1, [2 * half_ff])
    middle_1_far, cross_mixed_far, factor, normed_f1, slope_f1, active_1, part_1, cross_out_far = call(
        feed_second_kernel,
        place,
        [late(first_1), cross_part, cross_part_other, stats, stats_other, vecs, cross_out_w, feed_w1],
        [save(*shape_f), save(*shape_b), save(*shape_factor), shape_b, shape_active, shape_active, shape_b],
        name="feed_1",
        flops=feed_flops,
        keep=(6,),
    )
    own_cols = lambda v: pick(section, v[..., :half], v[..., half:])

    def meet_sums(rings, *values):
        flat = together(*[v for ring in rings for v in ring.front()], *values)
        for i, ring in enumerate(rings):
            ring.put_front(flat[2 * i : 2 * i + 2])
        return flat[2 * len(rings) :]

    def scatter(value):
        return lax.psum_scatter(value, "dp", scatter_dimension=0, tiled=True, axis_index_groups=groups)

    bias_grad_1, down_bias_grad_1, slope_1, back_1 = call(
        feed_back_last_kernel, place, [cot_all, vecs, feed_w1, slope_f1], [save(*shape_bias), save(*shape_one), shape_active, shape_b], name="feed_back_1", flops=feed_flops
    )
    back_1_other = swap(back_1)
    (feed_grad_1,) = call(
        functools.partial(products_kernel, order, ((0, 1), (2, 3))),
        place,
        [normed_f1, slope_1, active_1, cot_all],
        [save((width, 2 * half_ff), BF16)],
        name="feed_grads_1",
        flops=feed_flops,
    )
    back_1_other, feed_grad_1 = together(back_1_other, feed_grad_1)
    feed_got_1 = scatter(feed_grad_1)
    grad_middle_1, grad_low_1, feed_vec_1, query_part, grad_pairs = call(
        cross_back_kernel,
        place,
        [late(cot_all), back_1, back_1_other, late(middle_1_far), late(vecs_far), late(cross_out_far), late(queries), pairs, late(stats_far), late(factor), late(cross_mixed_far)],
        [shape_f, shape_b, save(*shape_vec), shape_b, shape_pairs],
        scratch=[pltpu.VMEM((rows, width), BF16)],
        name="cross_back",
        flops=4 * rows * width * width,
    )
    query_part_other = swap(query_part)
    ring_shape = lambda cols: ((count // 2, piece, cols), BF16)
    second_cols = 3 * half + 3 * width
    if aligned:
        *keys_grads, first_now, query_now, weights_now, qkv_now = call(
            functools.partial(keys_products_kernel, count, 3 * half + width),
            place,
            [late(image), grad_pairs],
            [save(*ring_shape(second_cols)), save(*ring_shape(second_cols))],
            vmem=20,
            name="keys_grads",
            flops=pair_flops,
            fetch=(first_1, query_far, weights_1_far, qkv_1),
        )
        query_part_other, *keys_grads = together(query_part_other, *keys_grads)
    else:
        first_now, query_now, weights_now, qkv_now = first_1, query_far, weights_1_far, qkv_1
    grad_first_1, head_low_1, grad_queries, grad_qkv_1, self_back_1, cross_vec_1 = call(
        self_back_second_kernel,
        place,
        [lengths, grad_middle_1, query_part, query_part_other, first_now, late(vecs_far), query_now, weights_now, qkv_now],
        [shape_f, save(*shape_b), shape_b, shape_qkv, shape_b, save(*shape_vec)],
        scratch=half_scratch,
        name="self_back_1",
        flops=2 * self_flops,
    )
    self_back_1_other = swap(self_back_1)
    if aligned:
        second_grads = call(
            functools.partial(second_products_kernel, count),
            place,
            [late(normed_c), grad_queries, late(cross_mixed_far), grad_low_1, late(normed_a1), grad_qkv_1],
            [save(*ring_shape(second_cols)), save(*ring_shape(second_cols))],
            vmem=20,
            name="second_grads",
            flops=2 * rows * width * (width + 3 * half),
            over=keys_grads,
        )
    else:
        pair_rows = lambda v: v.reshape(2, count, cross_piece, v.shape[1]).transpose(1, 0, 2, 3).reshape(width, v.shape[1])
        flat = lambda v: v.reshape(captions * half_image, v.shape[2])
        heads = pair_rows(jnp.concatenate([dot_tn(own_cols(normed_c), grad_queries), dot_tn(own_cols(cross_mixed_far), grad_low_1)], 0))
        second_grad = low(jnp.concatenate([dot_tn(normed_a1, grad_qkv_1), heads, pair_rows(dot_tn(flat(image), flat(grad_pairs)))], 1))
        parts = second_grad.reshape(count // 2, 2, piece, second_cols)
        second_grads = pick(core, parts[:, 0], parts[:, 1]), pick(core, parts[:, 1], parts[:, 0])
    self_back_1_other, *second_grads = together(self_back_1_other, *second_grads)
    ring_second = Scatter(*second_grads)
    ring_second.begin()
    (self_back_1_other,) = ring_second.step(self_back_1_other)
    grad_hidden, grad_hidden_low, self_vec_1, bias_grad_0, down_bias_grad_0, slope_0, back_0 = call(
        feed_back_first_kernel,
        place,
        [grad_first_1, self_back_1, self_back_1_other, late(hidden_far), late(vecs_far), late(feed_w0_far, *feed_blocks), late(slope_f0)],
        [shape_f, shape_b, save(*shape_vec), save(*shape_bias), save(*shape_one), shape_active, shape_b],
        name="feed_back_0",
        flops=feed_flops,
    )
    back_0_other = swap(back_0)
    (back_0,) = meet_sums([ring_second], back_0)
    (slope_0,) = ring_second.step(slope_0)
    (feed_grad_0,) = call(
        functools.partial(products_kernel, order, ((0, 1), (2, 3))),
        place,
        [late(normed_f0), slope_0, late(active_0), grad_hidden_low],
        [save((width, 2 * half_ff), BF16)],
        name="feed_grads_0",
        flops=feed_flops,
    )
    back_0_other, feed_grad_0, up, down = together(back_0_other, feed_grad_0, *ring_second.front())
    ring_second.put_front((up, down))
    feed_got_0 = scatter(feed_grad_0)
    (back_0_other,) = ring_second.step(back_0_other)
    grad_middle_0, head_low_0, grad_qkv_0, self_back_0, vecs_grad_0 = call(
        self_back_first_kernel,
        place,
        [lengths, grad_hidden, back_0, back_0_other, late(middle_0), text_all, late(vecs_far), late(weights_0_far, *attn_blocks), late(qkv_0)],
        [shape_f, shape_b, shape_qkv, shape_b, shape_vec],
        scratch=half_scratch,
        name="self_back_0",
        flops=2 * self_flops,
    )
    self_back_0_other = swap(self_back_0)
    (grad_qkv_0,) = meet_sums([ring_second], grad_qkv_0)
    (grad_qkv_0,) = ring_second.step(grad_qkv_0)
    cross_vec_woven = cross_vec_1
    if not aligned:
        cross_vec_woven = cross_vec_1.reshape(8, 2, count, cross_piece).transpose(0, 2, 1, 3).reshape(8, width)
    last_grads = call(
        functools.partial(last_products_kernel, count if aligned else 0),
        place,
        [late(normed_a0), grad_qkv_0, late(mixed_all_0), late(mixed_all_1), head_low_0, late(head_low_1), vecs_grad_0]
        + [late(v) for v in (self_vec_1, feed_vec_1, cross_vec_woven, down_bias_grad_0, down_bias_grad_1, bias_grad_0, bias_grad_1)],
        [save(*ring_shape(core_cols + 128)), ring_shape(core_cols + 128)],
        name="last_grads",
        flops=2 * rows * width * core_cols,
    )
    *last_grads, feed_got_1, self_back_0_other = meet_sums([ring_second], *last_grads, feed_got_1, self_back_0_other)
    ring_last = Scatter(*last_grads)
    ring_last.begin()
    (grad_middle_0,) = ring_last.step(grad_middle_0)
    second_got = low(ring_second.result())
    (text_grad,) = call(text_grad_kernel, place, [grad_middle_0, self_back_0, self_back_0_other, text_all, late(vecs_far)], [((rows, half), F32)], name="text_grad")
    text_grad, second_got = meet_sums([ring_last], text_grad, second_got)
    (grad_pairs,) = ring_last.step(grad_pairs)
    image_grad = by_caption(image_grad_kernel, grad_pairs, keys_far, jax.ShapeDtypeStruct((captions, half_image, width), F32), "image_grad", pair_flops)
    (image_grad,) = meet_sums([ring_last], image_grad)
    ring_last.step()

    def other_half(first, later):
        return swap(pick(section, low(later), low(first)))

    (feed_got_0,) = meet_sums([ring_last], feed_got_0)
    feed_other = other_half(feed_got_0, feed_got_1)
    ring_last.step()
    got_part = swap(pick(section, part_1[:, half:], part_1[:, :half]))
    layer_out = own_cols(middle_1_far) + (own_cols(part_1).astype(F32) + got_part.astype(F32)) + own_cols(vecs_far[LAYER_VECS + DOWN_BIAS])
    cross_got = second_got[:, 3 * half : 3 * half + width]
    keys_got = second_got[:, 3 * half + width :]
    keys_other = swap(pick(section, keys_got[cross_piece:], keys_got[:cross_piece]))
    feed_own = pick(section, feed_got_0, feed_got_1)
    into_got_1 = second_got[:, : 3 * half]
    if aligned:
        up_grad, down_grad = call(
            functools.partial(finish_feed_kernel, count),
            place,
            [feed_own, feed_other],
            [((piece, 2 * half_ff), F32), ((2 * FOLDS * piece, width), F32)],
            name="finish_feed",
        )
        cross_query_grad, cross_keys_grad, cross_out_grad = call(
            finish_cross_kernel,
            place,
            [cross_got, keys_got, keys_other],
            [((cross_piece, width), F32), ((cross_piece, 2 * width), F32), ((cross_piece, width), F32)],
            name="finish_cross",
        )
        keys_other, cross_query_grad = together(keys_other, cross_query_grad)
    else:
        feed_parts = [v.astype(F32) for v in (pick(section, feed_own, feed_other), pick(section, feed_other, feed_own))]
        up_parts = [v[:, :half_ff].reshape(piece, FOLDS, count, piece).transpose(0, 2, 1, 3) for v in feed_parts]
        up_grad = jnp.stack(up_parts, 2).reshape(piece, 2 * half_ff)
        down_parts = [v[:, half_ff:].reshape(piece, FOLDS, width).transpose(1, 0, 2) for v in feed_parts]
        down_grad = jnp.stack(down_parts, 0).reshape(2 * FOLDS * piece, width)
        cross_query_grad, cross_out_grad = cross_got[:cross_piece].astype(F32), cross_got[cross_piece:].astype(F32)
        own_keys = pick(section, keys_got[:cross_piece], keys_got[cross_piece:])
        cross_keys_grad = own_keys.astype(F32) + keys_other.astype(F32)
    last_got = ring_last.result()
    vec_got = last_got[:, core_cols:]
    last_other = swap(low(jnp.concatenate([pick(section, into_got_1.astype(F32), last_got[:, : 3 * half]), vec_got], 1)))
    into_own = pick(section, last_got[:, : 3 * half], into_got_1.astype(F32))
    if aligned:
        shape_row = ((1, piece), F32)
        heads_in_grad, heads_out_grad, *rows_out, up_bias_grad = call(
            functools.partial(finish_heads_kernel, cross_piece),
            place,
            [last_got, into_own, last_other],
            [((piece, 6 * half), F32), ((piece, width), F32)] + [shape_row] * 5 + [((1, cross_piece), F32)] * 2 + [((1, 2 * FOLDS * piece), F32)],
            name="finish_heads",
        )
        cross_gain_grad, cross_shift_grad = rows_out[5][0], rows_out[6][0]
    else:
        into_other = last_other[:, : 3 * half].astype(F32)
        into_parts = pick(section, into_own, into_other), pick(section, into_other, into_own)
        heads_in_grad = jnp.stack([v.reshape(piece, 3, half) for v in into_parts], 2).reshape(piece, 6 * half)
        heads_out_grad = last_got[:, 3 * half : core_cols]
        own_vec, other_vec = vec_got.T, last_other[:, 3 * half :].astype(F32).T
        mine = lambda v, begin, size: pick(section, v[begin : begin + size], v[begin + size : begin + 2 * size])
        self_vec = mine(own_vec, 0, 2) + mine(other_vec, 0, 2)
        rows_out = [self_vec[0:1], self_vec[1:2], own_vec[4:5], own_vec[5:6], own_vec[6:7]]
        bias = mine(own_vec, 7, FOLDS), mine(other_vec, 7, FOLDS)
        up_bias_grad = jnp.concatenate([pick(section, *bias), pick(section, *bias[::-1])], 0).reshape(1, 2 * FOLDS * piece)
        cross_vec = pick(section, own_vec[7 + 2 * FOLDS : 9 + 2 * FOLDS, :cross_piece], own_vec[7 + 2 * FOLDS : 9 + 2 * FOLDS, cross_piece:])
        cross_gain_grad, cross_shift_grad = cross_vec[0], cross_vec[1]
    return (
        layer_out,
        text_grad,
        image_grad,
        rows_out[0],
        rows_out[1],
        heads_in_grad[None],
        heads_out_grad[None],
        rows_out[2],
        rows_out[3],
        up_grad[None],
        up_bias_grad,
        down_grad[None],
        rows_out[4],
        cross_gain_grad,
        cross_shift_grad,
        cross_query_grad,
        cross_keys_grad,
        cross_out_grad,
    )


def solution(mesh):
    placed = (
        P("dp", "section"),
        P("dp", "section", None),
        P("dp"),
        P("section", "dp"),
        P("section", "dp"),
        P("section", "dp", None),
        P("section", "dp", None),
        P("section", "dp"),
        P("section", "dp"),
        P("section", "dp", None),
        P("section", "dp"),
        P("section", "dp", None),
        P("section", "dp"),
        P(("section", "dp")),
        P(("section", "dp")),
        P(("section", "dp"), None),
        P(("section", "dp"), None),
        P(("section", "dp"), None),
        P("dp", "section"),
    )
    return jax.shard_map(
        body,
        mesh=mesh,
        in_specs=placed,
        out_specs=(P("dp", "section"), P("dp", "section"), P("dp", "section", None)) + placed[3:18],
        check_vma=False,
    )
```

```python
import functools

import jax
import jax.numpy as jnp
from jax import lax
from jax.experimental import pallas as pl
from jax.experimental.pallas import tpu as pltpu
from jax.sharding import PartitionSpec as P

HEAD_DIM = 64
PAIR = 2 * HEAD_DIM
QUAD = 4 * HEAD_DIM
EPS = 1e-05
MASKED = -1000000000.0
SCALE = HEAD_DIM**-0.5
F32 = jnp.float32
BF16 = jnp.bfloat16
MIB = 1 << 20


def swap(value):
    return lax.ppermute(value, "section", [(0, 1), (1, 0)])


def pick(section, first, later):
    return jnp.where(section == 0, first, later)


def side(own, other, section, axis):
    return jnp.concatenate([pick(section, own, other), pick(section, other, own)], axis)


def low(values):
    return values.astype(BF16)


def ring_chip(place, chips):
    return jnp.where(place < chips // 2, 2 * place, 2 * (chips - 1 - place) + 1)


def ring_order():
    chips = lax.axis_size("dp") // 2
    return list(range(0, chips, 2)) + list(range(chips - 1, 0, -2))


def ring_steps(shift):
    order = ring_order()
    chips = len(order)
    return [(2 * order[i] + core, 2 * order[(i + shift) % chips] + core) for i in range(chips) for core in range(2)]


def ring_move(value, shift):
    return lax.ppermute(value, "dp", ring_steps(shift))


def core_swap(value):
    return lax.ppermute(value, "dp", [(i, i ^ 1) for i in range(lax.axis_size("dp"))])


def my_place():
    chips = lax.axis_size("dp") // 2
    me = lax.axis_index("dp")
    chip, core = me // 2, me % 2
    return jnp.where(chip % 2 == 0, chip // 2, chips - 1 - chip // 2), core


def pack_kernel(cut, spots, *refs):
    *sources, out = refs
    chips = out.shape[0]
    for i, source in enumerate(sources[: chips - 1]):
        out[spots[i]] = source[...]
    out[spots[chips - 1], :, :cut] = sources[chips - 1][...]
    out[spots[chips - 1], :, cut:] = sources[chips][...]


def join_kernel(place, mine, other, out):
    core = place[1]
    for chip in range(mine.shape[0]):
        out[2 * chip + core] = mine[chip]
        out[2 * chip + 1 - core] = other[chip]


def reorder_kernel(order, parts, place, source, *outs):
    rows = source.shape[0] // len(order)
    width = sum(out.shape[1] for out in outs)
    for part in range(parts):
        offset = part * width
        for out in outs:
            for i, spot in enumerate(order):
                begin = part * source.shape[0] + spot * rows
                out[begin : begin + rows, :] = source[i * rows : (i + 1) * rows, offset : offset + out.shape[1]]
            offset += out.shape[1]


class Gather:
    def __init__(self, shard):
        self.chips = lax.axis_size("dp") // 2
        self.steps = self.chips // 2
        self.rows, self.width = shard.shape
        self.cut = self.width // 256 * 128
        self.got = {0: shard}
        self.step = 0
        self.last = ()

    def front(self):
        return self.last or (self.got[-self.step], self.got[self.step])

    def put_front(self, values):
        if self.last:
            self.last = values
        else:
            self.got[-self.step], self.got[self.step] = values

    def move(self):
        self.step += 1
        up, down = self.got[1 - self.step], self.got[self.step - 1]
        if self.step < self.steps:
            self.got[-self.step], self.got[self.step] = ring_move(up, 1), ring_move(down, -1)
        else:
            self.last = (ring_move(up[:, : self.cut], 1), ring_move(down[:, self.cut :], -1))

    def pack(self):
        chips, half = self.chips, self.steps
        steps = list(range(1 - half, half + 1))
        place, _ = my_place()
        spots = jnp.stack([ring_chip((place + step + chips) % chips, chips) for step in steps]).astype(jnp.int32)
        (self.mine,) = call(
            functools.partial(pack_kernel, self.cut), spots, [self.got[step] for step in steps[:-1]] + list(self.last), [((chips, self.rows, self.width), BF16)], name="pack"
        )
        self.other = core_swap(self.mine)

    def result(self, place):
        rows = 2 * self.chips * self.rows
        if self.rows % 16 == 0:
            (full,) = call(join_kernel, place, [self.mine, self.other], [((2 * self.chips, self.rows, self.width), BF16)], name="join")
            return full.reshape(rows, self.width)
        first, later = pick(place[1], self.mine, self.other), pick(place[1], self.other, self.mine)
        return jnp.stack([first, later], 1).reshape(rows, self.width)


def together(*values):
    return lax.optimization_barrier(values)


def meet(rings, *values):
    fronts = [ring.front() for ring in rings]
    flat = together(*[v for front in fronts for v in front], *values)
    for i, ring in enumerate(rings):
        ring.put_front((flat[2 * i], flat[2 * i + 1]))
    return flat[2 * len(rings) :]


class Scatter:
    def __init__(self, mine, sent):
        self.mine, self.sent = mine, sent
        self.chips, self.rows, self.width = mine.shape
        self.steps = self.left = self.chips // 2
        self.cut = self.width // 256 * 128
        self.place, _ = my_place()

    def begin(self, early=None):
        self.first = None
        if early is not None:
            self.first = core_swap(lax.dynamic_index_in_dim(early, self.chip(self.steps), 0, False))
        self.got = core_swap(self.sent)

    def chip(self, step):
        return ring_chip((self.place + step + self.chips) % self.chips, self.chips)

    def own(self, step, begin=0, end=None):
        chip = self.chip(step)
        cut_out = lambda v: lax.dynamic_index_in_dim(v, chip, 0, False)[:, begin:end].astype(F32)
        if self.first is not None and abs(step) == self.steps:
            return cut_out(self.mine) + self.first[:, begin:end].astype(F32)
        return cut_out(self.mine) + cut_out(self.got)

    def front(self):
        return self.up, self.down

    def put_front(self, values):
        self.up, self.down = values

    def step(self, *pins):
        left, cut = self.left, self.cut
        if left == self.steps:
            up, down = self.own(left, 0, cut), self.own(-left, cut)
        else:
            up, down = self.added()
            up, down = self.own(left) + up, self.own(-left) + down
        up, down, *pins = together(low(up), low(down), *pins)
        self.up, self.down = ring_move(up, 1), ring_move(down, -1)
        self.left -= 1
        return pins

    def added(self):
        up, down = self.up.astype(F32), self.down.astype(F32)
        if self.left == self.steps - 1:
            up = jnp.concatenate([up, jnp.zeros((self.rows, self.width - self.cut), F32)], 1)
            down = jnp.concatenate([jnp.zeros((self.rows, self.cut), F32), down], 1)
        return up, down

    def after_here(self, *values):
        self.mine, self.got, *_ = together(self.mine, self.got, *values)

    def result(self):
        up, down = self.added()
        return self.own(0) + up + down


def norm_unit(values):
    centred = values - jnp.mean(values, -1, keepdims=True)
    scale = lax.rsqrt(jnp.mean(centred * centred, -1, keepdims=True) + EPS)
    return centred * scale, scale


def norm_back(values, gain, grad):
    unit, scale = norm_unit(values)
    wide = grad * gain
    inner = wide - jnp.mean(wide, -1, keepdims=True) - unit * jnp.mean(wide * unit, -1, keepdims=True)
    return inner * scale, jnp.sum(grad * unit, 0, keepdims=True), jnp.sum(grad, 0, keepdims=True)


def dot(left, right):
    return jnp.dot(left, right, preferred_element_type=F32)


def dot_tn(left, right):
    return lax.dot_general(left, right, (((0,), (0,)), ((), ())), preferred_element_type=F32)


def dot_nt(left, right):
    return lax.dot_general(left, right, (((1,), (1,)), ((), ())), preferred_element_type=F32)


def heads_of(shape):
    return lax.broadcasted_iota(jnp.int32, shape, 1) // HEAD_DIM


def stacked(block):
    head = heads_of(block.shape)
    zero = jnp.zeros_like(block)
    return jnp.concatenate([jnp.where(head == h, block, zero) for h in range(block.shape[1] // HEAD_DIM)], 0)


def unstacked(rows):
    heads = rows.shape[1] // HEAD_DIM
    slots = rows.shape[0] // heads
    head = heads_of((slots, rows.shape[1]))
    out = rows[:slots]
    for h in range(1, heads):
        out = jnp.where(head == h, rows[h * slots : (h + 1) * slots], out)
    return out


def row_sums(values):
    high = low(values)
    rest = low(values - high.astype(F32))
    ones = jnp.ones((8, values.shape[1]), BF16)
    return (dot_nt(ones, high) + dot_nt(ones, rest))[0:1]


def keep_mask(length, slots):
    query = lax.broadcasted_iota(jnp.int32, (2 * slots, slots), 0) % slots
    key = lax.broadcasted_iota(jnp.int32, (2 * slots, slots), 1)
    return (key <= query) & (key < length)


def self_chances(queries, keys, keep):
    scores = jnp.where(keep, dot_nt(queries, keys) * SCALE, MASKED)
    raised = jnp.exp(scores - jnp.max(scores, -1, keepdims=True))
    return raised / jnp.sum(raised, -1, keepdims=True)


def keep_mask_turned(length, slots):
    key = lax.broadcasted_iota(jnp.int32, (slots, 2 * slots), 0)
    query = lax.broadcasted_iota(jnp.int32, (slots, 2 * slots), 1) % slots
    return (key <= query) & (key < length)


def self_chances_turned(queries, keys, keep):
    scores = jnp.where(keep, dot_nt(keys, queries) * SCALE, MASKED)
    raised = jnp.exp(scores - jnp.max(scores, 0, keepdims=True))
    return raised / jnp.sum(raised, 0, keepdims=True)


class Late:
    def __init__(self, source, scratch, sems, blocks):
        self.scratch, self.shape = scratch, scratch.shape
        self.copies = {}
        for i, (begin, end) in enumerate(blocks or [(0, None)]):
            here = (slice(None), slice(begin, end)) if blocks else Ellipsis
            copy = pltpu.make_async_copy(source.at[here] if blocks else source, scratch.at[here] if blocks else scratch, sems.at[i])
            copy.start()
            self.copies[(begin, end)] = copy

    def __getitem__(self, index):
        wanted = index[-1] if isinstance(index, tuple) and len(self.shape) == 2 else slice(None)
        low_end, high_end = wanted.start or 0, wanted.stop or self.shape[-1]
        for block in list(self.copies):
            if block[0] < high_end and (block[1] is None or block[1] > low_end):
                self.copies.pop(block).wait()
        return self.scratch[index]


class Save:
    def __init__(self, buffer, target, sems):
        self.buffer, self.target, self.sems, self.shape = buffer, target, sems, buffer.shape
        self.copies, self.whole = [], False

    def __getitem__(self, index):
        return self.buffer[index]

    def __setitem__(self, index, value):
        self.buffer[index] = value

    def flush(self, cols=None):
        if self.whole:
            return
        self.whole = cols is None
        here = (slice(None),) * (len(self.shape) - 1) + (cols,)
        copy = pltpu.make_async_copy(self.buffer if cols is None else self.buffer.at[here], self.target if cols is None else self.target.at[here], self.sems.at[len(self.copies)])
        copy.start()
        self.copies.append(copy)


def flush(ref, cols=None):
    if isinstance(ref, Save):
        ref.flush(cols)


def late(array, *blocks):
    return (array, blocks)


def save(shape, dtype):
    return (shape, dtype, "save")


def both(shape, dtype):
    return (shape, dtype, "both")


FLUSHES = 10


def run_kernel(kernel, in_kinds, out_kinds, kept, n_over, n_fetch, n_results, *refs):
    n_ins = 1 + len(in_kinds) + n_over + n_fetch
    ins, results, scratch = refs[1:n_ins], list(refs[n_ins : n_ins + n_results]), list(refs[n_ins + n_results :])
    given = []
    for ref, blocks in zip(ins, in_kinds):
        given.append(ref if blocks is None else Late(ref, scratch.pop(0), scratch.pop(0), blocks))
    saves, outs = [], []
    for i in kept:
        saves.append(Save(ins[i], results.pop(), scratch.pop(0)))
        saves[-1].flush()
    fetches = []
    for i in range(n_fetch):
        copy = pltpu.make_async_copy(refs[n_ins - n_fetch + i], results[len(results) - n_fetch + i], scratch.pop(0).at[0])
        copy.start()
        fetches.append(copy)
    results = results[: len(results) - n_fetch]
    for kind in out_kinds:
        if kind == "near":
            outs.append(results.pop(0))
            continue
        buffer = scratch.pop(0) if kind == "save" else results.pop(0)
        saves.append(Save(buffer, results.pop(0), scratch.pop(0)))
        outs.append(saves[-1])
    kernel(refs[0], *given, *outs, *scratch)
    for item in saves:
        if not item.copies:
            item.flush()
    for item in saves:
        for copy in item.copies:
            copy.wait()
    for copy in fetches:
        copy.wait()


def call(kernel, place, ins, outs, scratch=(), vmem=14, name=None, flops=0, keep=(), over=(), fetch=()):
    smem, near, far = pl.BlockSpec(memory_space=pltpu.SMEM), pl.BlockSpec(memory_space=pltpu.VMEM), pl.BlockSpec(memory_space=pl.ANY)
    in_specs, arrays, in_kinds, buffers = [smem], [place], [], []
    for entry in ins:
        if isinstance(entry, tuple):
            array, blocks = entry
            array = pltpu.with_memory_space_constraint(array, pltpu.HBM)
            in_specs.append(far)
            in_kinds.append(tuple(blocks))
            buffers += [pltpu.VMEM(array.shape, array.dtype), pltpu.SemaphoreType.DMA((max(1, len(blocks)),))]
        else:
            array = entry
            in_specs.append(smem if array.dtype == jnp.int32 else near)
            in_kinds.append(None)
        arrays.append(array)
    for array in over:
        in_specs.append(far)
        arrays.append(pltpu.with_memory_space_constraint(array, pltpu.HBM))
    for array in fetch:
        in_specs.append(far)
        arrays.append(pltpu.with_memory_space_constraint(array, pltpu.HBM))
    buffers += [pltpu.SemaphoreType.DMA((1,)) for _ in list(keep) + list(fetch)]
    out_specs, out_shapes, out_kinds = [], [], []
    for entry in outs:
        shape, dtype, kind = entry if len(entry) == 3 else entry + ("near",)
        out_kinds.append(kind)
        if kind != "save":
            out_specs.append(near)
            out_shapes.append(jax.ShapeDtypeStruct(shape, dtype))
        else:
            buffers.append(pltpu.VMEM(shape, dtype))
        if kind != "near":
            out_specs.append(far)
            out_shapes.append(pltpu.HBM(shape, dtype))
            buffers.append(pltpu.SemaphoreType.DMA((FLUSHES,)))
    for array in fetch:
        out_specs.append(near)
        out_shapes.append(jax.ShapeDtypeStruct(array.shape, array.dtype))
    for i in reversed(keep):
        out_specs.append(far)
        out_shapes.append(pltpu.HBM(ins[i].shape, ins[i].dtype))
    moved = sum(a.size * a.dtype.itemsize for a in arrays)
    return pl.pallas_call(
        functools.partial(run_kernel, kernel, tuple(in_kinds), tuple(out_kinds), tuple(keep), len(over), len(fetch), len(out_shapes)),
        in_specs=in_specs,
        out_specs=out_specs,
        out_shape=out_shapes,
        scratch_shapes=buffers + list(scratch),
        input_output_aliases={1 + len(ins) + i: i for i in range(len(over))},
        compiler_params=pltpu.CompilerParams(vmem_limit_bytes=vmem * MIB),
        cost_estimate=pl.CostEstimate(flops=flops, bytes_accessed=moved, transcendentals=0),
        name=name,
    )(*arrays)


def prepare_kernel(count, place, into, out, up, down, vectors, up_bias, cross_gain, cross_shift, sent, own_attn, own_feed, own_vecs):
    rows, width = out.shape
    half = width // 2
    section = place[0]

    def choose(make):
        first, later = make(0), make(1)
        return jnp.where(section == 0, first, later), jnp.where(section == 0, later, first)

    def feed_of(side_index):
        parts = []
        for fold in range(FOLDS):
            for device in range(count):
                begin = ((device * 2 + side_index) * FOLDS + fold) * rows
                parts.append(up[:, begin : begin + rows])
        parts += [down[(side_index * FOLDS + fold) * rows : (side_index * FOLDS + fold + 1) * rows, :] for fold in range(FOLDS)]
        return jnp.concatenate(parts, 1)

    attn, attn_other = choose(lambda i: jnp.concatenate([into[:, (2 * j + i) * half : (2 * j + i + 1) * half] for j in range(3)], 1))
    feed, feed_other = choose(feed_of)
    wide = lambda v: jnp.concatenate([v, jnp.zeros((v.shape[0], 128 - v.shape[1]), F32)], 1)
    lines = [wide(vectors[...].astype(F32))] + [wide(up_bias[:, i * rows : (i + 1) * rows].astype(F32)) for i in range(2 * FOLDS)]
    lines += [wide(cross_gain[...].astype(F32)), wide(cross_shift[...].astype(F32))]
    vecs = low(jnp.concatenate(lines + [jnp.zeros((128 - LAYER_VECS - 2, 128), F32)], 0).T[:rows])
    own_attn[:, :width] = out[...]
    own_attn[:, width:] = attn
    own_feed[...] = feed
    own_vecs[...] = vecs
    cols = width + 3 * half
    sent[:, :width] = out[...]
    sent[:, width:cols] = attn_other
    sent[:, cols : cols + 128] = vecs
    sent[:, cols + 128 :] = feed_other


def merge_kernel(place, got, own_attn, own_feed, own_vecs, attn_first, attn_last, feed_first, feed_last):
    section = place[0]
    cols = own_attn.shape[1]
    first, last = (lambda own, other: jnp.where(section == 0, own, other)), (lambda own, other: jnp.where(section == 0, other, own))
    attn, attn_other = own_attn[...], got[:, :cols]
    attn_first[:, :cols] = first(attn, attn_other)
    attn_last[...] = last(attn, attn_other)
    feed, feed_other = own_feed[...], got[:, cols + 128 :]
    feed_first[...] = first(feed, feed_other)
    feed_last[...] = last(feed, feed_other)
    vecs, vecs_other = own_vecs[...].astype(F32), got[:, cols : cols + 128].astype(F32)
    vecs_0, vecs_1 = first(vecs, vecs_other), last(vecs, vecs_other)
    half = vecs.shape[0] // 2
    cross = jnp.concatenate([vecs_0[:half], vecs_1[:half]], 0)
    lane = lax.broadcasted_iota(jnp.int32, vecs.shape, 1)
    turned = lambda v: pltpu.roll(v, LAYER_VECS, 1)
    attn_first[:, cols:] = low(jnp.where(lane < LAYER_VECS, vecs_0, jnp.where(lane < 2 * LAYER_VECS, turned(vecs_1), turned(cross))))


SELF_GAIN, SELF_SHIFT, FEED_GAIN, FEED_SHIFT, DOWN_BIAS, UP_BIAS = range(6)
FOLDS = 2
LAYER_VECS = 5 + 2 * FOLDS
CROSS_GAIN, CROSS_SHIFT = 2 * LAYER_VECS, 2 * LAYER_VECS + 1
VECS = 24


def woven(first, later, blocks):
    parts = [v.reshape(blocks, v.shape[0] // blocks, v.shape[1]) for v in (first, later)]
    return jnp.concatenate(parts, 1).reshape(2 * first.shape[0], first.shape[1])


def unwoven(value, blocks):
    parts = value.reshape(blocks, value.shape[0] // blocks, value.shape[1])
    half = parts.shape[1] // 2
    return jnp.concatenate([parts[:, :half].reshape(-1, value.shape[1]), parts[:, half:].reshape(-1, value.shape[1])], 0)


def side_in(section, own, other):
    first = jnp.where(section == 0, own, other)
    return jnp.concatenate([first, jnp.where(section == 0, other, own)], 1)


def half_in(section, values):
    half = values.shape[1] // 2
    return jnp.where(section == 0, values[:, :half], values[:, half:])


def vec(ref, row):
    return ref[row : row + 1, :]


def up_bias_of(vecs, layer, section, fold):
    return vecs[pl.ds(LAYER_VECS * layer + UP_BIAS + FOLDS * section + fold, 1), :]


def self_part(values, layer, lengths, vecs, weights, normed_ref, projected, mixed_ref):
    base = LAYER_VECS * layer
    unit, _ = norm_unit(values)
    normed = low(unit * vec(vecs, base + SELF_GAIN) + vec(vecs, base + SELF_SHIFT))
    normed_ref[...] = normed
    flush(normed_ref)
    half = mixed_ref.shape[1]
    width = values.shape[1]
    projected[...] = low(dot(normed, weights[:, width : width + 3 * half]))
    flush(projected)
    captions = lengths.shape[0]
    slots = values.shape[0] // captions
    for c in range(captions):
        keep = keep_mask(lengths[c], slots)
        here = slice(c * slots, (c + 1) * slots)
        for j in range(half // PAIR):
            q, k, v = (projected[here, i * half + j * PAIR : i * half + (j + 1) * PAIR] for i in range(3))
            chances = self_chances(stacked(q), k, keep)
            mixed_ref[here, j * PAIR : (j + 1) * PAIR] = low(unstacked(dot(low(chances), v)))


def self_first_kernel(aligned, place, lengths, text, weights, vecs, normed, projected, mixed):
    columns = weights[:, weights.shape[1] - 128 :].astype(F32)
    if aligned:
        lane = lax.broadcasted_iota(jnp.int32, columns.shape, 1)
        columns = jnp.where(lane < CROSS_GAIN, columns, unwoven(columns, weights.shape[0] // 48))
    vecs[...] = columns.T[: vecs.shape[0]]
    flush(vecs)
    self_part(text[...].astype(F32), 0, lengths, vecs, weights, normed, projected, mixed)


def self_second_kernel(place, lengths, middle, own, other, vecs, weights, hidden, normed, projected, mixed):
    total = middle[...] + (own[...].astype(F32) + other[...].astype(F32)) + vec(vecs, DOWN_BIAS)
    hidden[...] = low(total)
    flush(hidden)
    self_part(hidden[...].astype(F32), 1, lengths, vecs, weights, normed, projected, mixed)


def heads_rows(weights, section):
    width = weights.shape[0]
    return weights[pl.ds(pl.multiple_of(section * (width // 2), width // 2), width // 2), :width]


def add_heads_out(values, mixed, weights):
    return values + dot(mixed[...], weights[:, : values.shape[1]])


def feed_part(middle, layer, section, vecs, feed, normed_ref, slope_ref, active_ref):
    base = LAYER_VECS * layer
    width = middle.shape[1]
    unit, _ = norm_unit(middle)
    normed = low(unit * vec(vecs, base + FEED_GAIN) + vec(vecs, base + FEED_SHIFT))
    normed_ref[...] = normed
    flush(normed_ref)
    total = jnp.zeros_like(middle)
    for i in range(FOLDS):
        here = slice(i * width, (i + 1) * width)
        raised = dot(normed, feed[:, here]) + up_bias_of(vecs, layer, section, i)
        chance = 0.5 * (1.0 + lax.erf(raised * 0.5**0.5))
        slope_ref[:, here] = low(chance + raised * jnp.exp(-0.5 * raised * raised) * 0.3989422804014327)
        active = low(raised * chance)
        active_ref[:, here] = active
        flush(slope_ref, here)
        flush(active_ref, here)
        total += dot(active, feed[:, (FOLDS + i) * width : (FOLDS + i + 1) * width])
    return low(total)


def feed_first_kernel(place, text, own, other, vecs, weights, feed, mixed_all, middle, normed, slope, active, part):
    mixed_all[...] = side_in(place[0], own[...], other[...])
    flush(mixed_all)
    values = add_heads_out(text[...].astype(F32), mixed_all, weights)
    middle[...] = values
    flush(middle)
    part[...] = feed_part(values, 0, place[0], vecs, feed, normed, slope, active)


def by_caption(kernel, array, weights, out, name, flops):
    block = lambda shape: pl.BlockSpec((1,) + shape[1:], lambda i: (i, 0, 0))
    moved = array.size * array.dtype.itemsize + out.size * out.dtype.itemsize
    return pl.pallas_call(
        kernel,
        grid=(array.shape[0],),
        in_specs=[block(array.shape), pl.BlockSpec(weights.shape, lambda i: (0, 0))],
        out_specs=block(out.shape),
        out_shape=pltpu.HBM(out.shape, out.dtype),
        compiler_params=pltpu.CompilerParams(vmem_limit_bytes=24 * MIB),
        cost_estimate=pl.CostEstimate(flops=flops, bytes_accessed=moved, transcendentals=0),
        name=name,
    )(array, weights)


def pairs_kernel(place, image, keys, pairs):
    for c in range(image.shape[0]):
        pairs[c] = low(dot(image[c], keys[...]))


def image_grad_kernel(grad_pairs, keys, grad):
    grad[0] = dot_nt(grad_pairs[0], keys[...])


def cross_kernel(place, hidden, own, other, vecs, weights, query, pairs, mixed_all, first, normed_ref, queries, part, stats):
    mixed_all[...] = side_in(place[0], own[...], other[...])
    flush(mixed_all)
    values = add_heads_out(hidden[...].astype(F32), mixed_all, weights)
    first[...] = values
    flush(first)
    unit, _ = norm_unit(values)
    normed = low(unit * vec(vecs, CROSS_GAIN) + vec(vecs, CROSS_SHIFT))
    normed_ref[...] = normed
    flush(normed_ref)
    rows, width = values.shape
    queries[...] = low(dot(normed, query[...]))
    flush(queries)
    captions = pairs.shape[0]
    slots = rows // captions
    quads = width // QUAD
    for c in range(captions):
        here = slice(c * slots, (c + 1) * slots)
        for j in range(quads):
            cols = slice(j * QUAD, (j + 1) * QUAD)
            k, v = pairs[c, :, cols], pairs[c, :, width + j * QUAD : width + (j + 1) * QUAD]
            scores = dot_nt(k, stacked(queries[here, cols])) * SCALE
            top = jnp.max(scores, 0, keepdims=True)
            raised = jnp.exp(scores - top)
            part[here, cols] = low(unstacked(dot_tn(low(raised), v)))
            row = c * quads + j
            stats[row : row + 1, :] = top
            stats[STATS + row : STATS + row + 1, :] = jnp.sum(raised, 0, keepdims=True)


STATS = 16


def feed_second_kernel(place, first, own, other, own_stats, other_stats, vecs, out, feed, middle, mixed, factor, normed, slope, active, part):
    rows, width = first.shape
    quads = width // QUAD
    top, top_other = own_stats[:STATS], other_stats[:STATS]
    best = jnp.maximum(top, top_other)
    own_weight, other_weight = jnp.exp(top - best), jnp.exp(top_other - best)
    inverse = 1.0 / (own_stats[STATS:] * own_weight + other_stats[STATS:] * other_weight)
    own_factor, other_factor = own_weight * inverse, other_weight * inverse
    factor[...] = own_factor
    flush(factor)
    columns = jnp.concatenate([own_factor, other_factor, jnp.zeros((PAIR - 2 * STATS, QUAD), F32)], 0).T
    slots = QUAD // 4
    head = heads_of((slots, QUAD))
    for c in range(rows // slots):
        here = slice(c * slots, (c + 1) * slots)
        for j in range(quads):
            cols = slice(j * QUAD, (j + 1) * QUAD)

            def spread(column):
                out = columns[:slots, column : column + 1]
                for h in range(1, 4):
                    out = jnp.where(head == h, columns[h * slots : (h + 1) * slots, column : column + 1], out)
                return out

            row = c * quads + j
            mixed[here, cols] = low(spread(row) * own[here, cols].astype(F32) + spread(STATS + row) * other[here, cols].astype(F32))
    flush(mixed)
    values = first[...] + dot(mixed[...], out[...])
    middle[...] = values
    flush(middle)
    part[...] = feed_part(values, 1, place[0], vecs, feed, normed, slope, active)


def feed_back(grad, vecs, feed, slope, bias_grad, down_bias_grad, slope_ref, part):
    width = grad.shape[1]
    grad_low = low(grad)
    down_bias_grad[...] = jnp.sum(grad, 0, keepdims=True)
    total = jnp.zeros(grad.shape, F32)
    for i in range(FOLDS):
        here = slice(i * width, (i + 1) * width)
        down = feed[:, (FOLDS + i) * width : (FOLDS + i + 1) * width]
        grad_raised = low(dot_nt(grad_low, down) * slope[:, here].astype(F32))
        slope_ref[:, here] = grad_raised
        bias_grad[i : i + 1, :] = jnp.sum(grad_raised.astype(F32), 0, keepdims=True)
        total += dot_nt(grad_raised, feed[:, here])
    part[...] = low(total)


def feed_back_last_kernel(place, cot, vecs, feed, slope, bias_grad, down_bias_grad, grad_raised, part):
    feed_back(cot[...].astype(F32), vecs, feed, slope, bias_grad, down_bias_grad, grad_raised, part)


def cross_back_kernel(place, own, other, middle, vecs, cot, out, queries, pairs, stats, factor, mixed, grad_ref, low_ref, vec_grad, query_part, grad_pairs, grad_mixed):
    rows, width = middle.shape
    inner = own[...].astype(F32) + other[...].astype(F32)
    step, gain_grad, shift_grad = norm_back(middle[...], vec(vecs, LAYER_VECS + FEED_GAIN), inner)
    vec_grad[0:1, :] = gain_grad
    vec_grad[1:2, :] = shift_grad
    grad = step + cot[...].astype(F32)
    grad_ref[...] = grad
    low_ref[...] = low(grad)
    grad_mixed[...] = low(dot_nt(low(grad), out[...]))
    captions = pairs.shape[0]
    slots = rows // captions
    quads = width // QUAD
    for c in range(captions):
        here = slice(c * slots, (c + 1) * slots)
        for j in range(quads):
            cols = slice(j * QUAD, (j + 1) * QUAD)
            later = slice(width + j * QUAD, width + (j + 1) * QUAD)
            row = slice(c * quads + j, c * quads + j + 1)
            k, v = pairs[c, :, cols], pairs[c, :, later]
            q = stacked(queries[here, cols])
            grad_block = grad_mixed[here, cols]
            grads = stacked(grad_block)
            delta = row_sums(stacked(grad_block.astype(F32) * mixed[here, cols].astype(F32)))
            chances = jnp.exp(dot_nt(k, q) * SCALE - stats[row, :]) * factor[row, :]
            slope = low(chances * (dot_nt(v, grads) - delta))
            query_part[here, cols] = low(unstacked(dot_tn(slope, k)) * SCALE)
            grad_pairs[c, :, cols] = low(dot(slope, q) * SCALE)
            grad_pairs[c, :, later] = low(dot(low(chances), grads))


def self_back(grad, section, lengths, weights, projected, low_ref, grad_projected, grad_mixed):
    half = grad_mixed.shape[1]
    low_ref[...] = low(grad)
    flush(low_ref)
    grad_mixed[...] = low(dot_nt(low(grad), heads_rows(weights, section)))
    captions = lengths.shape[0]
    slots = grad.shape[0] // captions
    for c in range(captions):
        keep = keep_mask_turned(lengths[c], slots)
        here = slice(c * slots, (c + 1) * slots)
        for j in range(half // PAIR):
            cols = [slice(i * half + j * PAIR, i * half + (j + 1) * PAIR) for i in range(3)]
            q, k, v = (projected[here, cols[i]] for i in range(3))
            q = stacked(q)
            chances = self_chances_turned(q, k, keep)
            grads = stacked(grad_mixed[here, cols[0]])
            grad_chances = dot_nt(v, grads)
            slope = low(chances * (grad_chances - jnp.sum(grad_chances * chances, 0, keepdims=True)))
            grad_projected[here, cols[0]] = low(unstacked(dot_tn(slope, k)) * SCALE)
            grad_projected[here, cols[1]] = low(dot(slope, q) * SCALE)
            grad_projected[here, cols[2]] = low(dot(low(chances), grads))
    width = grad.shape[1]
    return dot_nt(grad_projected[...], weights[:, width : width + 3 * half])


def self_back_second_kernel(place, lengths, grad_middle, own, other, first, vecs, query, weights, projected, grad_ref, low_ref, grad_queries, grad_projected, part, vec_grad, grad_mixed):
    total = low(own[...].astype(F32) + other[...].astype(F32))
    grad_queries[...] = total
    inner = dot_nt(total, query[...])
    step, gain_grad, shift_grad = norm_back(first[...], vec(vecs, CROSS_GAIN), inner)
    vec_grad[0:1, :] = gain_grad
    vec_grad[1:2, :] = shift_grad
    grad = step + grad_middle[...]
    grad_ref[...] = grad
    part[...] = low(self_back(grad, place[0], lengths, weights, projected, low_ref, grad_projected, grad_mixed))


def feed_back_first_kernel(place, grad_first, own, other, hidden, vecs, slope, feed, grad_ref, low_ref, vec_grad, bias_grad, down_bias_grad, grad_raised, part):
    inner = own[...].astype(F32) + other[...].astype(F32)
    step, gain_grad, shift_grad = norm_back(hidden[...].astype(F32), vec(vecs, LAYER_VECS + SELF_GAIN), inner)
    vec_grad[0:1, :] = gain_grad
    vec_grad[1:2, :] = shift_grad
    low_ref[...] = low(step + grad_first[...])
    grad = low_ref[...].astype(F32)
    grad_ref[...] = grad
    feed_back(grad, vecs, feed, slope, bias_grad, down_bias_grad, grad_raised, part)


def self_back_first_kernel(place, lengths, grad_hidden, own, other, middle, text, vecs, projected, weights, grad_ref, low_ref, grad_projected, part, vec_grad, grad_mixed):
    inner = own[...].astype(F32) + other[...].astype(F32)
    step, gain_grad, shift_grad = norm_back(middle[...], vec(vecs, FEED_GAIN), inner)
    vec_grad[0:1, :] = gain_grad
    vec_grad[1:2, :] = shift_grad
    grad = step + grad_hidden[...]
    grad_ref[...] = grad
    total = self_back(grad, place[0], lengths, weights, projected, low_ref, grad_projected, grad_mixed)
    part[...] = low(total)
    unit, _ = norm_unit(text[...].astype(F32))
    vec_grad[2:3, :] = jnp.sum(total * unit, 0, keepdims=True)
    vec_grad[3:4, :] = jnp.sum(total, 0, keepdims=True)


def text_grad_kernel(place, grad_middle, own, other, text, vecs, out):
    inner = own[...].astype(F32) + other[...].astype(F32)
    step, _, _ = norm_back(text[...].astype(F32), vec(vecs, SELF_GAIN), inner)
    total = step + grad_middle[...]
    half = out.shape[1]
    out[...] = jnp.where(place[0] == 0, total[:, :half], total[:, half:])


BLOCK = 384


def weight_grads(pieces, refs, put):
    offset = 0
    rows = min(refs[left].shape[1] for left, _ in pieces)
    for left, right in pieces:
        for i in range(refs[left].shape[1] // rows):
            for j in range(refs[right].shape[1] // BLOCK):
                put(offset, dot_tn(refs[left][:, i * rows : (i + 1) * rows], refs[right][:, j * BLOCK : (j + 1) * BLOCK]))
                offset += BLOCK
    return offset


def put_in_order(order, out, cols, value):
    rows = value.shape[0] // len(order)
    for i, device in enumerate(order):
        out[i * rows : (i + 1) * rows, cols] = low(value[device * rows : (device + 1) * rows])
    flush(out, cols)


def products_kernel(order, pieces, place, *refs):
    weight_grads(pieces, refs, lambda offset, value: put_in_order(order, refs[-1], slice(offset, offset + value.shape[1]), value))


def put_by_core(core, mine, sent):
    chips, rows, _ = mine.shape

    def put(offset, value):
        cols = slice(offset, offset + value.shape[1])
        for chip in range(chips):
            first = value[2 * chip * rows : (2 * chip + 1) * rows]
            later = value[(2 * chip + 1) * rows : (2 * chip + 2) * rows]
            mine[chip, :, cols] = low(jnp.where(core == 0, first, later))
            sent[chip, :, cols] = low(jnp.where(core == 0, later, first))
        flush(mine, cols)
        flush(sent, cols)

    return put


def ring_products_kernel(pieces, place, *refs):
    weight_grads(pieces, refs, put_by_core(place[1], *refs[-2:]))


def last_products_kernel(
    blocks, place, normed, grad_projected, mixed_0, mixed_1, low_0, low_1, vecs_0, self_vecs_1, feed_vecs_1, cross_vecs, down_0, down_1, bias_0, bias_1, mine, sent
):
    section = place[0]
    put = put_by_core(place[1], mine, sent)
    width = normed.shape[1]
    offset = weight_grads(((0, 1),), (normed, grad_projected), put)
    mixed = jnp.where(section == 0, mixed_0[...], mixed_1[...])
    head_low = jnp.where(section == 0, low_0[...], low_1[...])
    for j in range(width // BLOCK):
        put(offset, dot_tn(mixed, head_low[:, j * BLOCK : (j + 1) * BLOCK]))
        offset += BLOCK
    rows = [
        vecs_0[2:4, :],
        jnp.where(section == 0, 0.0, self_vecs_1[0:2, :]),
        jnp.where(section == 0, vecs_0[0:2, :], feed_vecs_1[0:2, :]),
        jnp.where(section == 0, down_0[...], down_1[...]),
        bias_0[...],
        bias_1[...],
        cross_vecs[0:2, :],
    ]
    used = 7 + 2 * FOLDS
    columns = jnp.concatenate(rows + [jnp.zeros((128 - used - 2, width), F32)], 0).T
    if blocks:
        lane = lax.broadcasted_iota(jnp.int32, columns.shape, 1)
        columns = jnp.where(lane < used, columns, woven(columns[: width // 2], columns[width // 2 :], blocks))
    put(offset, columns)


def keys_products_kernel(blocks, offset, place, image, grad_pairs, mine, sent):
    put = put_by_core(place[1], mine, sent)
    half = image.shape[2] // 2
    for j in range(grad_pairs.shape[2] // BLOCK):
        value = sum(dot_tn(image[c], grad_pairs[c, :, j * BLOCK : (j + 1) * BLOCK]) for c in range(image.shape[0]))
        put(offset + j * BLOCK, woven(value[:half], value[half:], blocks))


def second_products_kernel(blocks, place, normed, grad_queries, mixed, grad_low, self_normed, grad_projected, mine, sent):
    put = put_by_core(place[1], mine, sent)
    offset = weight_grads(((0, 1),), (self_normed, grad_projected), put)
    own_normed, own_mixed = half_in(place[0], normed[...]), half_in(place[0], mixed[...])
    for j in range(grad_queries.shape[1] // BLOCK):
        cols = slice(j * BLOCK, (j + 1) * BLOCK)
        put(offset, woven(dot_tn(own_normed, grad_queries[:, cols]), dot_tn(own_mixed, grad_low[:, cols]), blocks))
        offset += BLOCK


def in_order(section, own, other):
    own, other = own.astype(F32), other.astype(F32)
    return jnp.where(section == 0, own, other), jnp.where(section == 0, other, own)


def finish_feed_kernel(count, place, own, other, up, down):
    rows, width = own.shape[0], down.shape[1]
    halves = in_order(place[0], own[...], other[...])
    parts = []
    for device in range(count):
        for half in halves:
            for fold in range(FOLDS):
                begin = fold * width + device * rows
                parts.append(half[:, begin : begin + rows])
    up[...] = jnp.concatenate(parts, 1)
    for i, half in enumerate(halves):
        for fold in range(FOLDS):
            begin = (i * FOLDS + fold) * rows
            down[begin : begin + rows, :] = half[:, (FOLDS + fold) * width : (FOLDS + fold + 1) * width]


def finish_cross_kernel(place, heads, keys, keys_other, query_grad, keys_grad, out_grad):
    rows = query_grad.shape[0]
    heads32, keys32 = heads[...].astype(F32), keys[...].astype(F32)
    query_grad[...] = heads32[:rows]
    out_grad[...] = heads32[rows:]
    keys_grad[...] = jnp.where(place[0] == 0, keys32[:rows], keys32[rows:]) + keys_other[...].astype(F32)


def finish_heads_kernel(cross_rows, place, sums, own, other, into, out, gain, shift, feed_gain, feed_shift, down_bias, cross_gain, cross_shift, up_bias):
    rows, width = out.shape
    half = width // 2
    section = place[0]
    halves = in_order(section, own[...], other[:, : 3 * half])
    for i in range(3):
        for j, part in enumerate(halves):
            into[:, (2 * i + j) * half : (2 * i + j + 1) * half] = part[:, i * half : (i + 1) * half]
    out[...] = sums[:, 3 * half : 3 * half + width]
    flipped = lambda v: jnp.concatenate([v.astype(F32), jnp.zeros((128 - rows, 128), F32)], 0).T[:, :rows]
    own_vec, other_vec = flipped(sums[:, 3 * half + width :]), flipped(other[:, 3 * half :])
    mine = lambda v, first, later: jnp.where(section == 0, v[first : first + 1], v[later : later + 1])
    gain[...] = mine(own_vec, 0, 2) + mine(other_vec, 0, 2)
    shift[...] = mine(own_vec, 1, 3) + mine(other_vec, 1, 3)
    feed_gain[...] = own_vec[4:5]
    feed_shift[...] = own_vec[5:6]
    down_bias[...] = own_vec[6:7]
    bias = [[mine(v, 7 + i, 7 + FOLDS + i) for i in range(FOLDS)] for v in (own_vec, other_vec)]
    ordered = [jnp.where(section == 0, a, b) for a, b in zip(*bias)] + [jnp.where(section == 0, b, a) for a, b in zip(*bias)]
    up_bias[...] = jnp.concatenate(ordered, 1)
    for i, ref in enumerate((cross_gain, cross_shift)):
        row = own_vec[7 + 2 * FOLDS + i : 8 + 2 * FOLDS + i]
        ref[...] = jnp.where(section == 0, row[:, :cross_rows], row[:, cross_rows:])


def body(
    text,
    image,
    lengths,
    self_gain,
    self_shift,
    heads_in,
    heads_out,
    feed_gain,
    feed_shift,
    up_weight,
    up_bias,
    down_weight,
    down_bias,
    cross_gain,
    cross_shift,
    cross_query,
    cross_keys,
    cross_out,
    cotangent,
):
    section = lax.axis_index("section")
    count = lax.axis_size("dp")
    core = lax.axis_index("dp") % 2
    place = jnp.stack([section, core]).astype(jnp.int32)
    captions, half_image, width = image.shape
    rows = text.shape[0]
    piece = heads_in.shape[1]
    cross_piece = cross_query.shape[0]
    half = width // 2
    half_ff = FOLDS * width
    aligned = piece % 16 == 0
    order = [2 * chip + i for chip in ring_order() for i in range(2)] if aligned else list(range(count))
    groups = [order]

    def both_layers(first, later):
        own, got = pick(section, first, later), swap(pick(section, later, first))
        return pick(section, own, got), pick(section, got, own)

    core_cols = width + 3 * half
    cross_own = jnp.concatenate([cross_keys, cross_query, cross_out], 1)
    if aligned:
        vectors = jnp.concatenate([self_gain, self_shift, feed_gain, feed_shift, down_bias], 0)
        sent, own_attn, own_feed, own_vecs = call(
            functools.partial(prepare_kernel, count),
            place,
            [late(v) for v in (heads_in[0], heads_out[0], up_weight[0], down_weight[0], vectors, up_bias, cross_gain[None], cross_shift[None])],
            [((piece, cols), BF16) for cols in (core_cols + 128 + 2 * half_ff, core_cols, 2 * half_ff, 128)],
            name="prepare",
        )
        attn_rows_0, attn_1, feed_0, feed_1 = call(
            merge_kernel, place, [swap(sent), own_attn, own_feed, own_vecs], [((piece, cols), BF16) for cols in (core_cols + 128, core_cols, 2 * half_ff, 2 * half_ff)], name="merge"
        )
    else:
        up = up_weight[0].reshape(piece, count, 2, FOLDS, piece).transpose(2, 0, 3, 1, 4).reshape(2, piece, half_ff)
        down = down_weight[0].reshape(2, FOLDS, piece, width)
        feed_own = [jnp.concatenate([up[i]] + [down[i, j] for j in range(FOLDS)], 1) for i in range(2)]
        into = heads_in[0].reshape(piece, 3, 2, half)
        attn_own = [jnp.concatenate([heads_out[0], into[:, :, i].reshape(piece, 3 * half)], 1) for i in range(2)]
        own_vecs = jnp.concatenate([self_gain, self_shift, feed_gain, feed_shift, down_bias, up_bias.reshape(2 * FOLDS, piece)], 0)
        own_cross_vecs = jnp.concatenate([cross_gain[None], cross_shift[None]], 0)
        sent_vecs = jnp.concatenate([own_vecs, jnp.pad(own_cross_vecs, ((0, 0), (0, piece - cross_piece)))], 0)
        feed_0, feed_1 = both_layers(*feed_own)
        feed_0, feed_1, sent_vecs, *attn_own = together(feed_0, feed_1, sent_vecs, *attn_own)
        attn_0, attn_1 = both_layers(*attn_own)
        got_vecs = swap(sent_vecs)
        cross_vec_rows = side(own_cross_vecs, got_vecs[LAYER_VECS:, :cross_piece], section, 1)
        vec_cols = jnp.concatenate([pick(section, own_vecs, got_vecs[:LAYER_VECS]), pick(section, got_vecs[:LAYER_VECS], own_vecs), cross_vec_rows], 0)
        vec_cols = jnp.pad(vec_cols, ((0, 128 - vec_cols.shape[0]), (0, 0))).T
        attn_rows_0 = jnp.concatenate([attn_0, vec_cols], 1)
    ring_f = Gather(feed_0)
    ring_f.move()

    def gather(value):
        return lax.all_gather(value, "dp", axis=0, tiled=True, axis_index_groups=groups)

    def reordered(value, blocks, parts, widths):
        rows_out = value.shape[0] * parts
        if aligned:
            return call(functools.partial(reorder_kernel, blocks, parts), place, [value], [((rows_out, w), BF16) for w in widths], name="reorder")
        whole = value.reshape(value.shape[0], parts, sum(widths)).transpose(1, 0, 2).reshape(rows_out, sum(widths))
        ends = [sum(widths[: i + 1]) for i in range(len(widths))]
        return [whole[:, end - w : end] for end, w in zip(ends, widths)]

    attn_first = gather(attn_rows_0)
    attn_1, feed_1, cross_own, text_own, cot_own = meet([ring_f], attn_1, feed_1, cross_own, text, cotangent)
    cross_got = swap(cross_own)
    text_all = side(text, swap(text_own), section, 1)
    feed_last = gather(feed_1)
    cot_all = side(cotangent, swap(cot_own), section, 1)
    ring_d = Gather(attn_1)
    for i in range(ring_f.steps - 2):
        ring_f.move()
        ring_d.move()
        if i == 0:
            (cross_got,) = meet([ring_f, ring_d], cross_got)
            cross_all = gather(side(cross_own, cross_got, section, 1))
        elif i < ring_f.steps - 3:
            meet([ring_f, ring_d])
    (attn_first,) = meet([ring_f, ring_d], attn_first)
    ring_f.move()
    ring_d.move()
    (weights_0,) = reordered(attn_first, order, 1, [core_cols + 128])

    shape_f = ((rows, width), F32)
    shape_b = ((rows, width), BF16)
    shape_half = ((rows, half), BF16)
    shape_qkv = ((rows, 3 * half), BF16)
    shape_active = ((rows, half_ff), BF16)
    shape_stats = ((2 * STATS, QUAD), F32)
    shape_factor = ((STATS, QUAD), F32)
    shape_pairs = ((captions, half_image, 2 * width), BF16)
    shape_vec = ((8, width), F32)
    shape_bias = ((FOLDS, width), F32)
    shape_one = ((1, width), F32)
    half_scratch = [pltpu.VMEM((rows, half), BF16)]
    self_flops, feed_flops, pair_flops = 6 * rows * width * half, 4 * rows * width * half_ff, 4 * captions * half_image * width * width
    feed_blocks = [(i * width, (i + 1) * width) for i in (2, 0, 3, 1)]
    attn_blocks = [(0, width), (width, core_cols)]

    vecs, vecs_far, normed_a0, qkv_0, mixed_0, weights_0_far = call(
        functools.partial(self_first_kernel, aligned),
        place,
        [lengths, text_all, weights_0],
        [both((VECS, width), F32), save(*shape_b), save(*shape_qkv), shape_half],
        name="self_0",
        flops=self_flops,
        keep=(2,),
    )
    if not aligned:
        straight = lambda v: jnp.concatenate([v[:CROSS_GAIN], v[CROSS_GAIN : CROSS_GAIN + 2].reshape(2, count, 2, cross_piece).transpose(0, 2, 1, 3).reshape(2, width), v[CROSS_GAIN + 2 :]], 0)
        vecs, vecs_far = straight(vecs), straight(vecs_far)
    other_0 = swap(mixed_0)
    (mixed_0,) = meet([ring_f, ring_d], mixed_0)
    ring_f.pack()
    while ring_d.step < ring_d.steps:
        ring_d.move()
    other_0, ring_f.other = together(other_0, ring_f.other)
    feed_w0 = ring_f.result(place)
    keys, query, cross_out_w = reordered(cross_all, ring_order() if aligned else [0], 2, [2 * width, width, width])
    mixed_all_0, middle_0, normed_f0, slope_f0, active_0, part_0, feed_w0_far = call(
        feed_first_kernel,
        place,
        [text_all, mixed_0, other_0, vecs, weights_0, feed_w0],
        [save(*shape_b), save(*shape_f), save(*shape_b), save(*shape_active), save(*shape_active), shape_b],
        name="feed_0",
        flops=feed_flops,
        keep=(5,),
    )
    part_0_other = swap(part_0)
    (part_0,) = meet([ring_d], part_0)
    ring_d.pack()
    weights_1 = ring_d.result(place)
    hidden, hidden_far, normed_a1, qkv_1, mixed_1 = call(
        self_second_kernel,
        place,
        [lengths, late(middle_0), part_0, part_0_other, vecs, weights_1],
        [both(*shape_b), save(*shape_b), save(*shape_qkv), shape_half],
        name="self_1",
        flops=self_flops,
    )
    other_1 = swap(mixed_1)
    pairs, keys_far = call(pairs_kernel, place, [late(image), keys], [shape_pairs], name="pairs", flops=pair_flops, keep=(1,))
    other_1, pairs = together(other_1, pairs)
    mixed_all_1, first_1, normed_c, queries, cross_part, stats, stats_far, query_far, weights_1_far = call(
        cross_kernel,
        place,
        [hidden, mixed_1, other_1, vecs, weights_1, query, pairs],
        [save(*shape_b), save(*shape_f), save(*shape_b), save(*shape_b), shape_b, both(*shape_stats)],
        name="cross_1",
        flops=4 * rows * width * width,
        keep=(4, 5),
    )
    cross_part_other, stats_other = swap(cross_part), swap(stats)
    (feed_w1,) = reordered(feed_last, order, 1, [2 * half_ff])
    middle_1_far, cross_mixed_far, factor, normed_f1, slope_f1, active_1, part_1, cross_out_far = call(
        feed_second_kernel,
        place,
        [late(first_1), cross_part, cross_part_other, stats, stats_other, vecs, cross_out_w, feed_w1],
        [save(*shape_f), save(*shape_b), save(*shape_factor), shape_b, shape_active, shape_active, shape_b],
        name="feed_1",
        flops=feed_flops,
        keep=(6,),
    )
    own_cols = lambda v: pick(section, v[..., :half], v[..., half:])

    def meet_sums(rings, *values):
        flat = together(*[v for ring in rings for v in ring.front()], *values)
        for i, ring in enumerate(rings):
            ring.put_front(flat[2 * i : 2 * i + 2])
        return flat[2 * len(rings) :]

    def scatter(value):
        return lax.psum_scatter(value, "dp", scatter_dimension=0, tiled=True, axis_index_groups=groups)

    bias_grad_1, down_bias_grad_1, slope_1, back_1 = call(
        feed_back_last_kernel, place, [cot_all, vecs, feed_w1, slope_f1], [save(*shape_bias), save(*shape_one), shape_active, shape_b], name="feed_back_1", flops=feed_flops
    )
    back_1_other = swap(back_1)
    (feed_grad_1,) = call(
        functools.partial(products_kernel, order, ((0, 1), (2, 3))),
        place,
        [normed_f1, slope_1, active_1, cot_all],
        [save((width, 2 * half_ff), BF16)],
        name="feed_grads_1",
        flops=feed_flops,
    )
    back_1_other, feed_grad_1 = together(back_1_other, feed_grad_1)
    feed_got_1 = scatter(feed_grad_1)
    grad_middle_1, grad_low_1, feed_vec_1, query_part, grad_pairs = call(
        cross_back_kernel,
        place,
        [back_1, back_1_other, late(middle_1_far), late(vecs_far), late(cot_all), late(cross_out_far), late(queries), pairs, late(stats_far), late(factor), late(cross_mixed_far)],
        [shape_f, shape_b, save(*shape_vec), shape_b, shape_pairs],
        scratch=[pltpu.VMEM((rows, width), BF16)],
        name="cross_back",
        flops=4 * rows * width * width,
    )
    query_part_other = swap(query_part)
    ring_shape = lambda cols: ((count // 2, piece, cols), BF16)
    second_cols = 3 * half + 3 * width
    if aligned:
        *keys_grads, first_now, query_now, weights_now, qkv_now = call(
            functools.partial(keys_products_kernel, count, 3 * half + width),
            place,
            [late(image), grad_pairs],
            [save(*ring_shape(second_cols)), save(*ring_shape(second_cols))],
            vmem=20,
            name="keys_grads",
            flops=pair_flops,
            fetch=(first_1, query_far, weights_1_far, qkv_1),
        )
        query_part_other, *keys_grads = together(query_part_other, *keys_grads)
    else:
        first_now, query_now, weights_now, qkv_now = first_1, query_far, weights_1_far, qkv_1
    grad_first_1, head_low_1, grad_queries, grad_qkv_1, self_back_1, cross_vec_1 = call(
        self_back_second_kernel,
        place,
        [lengths, grad_middle_1, query_part, query_part_other, first_now, late(vecs_far), query_now, weights_now, qkv_now],
        [shape_f, save(*shape_b), shape_b, shape_qkv, shape_b, save(*shape_vec)],
        scratch=half_scratch,
        name="self_back_1",
        flops=2 * self_flops,
    )
    self_back_1_other = swap(self_back_1)
    if aligned:
        second_grads = call(
            functools.partial(second_products_kernel, count),
            place,
            [late(normed_c), grad_queries, late(cross_mixed_far), grad_low_1, late(normed_a1), grad_qkv_1],
            [save(*ring_shape(second_cols)), save(*ring_shape(second_cols))],
            vmem=20,
            name="second_grads",
            flops=2 * rows * width * (width + 3 * half),
            over=keys_grads,
        )
    else:
        pair_rows = lambda v: v.reshape(2, count, cross_piece, v.shape[1]).transpose(1, 0, 2, 3).reshape(width, v.shape[1])
        flat = lambda v: v.reshape(captions * half_image, v.shape[2])
        heads = pair_rows(jnp.concatenate([dot_tn(own_cols(normed_c), grad_queries), dot_tn(own_cols(cross_mixed_far), grad_low_1)], 0))
        second_grad = low(jnp.concatenate([dot_tn(normed_a1, grad_qkv_1), heads, pair_rows(dot_tn(flat(image), flat(grad_pairs)))], 1))
        parts = second_grad.reshape(count // 2, 2, piece, second_cols)
        second_grads = pick(core, parts[:, 0], parts[:, 1]), pick(core, parts[:, 1], parts[:, 0])
    early_grads = second_grads[1]
    self_back_1_other, *second_grads = together(self_back_1_other, *second_grads)
    ring_second = Scatter(*second_grads)
    ring_second.begin(early_grads)
    (self_back_1_other,) = ring_second.step(self_back_1_other)
    grad_hidden, grad_hidden_low, self_vec_1, bias_grad_0, down_bias_grad_0, slope_0, back_0 = call(
        feed_back_first_kernel,
        place,
        [grad_first_1, self_back_1, self_back_1_other, late(hidden_far), late(vecs_far), late(slope_f0, *[(i * width, (i + 1) * width) for i in range(FOLDS)]), late(feed_w0_far, *feed_blocks)],
        [shape_f, shape_b, save(*shape_vec), save(*shape_bias), save(*shape_one), shape_active, shape_b],
        name="feed_back_0",
        flops=feed_flops,
    )
    back_0_other = swap(back_0)
    (back_0,) = meet_sums([ring_second], back_0)
    (slope_0,) = ring_second.step(slope_0)
    (feed_grad_0,) = call(
        functools.partial(products_kernel, order, ((0, 1), (2, 3))),
        place,
        [late(normed_f0), slope_0, late(active_0), grad_hidden_low],
        [save((width, 2 * half_ff), BF16)],
        name="feed_grads_0",
        flops=feed_flops,
    )
    back_0_other, feed_grad_0, up, down = together(back_0_other, feed_grad_0, *ring_second.front())
    ring_second.put_front((up, down))
    feed_got_0 = scatter(feed_grad_0)
    (back_0_other,) = ring_second.step(back_0_other)
    grad_middle_0, head_low_0, grad_qkv_0, self_back_0, vecs_grad_0 = call(
        self_back_first_kernel,
        place,
        [lengths, grad_hidden, back_0, back_0_other, late(middle_0), text_all, late(vecs_far), late(qkv_0), late(weights_0_far, *attn_blocks)],
        [shape_f, shape_b, shape_qkv, shape_b, shape_vec],
        scratch=half_scratch,
        name="self_back_0",
        flops=2 * self_flops,
    )
    self_back_0_other = swap(self_back_0)
    (grad_qkv_0,) = meet_sums([ring_second], grad_qkv_0)
    grad_qkv_0, grad_pairs = ring_second.step(grad_qkv_0, grad_pairs)
    image_grad = by_caption(image_grad_kernel, grad_pairs, keys_far, jax.ShapeDtypeStruct((captions, half_image, width), F32), "image_grad", pair_flops)
    cross_vec_woven = cross_vec_1
    if not aligned:
        cross_vec_woven = cross_vec_1.reshape(8, 2, count, cross_piece).transpose(0, 2, 1, 3).reshape(8, width)
    last_grads = call(
        functools.partial(last_products_kernel, count if aligned else 0),
        place,
        [late(normed_a0), grad_qkv_0, late(mixed_all_0), late(mixed_all_1), head_low_0, late(head_low_1), vecs_grad_0]
        + [late(v) for v in (self_vec_1, feed_vec_1, cross_vec_woven, down_bias_grad_0, down_bias_grad_1, bias_grad_0, bias_grad_1)],
        [save(*ring_shape(core_cols + 128)), save(*ring_shape(core_cols + 128))],
        vmem=20,
        name="last_grads",
        flops=2 * rows * width * core_cols,
    )
    *last_grads, feed_got_1, self_back_0_other, image_grad = meet_sums([ring_second], *last_grads, feed_got_1, self_back_0_other, image_grad)
    ring_last = Scatter(*last_grads)
    ring_last.begin()
    (grad_middle_0,) = ring_last.step(grad_middle_0)
    (text_grad,) = call(text_grad_kernel, place, [grad_middle_0, self_back_0, self_back_0_other, text_all, late(vecs_far)], [((rows, half), F32)], name="text_grad")
    (text_grad,) = meet_sums([ring_last], text_grad)
    (ring_second.mine,) = ring_last.step(ring_second.mine)
    second_got = low(ring_second.result())
    (second_got,) = meet_sums([ring_last], second_got)
    ring_last.step()

    def other_half(first, later):
        return swap(pick(section, low(later), low(first)))

    (feed_got_0,) = meet_sums([ring_last], feed_got_0)
    feed_other = other_half(feed_got_0, feed_got_1)
    ring_last.step()
    got_part = swap(pick(section, part_1[:, half:], part_1[:, :half]))
    layer_out = own_cols(middle_1_far) + (own_cols(part_1).astype(F32) + got_part.astype(F32)) + own_cols(vecs_far[LAYER_VECS + DOWN_BIAS])
    cross_got = second_got[:, 3 * half : 3 * half + width]
    keys_got = second_got[:, 3 * half + width :]
    keys_other = swap(pick(section, keys_got[cross_piece:], keys_got[:cross_piece]))
    feed_own = pick(section, feed_got_0, feed_got_1)
    into_got_1 = second_got[:, : 3 * half]
    if aligned:
        up_grad, down_grad = call(
            functools.partial(finish_feed_kernel, count),
            place,
            [feed_own, feed_other],
            [((piece, 2 * half_ff), F32), ((2 * FOLDS * piece, width), F32)],
            name="finish_feed",
        )
        cross_query_grad, cross_keys_grad, cross_out_grad = call(
            finish_cross_kernel,
            place,
            [cross_got, keys_got, keys_other],
            [((cross_piece, width), F32), ((cross_piece, 2 * width), F32), ((cross_piece, width), F32)],
            name="finish_cross",
        )
        keys_other, cross_query_grad = together(keys_other, cross_query_grad)
    else:
        feed_parts = [v.astype(F32) for v in (pick(section, feed_own, feed_other), pick(section, feed_other, feed_own))]
        up_parts = [v[:, :half_ff].reshape(piece, FOLDS, count, piece).transpose(0, 2, 1, 3) for v in feed_parts]
        up_grad = jnp.stack(up_parts, 2).reshape(piece, 2 * half_ff)
        down_parts = [v[:, half_ff:].reshape(piece, FOLDS, width).transpose(1, 0, 2) for v in feed_parts]
        down_grad = jnp.stack(down_parts, 0).reshape(2 * FOLDS * piece, width)
        cross_query_grad, cross_out_grad = cross_got[:cross_piece].astype(F32), cross_got[cross_piece:].astype(F32)
        own_keys = pick(section, keys_got[:cross_piece], keys_got[cross_piece:])
        cross_keys_grad = own_keys.astype(F32) + keys_other.astype(F32)
    last_got = ring_last.result()
    vec_got = last_got[:, core_cols:]
    last_other = swap(low(jnp.concatenate([pick(section, into_got_1.astype(F32), last_got[:, : 3 * half]), vec_got], 1)))
    into_own = pick(section, last_got[:, : 3 * half], into_got_1.astype(F32))
    if aligned:
        shape_row = ((1, piece), F32)
        heads_in_grad, heads_out_grad, *rows_out, up_bias_grad = call(
            functools.partial(finish_heads_kernel, cross_piece),
            place,
            [last_got, into_own, last_other],
            [((piece, 6 * half), F32), ((piece, width), F32)] + [shape_row] * 5 + [((1, cross_piece), F32)] * 2 + [((1, 2 * FOLDS * piece), F32)],
            name="finish_heads",
        )
        cross_gain_grad, cross_shift_grad = rows_out[5][0], rows_out[6][0]
    else:
        into_other = last_other[:, : 3 * half].astype(F32)
        into_parts = pick(section, into_own, into_other), pick(section, into_other, into_own)
        heads_in_grad = jnp.stack([v.reshape(piece, 3, half) for v in into_parts], 2).reshape(piece, 6 * half)
        heads_out_grad = last_got[:, 3 * half : core_cols]
        own_vec, other_vec = vec_got.T, last_other[:, 3 * half :].astype(F32).T
        mine = lambda v, begin, size: pick(section, v[begin : begin + size], v[begin + size : begin + 2 * size])
        self_vec = mine(own_vec, 0, 2) + mine(other_vec, 0, 2)
        rows_out = [self_vec[0:1], self_vec[1:2], own_vec[4:5], own_vec[5:6], own_vec[6:7]]
        bias = mine(own_vec, 7, FOLDS), mine(other_vec, 7, FOLDS)
        up_bias_grad = jnp.concatenate([pick(section, *bias), pick(section, *bias[::-1])], 0).reshape(1, 2 * FOLDS * piece)
        cross_vec = pick(section, own_vec[7 + 2 * FOLDS : 9 + 2 * FOLDS, :cross_piece], own_vec[7 + 2 * FOLDS : 9 + 2 * FOLDS, cross_piece:])
        cross_gain_grad, cross_shift_grad = cross_vec[0], cross_vec[1]
    return (
        layer_out,
        text_grad,
        image_grad,
        rows_out[0],
        rows_out[1],
        heads_in_grad[None],
        heads_out_grad[None],
        rows_out[2],
        rows_out[3],
        up_grad[None],
        up_bias_grad,
        down_grad[None],
        rows_out[4],
        cross_gain_grad,
        cross_shift_grad,
        cross_query_grad,
        cross_keys_grad,
        cross_out_grad,
    )


def solution(mesh):
    placed = (
        P("dp", "section"),
        P("dp", "section", None),
        P("dp"),
        P("section", "dp"),
        P("section", "dp"),
        P("section", "dp", None),
        P("section", "dp", None),
        P("section", "dp"),
        P("section", "dp"),
        P("section", "dp", None),
        P("section", "dp"),
        P("section", "dp", None),
        P("section", "dp"),
        P(("section", "dp")),
        P(("section", "dp")),
        P(("section", "dp"), None),
        P(("section", "dp"), None),
        P(("section", "dp"), None),
        P("dp", "section"),
    )
    return jax.shard_map(
        body,
        mesh=mesh,
        in_specs=placed,
        out_specs=(P("dp", "section"), P("dp", "section"), P("dp", "section", None)) + placed[3:18],
        check_vma=False,
    )
```

```python
import functools

import jax
import jax.numpy as jnp
from jax import lax
from jax.experimental import pallas as pl
from jax.experimental.pallas import tpu as pltpu
from jax.sharding import PartitionSpec as P

HEAD_DIM = 64
PAIR = 2 * HEAD_DIM
QUAD = 4 * HEAD_DIM
EPS = 1e-05
MASKED = -1000000000.0
SCALE = HEAD_DIM**-0.5
F32 = jnp.float32
BF16 = jnp.bfloat16
MIB = 1 << 20


def swap(value):
    return lax.ppermute(value, "section", [(0, 1), (1, 0)])


def pick(section, first, later):
    return jnp.where(section == 0, first, later)


def side(own, other, section, axis):
    return jnp.concatenate([pick(section, own, other), pick(section, other, own)], axis)


def low(values):
    return values.astype(BF16)


def ring_chip(place, chips):
    return jnp.where(place < chips // 2, 2 * place, 2 * (chips - 1 - place) + 1)


def ring_order():
    chips = lax.axis_size("dp") // 2
    return list(range(0, chips, 2)) + list(range(chips - 1, 0, -2))


def ring_steps(shift):
    order = ring_order()
    chips = len(order)
    return [(2 * order[i] + core, 2 * order[(i + shift) % chips] + core) for i in range(chips) for core in range(2)]


def ring_move(value, shift):
    return lax.ppermute(value, "dp", ring_steps(shift))


def core_swap(value):
    return lax.ppermute(value, "dp", [(i, i ^ 1) for i in range(lax.axis_size("dp"))])


def my_place():
    chips = lax.axis_size("dp") // 2
    me = lax.axis_index("dp")
    chip, core = me // 2, me % 2
    return jnp.where(chip % 2 == 0, chip // 2, chips - 1 - chip // 2), core


def pack_kernel(cut, spots, *refs):
    *sources, out = refs
    chips = out.shape[0]
    for i, source in enumerate(sources[: chips - 1]):
        out[spots[i]] = source[...]
    out[spots[chips - 1], :, :cut] = sources[chips - 1][...]
    out[spots[chips - 1], :, cut:] = sources[chips][...]


def join_kernel(place, mine, other, out):
    core = place[1]
    for chip in range(mine.shape[0]):
        out[2 * chip + core] = mine[chip]
        out[2 * chip + 1 - core] = other[chip]


def reorder_kernel(order, parts, place, source, *outs):
    rows = source.shape[0] // len(order)
    width = sum(out.shape[1] for out in outs)
    for part in range(parts):
        offset = part * width
        for out in outs:
            for i, spot in enumerate(order):
                begin = part * source.shape[0] + spot * rows
                out[begin : begin + rows, :] = source[i * rows : (i + 1) * rows, offset : offset + out.shape[1]]
            offset += out.shape[1]


def reorder_late_kernel(order, blocks, place, source, out):
    rows = source.shape[0] // len(order)
    for begin, end in blocks:
        for i, spot in enumerate(order):
            out[spot * rows : (spot + 1) * rows, begin:end] = source[i * rows : (i + 1) * rows, begin:end]


class Gather:
    def __init__(self, shard):
        self.chips = lax.axis_size("dp") // 2
        self.steps = self.chips // 2
        self.rows, self.width = shard.shape
        self.cut = self.width // 256 * 128
        self.got = {0: shard}
        self.step = 0
        self.last = ()

    def front(self):
        return self.last or (self.got[-self.step], self.got[self.step])

    def put_front(self, values):
        if self.last:
            self.last = values
        else:
            self.got[-self.step], self.got[self.step] = values

    def move(self):
        self.step += 1
        up, down = self.got[1 - self.step], self.got[self.step - 1]
        if self.step < self.steps:
            self.got[-self.step], self.got[self.step] = ring_move(up, 1), ring_move(down, -1)
        else:
            self.last = (ring_move(up[:, : self.cut], 1), ring_move(down[:, self.cut :], -1))

    def pack(self):
        chips, half = self.chips, self.steps
        steps = list(range(1 - half, half + 1))
        place, _ = my_place()
        spots = jnp.stack([ring_chip((place + step + chips) % chips, chips) for step in steps]).astype(jnp.int32)
        (self.mine,) = call(
            functools.partial(pack_kernel, self.cut), spots, [self.got[step] for step in steps[:-1]] + list(self.last), [((chips, self.rows, self.width), BF16)], name="pack"
        )
        self.other = core_swap(self.mine)

    def result(self, place):
        rows = 2 * self.chips * self.rows
        if self.rows % 16 == 0:
            (full,) = call(join_kernel, place, [self.mine, self.other], [((2 * self.chips, self.rows, self.width), BF16)], name="join")
            return full.reshape(rows, self.width)
        first, later = pick(place[1], self.mine, self.other), pick(place[1], self.other, self.mine)
        return jnp.stack([first, later], 1).reshape(rows, self.width)


def together(*values):
    return lax.optimization_barrier(values)


def meet(rings, *values):
    fronts = [ring.front() for ring in rings]
    flat = together(*[v for front in fronts for v in front], *values)
    for i, ring in enumerate(rings):
        ring.put_front((flat[2 * i], flat[2 * i + 1]))
    return flat[2 * len(rings) :]


class Scatter:
    def __init__(self, mine, sent):
        self.mine, self.sent = mine, sent
        self.chips, self.rows, self.width = mine.shape
        self.steps = self.left = self.chips // 2
        self.cut = self.width // 256 * 128
        self.place, _ = my_place()

    def begin(self, early=None):
        self.first = None
        if early is not None:
            self.first = core_swap(lax.dynamic_index_in_dim(early, self.chip(self.steps), 0, False))
        self.got = core_swap(self.sent)

    def chip(self, step):
        return ring_chip((self.place + step + self.chips) % self.chips, self.chips)

    def own(self, step, begin=0, end=None):
        chip = self.chip(step)
        cut_out = lambda v: lax.dynamic_index_in_dim(v, chip, 0, False)[:, begin:end].astype(F32)
        if self.first is not None and abs(step) == self.steps:
            return cut_out(self.mine) + self.first[:, begin:end].astype(F32)
        return cut_out(self.mine) + cut_out(self.got)

    def front(self):
        return self.up, self.down

    def put_front(self, values):
        self.up, self.down = values

    def step(self, *pins):
        left, cut = self.left, self.cut
        if left == self.steps:
            up, down = self.own(left, 0, cut), self.own(-left, cut)
        else:
            up, down = self.added()
            up, down = self.own(left) + up, self.own(-left) + down
        up, down, *pins = together(low(up), low(down), *pins)
        self.up, self.down = ring_move(up, 1), ring_move(down, -1)
        self.left -= 1
        return pins

    def added(self):
        up, down = self.up.astype(F32), self.down.astype(F32)
        if self.left == self.steps - 1:
            up = jnp.concatenate([up, jnp.zeros((self.rows, self.width - self.cut), F32)], 1)
            down = jnp.concatenate([jnp.zeros((self.rows, self.cut), F32), down], 1)
        return up, down

    def after_here(self, *values):
        self.mine, self.got, *_ = together(self.mine, self.got, *values)

    def result(self):
        up, down = self.added()
        return self.own(0) + up + down


def norm_unit(values):
    centred = values - jnp.mean(values, -1, keepdims=True)
    scale = lax.rsqrt(jnp.mean(centred * centred, -1, keepdims=True) + EPS)
    return centred * scale, scale


def norm_back(values, gain, grad):
    unit, scale = norm_unit(values)
    wide = grad * gain
    inner = wide - jnp.mean(wide, -1, keepdims=True) - unit * jnp.mean(wide * unit, -1, keepdims=True)
    return inner * scale, jnp.sum(grad * unit, 0, keepdims=True), jnp.sum(grad, 0, keepdims=True)


def dot(left, right):
    return jnp.dot(left, right, preferred_element_type=F32)


def dot_tn(left, right):
    return lax.dot_general(left, right, (((0,), (0,)), ((), ())), preferred_element_type=F32)


def dot_nt(left, right):
    return lax.dot_general(left, right, (((1,), (1,)), ((), ())), preferred_element_type=F32)


def heads_of(shape):
    return lax.broadcasted_iota(jnp.int32, shape, 1) // HEAD_DIM


def stacked(block):
    head = heads_of(block.shape)
    zero = jnp.zeros_like(block)
    return jnp.concatenate([jnp.where(head == h, block, zero) for h in range(block.shape[1] // HEAD_DIM)], 0)


def unstacked(rows):
    heads = rows.shape[1] // HEAD_DIM
    slots = rows.shape[0] // heads
    head = heads_of((slots, rows.shape[1]))
    out = rows[:slots]
    for h in range(1, heads):
        out = jnp.where(head == h, rows[h * slots : (h + 1) * slots], out)
    return out


def row_sums(values):
    high = low(values)
    rest = low(values - high.astype(F32))
    ones = jnp.ones((8, values.shape[1]), BF16)
    return (dot_nt(ones, high) + dot_nt(ones, rest))[0:1]


def keep_mask(length, slots):
    query = lax.broadcasted_iota(jnp.int32, (2 * slots, slots), 0) % slots
    key = lax.broadcasted_iota(jnp.int32, (2 * slots, slots), 1)
    return (key <= query) & (key < length)


def self_chances(queries, keys, keep):
    scores = jnp.where(keep, dot_nt(queries, keys) * SCALE, MASKED)
    raised = jnp.exp(scores - jnp.max(scores, -1, keepdims=True))
    return raised / jnp.sum(raised, -1, keepdims=True)


def keep_mask_turned(length, slots):
    key = lax.broadcasted_iota(jnp.int32, (slots, 2 * slots), 0)
    query = lax.broadcasted_iota(jnp.int32, (slots, 2 * slots), 1) % slots
    return (key <= query) & (key < length)


def self_chances_turned(queries, keys, keep):
    scores = jnp.where(keep, dot_nt(keys, queries) * SCALE, MASKED)
    raised = jnp.exp(scores - jnp.max(scores, 0, keepdims=True))
    return raised / jnp.sum(raised, 0, keepdims=True)


class Late:
    def __init__(self, source, scratch, sems, blocks):
        self.scratch, self.shape = scratch, scratch.shape
        self.copies = {}
        for i, (begin, end) in enumerate(blocks or [(0, None)]):
            here = (slice(None), slice(begin, end)) if blocks else Ellipsis
            copy = pltpu.make_async_copy(source.at[here] if blocks else source, scratch.at[here] if blocks else scratch, sems.at[i])
            copy.start()
            self.copies[(begin, end)] = copy

    def __getitem__(self, index):
        wanted = index[-1] if isinstance(index, tuple) and len(self.shape) == 2 else slice(None)
        low_end, high_end = wanted.start or 0, wanted.stop or self.shape[-1]
        for block in list(self.copies):
            if block[0] < high_end and (block[1] is None or block[1] > low_end):
                self.copies.pop(block).wait()
        return self.scratch[index]


class Save:
    def __init__(self, buffer, target, sems):
        self.buffer, self.target, self.sems, self.shape = buffer, target, sems, buffer.shape
        self.copies, self.whole = [], False

    def __getitem__(self, index):
        return self.buffer[index]

    def __setitem__(self, index, value):
        self.buffer[index] = value

    def flush(self, cols=None):
        if self.whole:
            return
        self.whole = cols is None
        here = (slice(None),) * (len(self.shape) - 1) + (cols,)
        copy = pltpu.make_async_copy(self.buffer if cols is None else self.buffer.at[here], self.target if cols is None else self.target.at[here], self.sems.at[len(self.copies)])
        copy.start()
        self.copies.append(copy)


def flush(ref, cols=None):
    if isinstance(ref, Save):
        ref.flush(cols)


def late(array, *blocks):
    return (array, blocks)


def save(shape, dtype):
    return (shape, dtype, "save")


def both(shape, dtype):
    return (shape, dtype, "both")


FLUSHES = 10


def run_kernel(kernel, in_kinds, out_kinds, kept, n_over, n_fetch, n_results, *refs):
    n_ins = 1 + len(in_kinds) + n_over + n_fetch
    ins, results, scratch = refs[1:n_ins], list(refs[n_ins : n_ins + n_results]), list(refs[n_ins + n_results :])
    given = []
    for ref, blocks in zip(ins, in_kinds):
        given.append(ref if blocks is None else Late(ref, scratch.pop(0), scratch.pop(0), blocks))
    saves, outs = [], []
    for i in kept:
        saves.append(Save(ins[i], results.pop(), scratch.pop(0)))
        saves[-1].flush()
    fetches = []
    for i in range(n_fetch):
        copy = pltpu.make_async_copy(refs[n_ins - n_fetch + i], results[len(results) - n_fetch + i], scratch.pop(0).at[0])
        copy.start()
        fetches.append(copy)
    results = results[: len(results) - n_fetch]
    for kind in out_kinds:
        if kind == "near":
            outs.append(results.pop(0))
            continue
        buffer = scratch.pop(0) if kind == "save" else results.pop(0)
        saves.append(Save(buffer, results.pop(0), scratch.pop(0)))
        outs.append(saves[-1])
    kernel(refs[0], *given, *outs, *scratch)
    for item in saves:
        if not item.copies:
            item.flush()
    for item in saves:
        for copy in item.copies:
            copy.wait()
    for copy in fetches:
        copy.wait()


def call(kernel, place, ins, outs, scratch=(), vmem=14, name=None, flops=0, keep=(), over=(), fetch=()):
    smem, near, far = pl.BlockSpec(memory_space=pltpu.SMEM), pl.BlockSpec(memory_space=pltpu.VMEM), pl.BlockSpec(memory_space=pl.ANY)
    in_specs, arrays, in_kinds, buffers = [smem], [place], [], []
    for entry in ins:
        if isinstance(entry, tuple):
            array, blocks = entry
            array = pltpu.with_memory_space_constraint(array, pltpu.HBM)
            in_specs.append(far)
            in_kinds.append(tuple(blocks))
            buffers += [pltpu.VMEM(array.shape, array.dtype), pltpu.SemaphoreType.DMA((max(1, len(blocks)),))]
        else:
            array = entry
            in_specs.append(smem if array.dtype == jnp.int32 else near)
            in_kinds.append(None)
        arrays.append(array)
    for array in over:
        in_specs.append(far)
        arrays.append(pltpu.with_memory_space_constraint(array, pltpu.HBM))
    for array in fetch:
        in_specs.append(far)
        arrays.append(pltpu.with_memory_space_constraint(array, pltpu.HBM))
    buffers += [pltpu.SemaphoreType.DMA((1,)) for _ in list(keep) + list(fetch)]
    out_specs, out_shapes, out_kinds = [], [], []
    for entry in outs:
        shape, dtype, kind = entry if len(entry) == 3 else entry + ("near",)
        out_kinds.append(kind)
        if kind != "save":
            out_specs.append(near)
            out_shapes.append(jax.ShapeDtypeStruct(shape, dtype))
        else:
            buffers.append(pltpu.VMEM(shape, dtype))
        if kind != "near":
            out_specs.append(far)
            out_shapes.append(pltpu.HBM(shape, dtype))
            buffers.append(pltpu.SemaphoreType.DMA((FLUSHES,)))
    for array in fetch:
        out_specs.append(near)
        out_shapes.append(jax.ShapeDtypeStruct(array.shape, array.dtype))
    for i in reversed(keep):
        out_specs.append(far)
        out_shapes.append(pltpu.HBM(ins[i].shape, ins[i].dtype))
    moved = sum(a.size * a.dtype.itemsize for a in arrays)
    return pl.pallas_call(
        functools.partial(run_kernel, kernel, tuple(in_kinds), tuple(out_kinds), tuple(keep), len(over), len(fetch), len(out_shapes)),
        in_specs=in_specs,
        out_specs=out_specs,
        out_shape=out_shapes,
        scratch_shapes=buffers + list(scratch),
        input_output_aliases={1 + len(ins) + i: i for i in range(len(over))},
        compiler_params=pltpu.CompilerParams(vmem_limit_bytes=vmem * MIB),
        cost_estimate=pl.CostEstimate(flops=flops, bytes_accessed=moved, transcendentals=0),
        name=name,
    )(*arrays)


def prepare_kernel(count, place, into, out, up, down, vectors, up_bias, cross_gain, cross_shift, sent, own_attn, own_feed, own_vecs):
    rows, width = out.shape
    half = width // 2
    section = place[0]

    def choose(make):
        first, later = make(0), make(1)
        return jnp.where(section == 0, first, later), jnp.where(section == 0, later, first)

    def feed_of(side_index):
        parts = []
        for fold in range(FOLDS):
            for device in range(count):
                begin = ((device * 2 + side_index) * FOLDS + fold) * rows
                parts.append(up[:, begin : begin + rows])
        parts += [down[(side_index * FOLDS + fold) * rows : (side_index * FOLDS + fold + 1) * rows, :] for fold in range(FOLDS)]
        return jnp.concatenate(parts, 1)

    attn, attn_other = choose(lambda i: jnp.concatenate([into[:, (2 * j + i) * half : (2 * j + i + 1) * half] for j in range(3)], 1))
    feed, feed_other = choose(feed_of)
    wide = lambda v: jnp.concatenate([v, jnp.zeros((v.shape[0], 128 - v.shape[1]), F32)], 1)
    lines = [wide(vectors[...].astype(F32))] + [wide(up_bias[:, i * rows : (i + 1) * rows].astype(F32)) for i in range(2 * FOLDS)]
    lines += [wide(cross_gain[...].astype(F32)), wide(cross_shift[...].astype(F32))]
    vecs = low(jnp.concatenate(lines + [jnp.zeros((128 - LAYER_VECS - 2, 128), F32)], 0).T[:rows])
    own_attn[:, :width] = out[...]
    own_attn[:, width:] = attn
    own_feed[...] = feed
    own_vecs[...] = vecs
    cols = width + 3 * half
    sent[:, :width] = out[...]
    sent[:, width:cols] = attn_other
    sent[:, cols : cols + 128] = vecs
    sent[:, cols + 128 :] = feed_other


def merge_kernel(place, got, own_attn, own_feed, own_vecs, attn_first, attn_last, feed_first, feed_last):
    section = place[0]
    cols = own_attn.shape[1]
    first, last = (lambda own, other: jnp.where(section == 0, own, other)), (lambda own, other: jnp.where(section == 0, other, own))
    attn, attn_other = own_attn[...], got[:, :cols]
    attn_first[:, :cols] = first(attn, attn_other)
    attn_last[...] = last(attn, attn_other)
    feed, feed_other = own_feed[...], got[:, cols + 128 :]
    feed_first[...] = first(feed, feed_other)
    feed_last[...] = last(feed, feed_other)
    vecs, vecs_other = own_vecs[...].astype(F32), got[:, cols : cols + 128].astype(F32)
    vecs_0, vecs_1 = first(vecs, vecs_other), last(vecs, vecs_other)
    half = vecs.shape[0] // 2
    cross = jnp.concatenate([vecs_0[:half], vecs_1[:half]], 0)
    lane = lax.broadcasted_iota(jnp.int32, vecs.shape, 1)
    turned = lambda v: pltpu.roll(v, LAYER_VECS, 1)
    attn_first[:, cols:] = low(jnp.where(lane < LAYER_VECS, vecs_0, jnp.where(lane < 2 * LAYER_VECS, turned(vecs_1), turned(cross))))


SELF_GAIN, SELF_SHIFT, FEED_GAIN, FEED_SHIFT, DOWN_BIAS, UP_BIAS = range(6)
FOLDS = 2
LAYER_VECS = 5 + 2 * FOLDS
CROSS_GAIN, CROSS_SHIFT = 2 * LAYER_VECS, 2 * LAYER_VECS + 1
VECS = 24


def woven(first, later, blocks):
    parts = [v.reshape(blocks, v.shape[0] // blocks, v.shape[1]) for v in (first, later)]
    return jnp.concatenate(parts, 1).reshape(2 * first.shape[0], first.shape[1])


def unwoven(value, blocks):
    parts = value.reshape(blocks, value.shape[0] // blocks, value.shape[1])
    half = parts.shape[1] // 2
    return jnp.concatenate([parts[:, :half].reshape(-1, value.shape[1]), parts[:, half:].reshape(-1, value.shape[1])], 0)


def side_in(section, own, other):
    first = jnp.where(section == 0, own, other)
    return jnp.concatenate([first, jnp.where(section == 0, other, own)], 1)


def half_in(section, values):
    half = values.shape[1] // 2
    return jnp.where(section == 0, values[:, :half], values[:, half:])


def vec(ref, row):
    return ref[row : row + 1, :]


def up_bias_of(vecs, layer, section, fold):
    return vecs[pl.ds(LAYER_VECS * layer + UP_BIAS + FOLDS * section + fold, 1), :]


def self_part(values, layer, lengths, vecs, weights, normed_ref, projected, mixed_ref):
    base = LAYER_VECS * layer
    unit, _ = norm_unit(values)
    normed = low(unit * vec(vecs, base + SELF_GAIN) + vec(vecs, base + SELF_SHIFT))
    normed_ref[...] = normed
    flush(normed_ref)
    half = mixed_ref.shape[1]
    width = values.shape[1]
    projected[...] = low(dot(normed, weights[:, width : width + 3 * half]))
    flush(projected)
    captions = lengths.shape[0]
    slots = values.shape[0] // captions
    for c in range(captions):
        keep = keep_mask(lengths[c], slots)
        here = slice(c * slots, (c + 1) * slots)
        for j in range(half // PAIR):
            q, k, v = (projected[here, i * half + j * PAIR : i * half + (j + 1) * PAIR] for i in range(3))
            chances = self_chances(stacked(q), k, keep)
            mixed_ref[here, j * PAIR : (j + 1) * PAIR] = low(unstacked(dot(low(chances), v)))


def self_first_kernel(aligned, place, lengths, text, weights, vecs, normed, projected, mixed):
    columns = weights[:, weights.shape[1] - 128 :].astype(F32)
    if aligned:
        lane = lax.broadcasted_iota(jnp.int32, columns.shape, 1)
        columns = jnp.where(lane < CROSS_GAIN, columns, unwoven(columns, weights.shape[0] // 48))
    vecs[...] = columns.T[: vecs.shape[0]]
    flush(vecs)
    self_part(text[...].astype(F32), 0, lengths, vecs, weights, normed, projected, mixed)


def self_second_kernel(place, lengths, middle, own, other, vecs, weights, hidden, normed, projected, mixed):
    total = middle[...] + (own[...].astype(F32) + other[...].astype(F32)) + vec(vecs, DOWN_BIAS)
    hidden[...] = low(total)
    flush(hidden)
    self_part(hidden[...].astype(F32), 1, lengths, vecs, weights, normed, projected, mixed)


def heads_rows(weights, section):
    width = weights.shape[0]
    return weights[pl.ds(pl.multiple_of(section * (width // 2), width // 2), width // 2), :width]


def add_heads_out(values, mixed, weights):
    return values + dot(mixed[...], weights[:, : values.shape[1]])


def feed_part(middle, layer, section, vecs, feed, normed_ref, slope_ref, active_ref):
    base = LAYER_VECS * layer
    width = middle.shape[1]
    unit, _ = norm_unit(middle)
    normed = low(unit * vec(vecs, base + FEED_GAIN) + vec(vecs, base + FEED_SHIFT))
    normed_ref[...] = normed
    flush(normed_ref)
    total = jnp.zeros_like(middle)
    for i in range(FOLDS):
        here = slice(i * width, (i + 1) * width)
        raised = dot(normed, feed[:, here]) + up_bias_of(vecs, layer, section, i)
        chance = 0.5 * (1.0 + lax.erf(raised * 0.5**0.5))
        slope_ref[:, here] = low(chance + raised * jnp.exp(-0.5 * raised * raised) * 0.3989422804014327)
        active = low(raised * chance)
        active_ref[:, here] = active
        flush(slope_ref, here)
        flush(active_ref, here)
        total += dot(active, feed[:, (FOLDS + i) * width : (FOLDS + i + 1) * width])
    return low(total)


def feed_first_kernel(place, text, own, other, vecs, weights, feed, mixed_all, middle, normed, slope, active, part):
    mixed_all[...] = side_in(place[0], own[...], other[...])
    flush(mixed_all)
    values = add_heads_out(text[...].astype(F32), mixed_all, weights)
    middle[...] = values
    flush(middle)
    part[...] = feed_part(values, 0, place[0], vecs, feed, normed, slope, active)


def by_caption(kernel, array, weights, out, name, flops):
    block = lambda shape: pl.BlockSpec((1,) + shape[1:], lambda i: (i, 0, 0))
    moved = array.size * array.dtype.itemsize + out.size * out.dtype.itemsize
    return pl.pallas_call(
        kernel,
        grid=(array.shape[0],),
        in_specs=[block(array.shape), pl.BlockSpec(weights.shape, lambda i: (0, 0))],
        out_specs=block(out.shape),
        out_shape=pltpu.HBM(out.shape, out.dtype),
        compiler_params=pltpu.CompilerParams(vmem_limit_bytes=24 * MIB),
        cost_estimate=pl.CostEstimate(flops=flops, bytes_accessed=moved, transcendentals=0),
        name=name,
    )(array, weights)


def pairs_kernel(place, image, keys, pairs):
    for c in range(image.shape[0]):
        pairs[c] = low(dot(image[c], keys[...]))


def image_grad_kernel(grad_pairs, keys, grad):
    grad[0] = dot_nt(grad_pairs[0], keys[...])


def cross_kernel(place, hidden, own, other, vecs, weights, query, pairs, mixed_all, first, normed_ref, queries, part, stats):
    mixed_all[...] = side_in(place[0], own[...], other[...])
    flush(mixed_all)
    values = add_heads_out(hidden[...].astype(F32), mixed_all, weights)
    first[...] = values
    flush(first)
    unit, _ = norm_unit(values)
    normed = low(unit * vec(vecs, CROSS_GAIN) + vec(vecs, CROSS_SHIFT))
    normed_ref[...] = normed
    flush(normed_ref)
    rows, width = values.shape
    queries[...] = low(dot(normed, query[...]))
    flush(queries)
    captions = pairs.shape[0]
    slots = rows // captions
    quads = width // QUAD
    for c in range(captions):
        here = slice(c * slots, (c + 1) * slots)
        for j in range(quads):
            cols = slice(j * QUAD, (j + 1) * QUAD)
            k, v = pairs[c, :, cols], pairs[c, :, width + j * QUAD : width + (j + 1) * QUAD]
            scores = dot_nt(k, stacked(queries[here, cols])) * SCALE
            top = jnp.max(scores, 0, keepdims=True)
            raised = jnp.exp(scores - top)
            part[here, cols] = low(unstacked(dot_tn(low(raised), v)))
            row = c * quads + j
            stats[row : row + 1, :] = top
            stats[STATS + row : STATS + row + 1, :] = jnp.sum(raised, 0, keepdims=True)


STATS = 16


def feed_second_kernel(place, first, own, other, own_stats, other_stats, vecs, out, feed, middle, mixed, factor, normed, slope, active, part):
    rows, width = first.shape
    quads = width // QUAD
    top, top_other = own_stats[:STATS], other_stats[:STATS]
    best = jnp.maximum(top, top_other)
    own_weight, other_weight = jnp.exp(top - best), jnp.exp(top_other - best)
    inverse = 1.0 / (own_stats[STATS:] * own_weight + other_stats[STATS:] * other_weight)
    own_factor, other_factor = own_weight * inverse, other_weight * inverse
    factor[...] = own_factor
    flush(factor)
    columns = jnp.concatenate([own_factor, other_factor, jnp.zeros((PAIR - 2 * STATS, QUAD), F32)], 0).T
    slots = QUAD // 4
    head = heads_of((slots, QUAD))
    for c in range(rows // slots):
        here = slice(c * slots, (c + 1) * slots)
        for j in range(quads):
            cols = slice(j * QUAD, (j + 1) * QUAD)

            def spread(column):
                out = columns[:slots, column : column + 1]
                for h in range(1, 4):
                    out = jnp.where(head == h, columns[h * slots : (h + 1) * slots, column : column + 1], out)
                return out

            row = c * quads + j
            mixed[here, cols] = low(spread(row) * own[here, cols].astype(F32) + spread(STATS + row) * other[here, cols].astype(F32))
    flush(mixed)
    values = first[...] + dot(mixed[...], out[...])
    middle[...] = values
    flush(middle)
    part[...] = feed_part(values, 1, place[0], vecs, feed, normed, slope, active)


def feed_back(grad, vecs, feed, slope, bias_grad, down_bias_grad, slope_ref, part):
    width = grad.shape[1]
    grad_low = low(grad)
    down_bias_grad[...] = jnp.sum(grad, 0, keepdims=True)
    total = jnp.zeros(grad.shape, F32)
    for i in range(FOLDS):
        here = slice(i * width, (i + 1) * width)
        down = feed[:, (FOLDS + i) * width : (FOLDS + i + 1) * width]
        grad_raised = low(dot_nt(grad_low, down) * slope[:, here].astype(F32))
        slope_ref[:, here] = grad_raised
        bias_grad[i : i + 1, :] = jnp.sum(grad_raised.astype(F32), 0, keepdims=True)
        total += dot_nt(grad_raised, feed[:, here])
    part[...] = low(total)


def feed_back_last_kernel(place, cot, vecs, feed, slope, bias_grad, down_bias_grad, grad_raised, part):
    feed_back(cot[...].astype(F32), vecs, feed, slope, bias_grad, down_bias_grad, grad_raised, part)


def cross_back_kernel(place, own, other, middle, vecs, cot, out, queries, pairs, stats, factor, mixed, grad_ref, low_ref, vec_grad, query_part, grad_pairs, grad_mixed):
    rows, width = middle.shape
    inner = own[...].astype(F32) + other[...].astype(F32)
    step, gain_grad, shift_grad = norm_back(middle[...], vec(vecs, LAYER_VECS + FEED_GAIN), inner)
    vec_grad[0:1, :] = gain_grad
    vec_grad[1:2, :] = shift_grad
    grad = step + cot[...].astype(F32)
    grad_ref[...] = grad
    low_ref[...] = low(grad)
    grad_mixed[...] = low(dot_nt(low(grad), out[...]))
    captions = pairs.shape[0]
    slots = rows // captions
    quads = width // QUAD
    for c in range(captions):
        here = slice(c * slots, (c + 1) * slots)
        for j in range(quads):
            cols = slice(j * QUAD, (j + 1) * QUAD)
            later = slice(width + j * QUAD, width + (j + 1) * QUAD)
            row = slice(c * quads + j, c * quads + j + 1)
            k, v = pairs[c, :, cols], pairs[c, :, later]
            q = stacked(queries[here, cols])
            grad_block = grad_mixed[here, cols]
            grads = stacked(grad_block)
            delta = row_sums(stacked(grad_block.astype(F32) * mixed[here, cols].astype(F32)))
            chances = jnp.exp(dot_nt(k, q) * SCALE - stats[row, :]) * factor[row, :]
            slope = low(chances * (dot_nt(v, grads) - delta))
            query_part[here, cols] = low(unstacked(dot_tn(slope, k)) * SCALE)
            grad_pairs[c, :, cols] = low(dot(slope, q) * SCALE)
            grad_pairs[c, :, later] = low(dot(low(chances), grads))


def self_back(grad, section, lengths, weights, projected, low_ref, grad_projected, grad_mixed):
    half = grad_mixed.shape[1]
    low_ref[...] = low(grad)
    flush(low_ref)
    grad_mixed[...] = low(dot_nt(low(grad), heads_rows(weights, section)))
    captions = lengths.shape[0]
    slots = grad.shape[0] // captions
    for c in range(captions):
        keep = keep_mask_turned(lengths[c], slots)
        here = slice(c * slots, (c + 1) * slots)
        for j in range(half // PAIR):
            cols = [slice(i * half + j * PAIR, i * half + (j + 1) * PAIR) for i in range(3)]
            q, k, v = (projected[here, cols[i]] for i in range(3))
            q = stacked(q)
            chances = self_chances_turned(q, k, keep)
            grads = stacked(grad_mixed[here, cols[0]])
            grad_chances = dot_nt(v, grads)
            slope = low(chances * (grad_chances - jnp.sum(grad_chances * chances, 0, keepdims=True)))
            grad_projected[here, cols[0]] = low(unstacked(dot_tn(slope, k)) * SCALE)
            grad_projected[here, cols[1]] = low(dot(slope, q) * SCALE)
            grad_projected[here, cols[2]] = low(dot(low(chances), grads))
    width = grad.shape[1]
    return dot_nt(grad_projected[...], weights[:, width : width + 3 * half])


def self_back_second_kernel(place, lengths, grad_middle, own, other, first, vecs, query, weights, projected, grad_ref, low_ref, grad_queries, grad_projected, part, vec_grad, grad_mixed):
    total = low(own[...].astype(F32) + other[...].astype(F32))
    grad_queries[...] = total
    inner = dot_nt(total, query[...])
    step, gain_grad, shift_grad = norm_back(first[...], vec(vecs, CROSS_GAIN), inner)
    vec_grad[0:1, :] = gain_grad
    vec_grad[1:2, :] = shift_grad
    grad = step + grad_middle[...]
    grad_ref[...] = grad
    part[...] = low(self_back(grad, place[0], lengths, weights, projected, low_ref, grad_projected, grad_mixed))


def feed_back_first_kernel(place, grad_first, own, other, hidden, vecs, slope, feed, grad_ref, low_ref, vec_grad, bias_grad, down_bias_grad, grad_raised, part):
    inner = own[...].astype(F32) + other[...].astype(F32)
    step, gain_grad, shift_grad = norm_back(hidden[...].astype(F32), vec(vecs, LAYER_VECS + SELF_GAIN), inner)
    vec_grad[0:1, :] = gain_grad
    vec_grad[1:2, :] = shift_grad
    low_ref[...] = low(step + grad_first[...])
    grad = low_ref[...].astype(F32)
    grad_ref[...] = grad
    feed_back(grad, vecs, feed, slope, bias_grad, down_bias_grad, grad_raised, part)


def self_back_first_kernel(place, lengths, grad_hidden, own, other, middle, text, vecs, projected, weights, grad_ref, low_ref, grad_projected, part, vec_grad, grad_mixed):
    inner = own[...].astype(F32) + other[...].astype(F32)
    step, gain_grad, shift_grad = norm_back(middle[...], vec(vecs, FEED_GAIN), inner)
    vec_grad[0:1, :] = gain_grad
    vec_grad[1:2, :] = shift_grad
    grad = step + grad_hidden[...]
    grad_ref[...] = grad
    total = self_back(grad, place[0], lengths, weights, projected, low_ref, grad_projected, grad_mixed)
    part[...] = low(total)
    unit, _ = norm_unit(text[...].astype(F32))
    vec_grad[2:3, :] = jnp.sum(total * unit, 0, keepdims=True)
    vec_grad[3:4, :] = jnp.sum(total, 0, keepdims=True)


def text_grad_kernel(place, grad_middle, own, other, text, vecs, out):
    inner = own[...].astype(F32) + other[...].astype(F32)
    step, _, _ = norm_back(text[...].astype(F32), vec(vecs, SELF_GAIN), inner)
    total = step + grad_middle[...]
    half = out.shape[1]
    out[...] = jnp.where(place[0] == 0, total[:, :half], total[:, half:])


BLOCK = 384


def weight_grads(pieces, refs, put):
    offset = 0
    rows = min(refs[left].shape[1] for left, _ in pieces)
    for left, right in pieces:
        for i in range(refs[left].shape[1] // rows):
            for j in range(refs[right].shape[1] // BLOCK):
                put(offset, dot_tn(refs[left][:, i * rows : (i + 1) * rows], refs[right][:, j * BLOCK : (j + 1) * BLOCK]))
                offset += BLOCK
    return offset


def put_in_order(order, out, cols, value):
    rows = value.shape[0] // len(order)
    for i, device in enumerate(order):
        out[i * rows : (i + 1) * rows, cols] = low(value[device * rows : (device + 1) * rows])
    flush(out, cols)


def products_kernel(order, pieces, place, *refs):
    weight_grads(pieces, refs, lambda offset, value: put_in_order(order, refs[-1], slice(offset, offset + value.shape[1]), value))


def put_by_core(core, mine, sent):
    chips, rows, _ = mine.shape

    def put(offset, value):
        cols = slice(offset, offset + value.shape[1])
        for chip in range(chips):
            first = value[2 * chip * rows : (2 * chip + 1) * rows]
            later = value[(2 * chip + 1) * rows : (2 * chip + 2) * rows]
            mine[chip, :, cols] = low(jnp.where(core == 0, first, later))
            sent[chip, :, cols] = low(jnp.where(core == 0, later, first))
        flush(mine, cols)
        flush(sent, cols)

    return put


def ring_products_kernel(pieces, place, *refs):
    weight_grads(pieces, refs, put_by_core(place[1], *refs[-2:]))


def last_products_kernel(
    blocks, place, normed, grad_projected, mixed_0, mixed_1, low_0, low_1, vecs_0, self_vecs_1, feed_vecs_1, cross_vecs, down_0, down_1, bias_0, bias_1, mine, sent
):
    section = place[0]
    put = put_by_core(place[1], mine, sent)
    width = normed.shape[1]
    offset = weight_grads(((0, 1),), (normed, grad_projected), put)
    mixed = jnp.where(section == 0, mixed_0[...], mixed_1[...])
    head_low = jnp.where(section == 0, low_0[...], low_1[...])
    for j in range(width // BLOCK):
        put(offset, dot_tn(mixed, head_low[:, j * BLOCK : (j + 1) * BLOCK]))
        offset += BLOCK
    rows = [
        vecs_0[2:4, :],
        jnp.where(section == 0, 0.0, self_vecs_1[0:2, :]),
        jnp.where(section == 0, vecs_0[0:2, :], feed_vecs_1[0:2, :]),
        jnp.where(section == 0, down_0[...], down_1[...]),
        bias_0[...],
        bias_1[...],
        cross_vecs[0:2, :],
    ]
    used = 7 + 2 * FOLDS
    columns = jnp.concatenate(rows + [jnp.zeros((128 - used - 2, width), F32)], 0).T
    if blocks:
        lane = lax.broadcasted_iota(jnp.int32, columns.shape, 1)
        columns = jnp.where(lane < used, columns, woven(columns[: width // 2], columns[width // 2 :], blocks))
    put(offset, columns)


def keys_products_kernel(blocks, offset, place, image, grad_pairs, mine, sent):
    put = put_by_core(place[1], mine, sent)
    half = image.shape[2] // 2
    for j in range(grad_pairs.shape[2] // BLOCK):
        value = sum(dot_tn(image[c], grad_pairs[c, :, j * BLOCK : (j + 1) * BLOCK]) for c in range(image.shape[0]))
        put(offset + j * BLOCK, woven(value[:half], value[half:], blocks))


def second_products_kernel(blocks, place, normed, grad_queries, mixed, grad_low, self_normed, grad_projected, mine, sent):
    put = put_by_core(place[1], mine, sent)
    offset = weight_grads(((0, 1),), (self_normed, grad_projected), put)
    own_normed, own_mixed = half_in(place[0], normed[...]), half_in(place[0], mixed[...])
    for j in range(grad_queries.shape[1] // BLOCK):
        cols = slice(j * BLOCK, (j + 1) * BLOCK)
        put(offset, woven(dot_tn(own_normed, grad_queries[:, cols]), dot_tn(own_mixed, grad_low[:, cols]), blocks))
        offset += BLOCK


def in_order(section, own, other):
    own, other = own.astype(F32), other.astype(F32)
    return jnp.where(section == 0, own, other), jnp.where(section == 0, other, own)


def finish_feed_kernel(count, place, own, other, up, down):
    rows, width = own.shape[0], down.shape[1]
    halves = in_order(place[0], own[...], other[...])
    parts = []
    for device in range(count):
        for half in halves:
            for fold in range(FOLDS):
                begin = fold * width + device * rows
                parts.append(half[:, begin : begin + rows])
    up[...] = jnp.concatenate(parts, 1)
    for i, half in enumerate(halves):
        for fold in range(FOLDS):
            begin = (i * FOLDS + fold) * rows
            down[begin : begin + rows, :] = half[:, (FOLDS + fold) * width : (FOLDS + fold + 1) * width]


def finish_cross_kernel(place, heads, keys, keys_other, query_grad, keys_grad, out_grad):
    rows = query_grad.shape[0]
    heads32, keys32 = heads[...].astype(F32), keys[...].astype(F32)
    query_grad[...] = heads32[:rows]
    out_grad[...] = heads32[rows:]
    keys_grad[...] = jnp.where(place[0] == 0, keys32[:rows], keys32[rows:]) + keys_other[...].astype(F32)


def finish_heads_kernel(cross_rows, place, sums, own, other, into, out, gain, shift, feed_gain, feed_shift, down_bias, cross_gain, cross_shift, up_bias):
    rows, width = out.shape
    half = width // 2
    section = place[0]
    halves = in_order(section, own[...], other[:, : 3 * half])
    for i in range(3):
        for j, part in enumerate(halves):
            into[:, (2 * i + j) * half : (2 * i + j + 1) * half] = part[:, i * half : (i + 1) * half]
    out[...] = sums[:, 3 * half : 3 * half + width]
    flipped = lambda v: jnp.concatenate([v.astype(F32), jnp.zeros((128 - rows, 128), F32)], 0).T[:, :rows]
    own_vec, other_vec = flipped(sums[:, 3 * half + width :]), flipped(other[:, 3 * half :])
    mine = lambda v, first, later: jnp.where(section == 0, v[first : first + 1], v[later : later + 1])
    gain[...] = mine(own_vec, 0, 2) + mine(other_vec, 0, 2)
    shift[...] = mine(own_vec, 1, 3) + mine(other_vec, 1, 3)
    feed_gain[...] = own_vec[4:5]
    feed_shift[...] = own_vec[5:6]
    down_bias[...] = own_vec[6:7]
    bias = [[mine(v, 7 + i, 7 + FOLDS + i) for i in range(FOLDS)] for v in (own_vec, other_vec)]
    ordered = [jnp.where(section == 0, a, b) for a, b in zip(*bias)] + [jnp.where(section == 0, b, a) for a, b in zip(*bias)]
    up_bias[...] = jnp.concatenate(ordered, 1)
    for i, ref in enumerate((cross_gain, cross_shift)):
        row = own_vec[7 + 2 * FOLDS + i : 8 + 2 * FOLDS + i]
        ref[...] = jnp.where(section == 0, row[:, :cross_rows], row[:, cross_rows:])


def body(
    text,
    image,
    lengths,
    self_gain,
    self_shift,
    heads_in,
    heads_out,
    feed_gain,
    feed_shift,
    up_weight,
    up_bias,
    down_weight,
    down_bias,
    cross_gain,
    cross_shift,
    cross_query,
    cross_keys,
    cross_out,
    cotangent,
):
    section = lax.axis_index("section")
    count = lax.axis_size("dp")
    core = lax.axis_index("dp") % 2
    place = jnp.stack([section, core]).astype(jnp.int32)
    captions, half_image, width = image.shape
    rows = text.shape[0]
    piece = heads_in.shape[1]
    cross_piece = cross_query.shape[0]
    half = width // 2
    half_ff = FOLDS * width
    aligned = piece % 16 == 0
    order = [2 * chip + i for chip in ring_order() for i in range(2)] if aligned else list(range(count))
    groups = [order]

    def both_layers(first, later):
        own, got = pick(section, first, later), swap(pick(section, later, first))
        return pick(section, own, got), pick(section, got, own)

    core_cols = width + 3 * half
    cross_own = jnp.concatenate([cross_keys, cross_query, cross_out], 1)
    if aligned:
        vectors = jnp.concatenate([self_gain, self_shift, feed_gain, feed_shift, down_bias], 0)
        sent, own_attn, own_feed, own_vecs = call(
            functools.partial(prepare_kernel, count),
            place,
            [late(v) for v in (heads_in[0], heads_out[0], up_weight[0], down_weight[0], vectors, up_bias, cross_gain[None], cross_shift[None])],
            [((piece, cols), BF16) for cols in (core_cols + 128 + 2 * half_ff, core_cols, 2 * half_ff, 128)],
            name="prepare",
        )
        attn_rows_0, attn_1, feed_0, feed_1 = call(
            merge_kernel, place, [swap(sent), own_attn, own_feed, own_vecs], [((piece, cols), BF16) for cols in (core_cols + 128, core_cols, 2 * half_ff, 2 * half_ff)], name="merge"
        )
    else:
        up = up_weight[0].reshape(piece, count, 2, FOLDS, piece).transpose(2, 0, 3, 1, 4).reshape(2, piece, half_ff)
        down = down_weight[0].reshape(2, FOLDS, piece, width)
        feed_own = [jnp.concatenate([up[i]] + [down[i, j] for j in range(FOLDS)], 1) for i in range(2)]
        into = heads_in[0].reshape(piece, 3, 2, half)
        attn_own = [jnp.concatenate([heads_out[0], into[:, :, i].reshape(piece, 3 * half)], 1) for i in range(2)]
        own_vecs = jnp.concatenate([self_gain, self_shift, feed_gain, feed_shift, down_bias, up_bias.reshape(2 * FOLDS, piece)], 0)
        own_cross_vecs = jnp.concatenate([cross_gain[None], cross_shift[None]], 0)
        sent_vecs = jnp.concatenate([own_vecs, jnp.pad(own_cross_vecs, ((0, 0), (0, piece - cross_piece)))], 0)
        feed_0, feed_1 = both_layers(*feed_own)
        feed_0, feed_1, sent_vecs, *attn_own = together(feed_0, feed_1, sent_vecs, *attn_own)
        attn_0, attn_1 = both_layers(*attn_own)
        got_vecs = swap(sent_vecs)
        cross_vec_rows = side(own_cross_vecs, got_vecs[LAYER_VECS:, :cross_piece], section, 1)
        vec_cols = jnp.concatenate([pick(section, own_vecs, got_vecs[:LAYER_VECS]), pick(section, got_vecs[:LAYER_VECS], own_vecs), cross_vec_rows], 0)
        vec_cols = jnp.pad(vec_cols, ((0, 128 - vec_cols.shape[0]), (0, 0))).T
        attn_rows_0 = jnp.concatenate([attn_0, vec_cols], 1)
    ring_f = Gather(feed_0)
    ring_f.move()

    def gather(value):
        return lax.all_gather(value, "dp", axis=0, tiled=True, axis_index_groups=groups)

    def reordered(value, blocks, parts, widths):
        rows_out = value.shape[0] * parts
        if aligned:
            return call(functools.partial(reorder_kernel, blocks, parts), place, [value], [((rows_out, w), BF16) for w in widths], name="reorder")
        whole = value.reshape(value.shape[0], parts, sum(widths)).transpose(1, 0, 2).reshape(rows_out, sum(widths))
        ends = [sum(widths[: i + 1]) for i in range(len(widths))]
        return [whole[:, end - w : end] for end, w in zip(ends, widths)]

    attn_first = gather(attn_rows_0)
    attn_1, feed_1, cross_own, text_own, cot_own = meet([ring_f], attn_1, feed_1, cross_own, text, cotangent)
    cross_got = swap(cross_own)
    text_all = side(text, swap(text_own), section, 1)
    feed_last = gather(feed_1)
    cot_all = side(cotangent, swap(cot_own), section, 1)
    ring_d = Gather(attn_1)
    for i in range(ring_f.steps - 2):
        ring_f.move()
        ring_d.move()
        if i == 0:
            (cross_got,) = meet([ring_f, ring_d], cross_got)
            cross_all = gather(side(cross_own, cross_got, section, 1))
        elif i < ring_f.steps - 3:
            meet([ring_f, ring_d])
    (attn_first,) = meet([ring_f, ring_d], attn_first)
    ring_f.move()
    ring_d.move()
    (weights_0,) = reordered(attn_first, order, 1, [core_cols + 128])

    shape_f = ((rows, width), F32)
    shape_b = ((rows, width), BF16)
    shape_half = ((rows, half), BF16)
    shape_qkv = ((rows, 3 * half), BF16)
    shape_active = ((rows, half_ff), BF16)
    shape_stats = ((2 * STATS, QUAD), F32)
    shape_factor = ((STATS, QUAD), F32)
    shape_pairs = ((captions, half_image, 2 * width), BF16)
    shape_vec = ((8, width), F32)
    shape_bias = ((FOLDS, width), F32)
    shape_one = ((1, width), F32)
    half_scratch = [pltpu.VMEM((rows, half), BF16)]
    self_flops, feed_flops, pair_flops = 6 * rows * width * half, 4 * rows * width * half_ff, 4 * captions * half_image * width * width
    feed_blocks = [(i * width, (i + 1) * width) for i in (2, 0, 3, 1)]
    attn_blocks = [(0, width), (width, core_cols)]

    vecs, vecs_far, normed_a0, qkv_0, mixed_0, weights_0_far = call(
        functools.partial(self_first_kernel, aligned),
        place,
        [lengths, text_all, weights_0],
        [both((VECS, width), F32), save(*shape_b), save(*shape_qkv), shape_half],
        name="self_0",
        flops=self_flops,
        keep=(2,),
    )
    if not aligned:
        straight = lambda v: jnp.concatenate([v[:CROSS_GAIN], v[CROSS_GAIN : CROSS_GAIN + 2].reshape(2, count, 2, cross_piece).transpose(0, 2, 1, 3).reshape(2, width), v[CROSS_GAIN + 2 :]], 0)
        vecs, vecs_far = straight(vecs), straight(vecs_far)
    other_0 = swap(mixed_0)
    (mixed_0,) = meet([ring_f, ring_d], mixed_0)
    ring_f.pack()
    while ring_d.step < ring_d.steps:
        ring_d.move()
    other_0, ring_f.other = together(other_0, ring_f.other)
    feed_w0 = ring_f.result(place)
    keys, query, cross_out_w = reordered(cross_all, ring_order() if aligned else [0], 2, [2 * width, width, width])
    mixed_all_0, middle_0, normed_f0, slope_f0, active_0, part_0, feed_w0_far = call(
        feed_first_kernel,
        place,
        [text_all, mixed_0, other_0, vecs, weights_0, feed_w0],
        [save(*shape_b), save(*shape_f), save(*shape_b), save(*shape_active), save(*shape_active), shape_b],
        name="feed_0",
        flops=feed_flops,
        keep=(5,),
    )
    part_0_other = swap(part_0)
    (part_0,) = meet([ring_d], part_0)
    ring_d.pack()
    weights_1 = ring_d.result(place)
    hidden, hidden_far, normed_a1, qkv_1, mixed_1 = call(
        self_second_kernel,
        place,
        [lengths, late(middle_0), part_0, part_0_other, vecs, weights_1],
        [both(*shape_b), save(*shape_b), save(*shape_qkv), shape_half],
        name="self_1",
        flops=self_flops,
    )
    other_1 = swap(mixed_1)
    pairs, keys_far = call(pairs_kernel, place, [late(image), keys], [shape_pairs], name="pairs", flops=pair_flops, keep=(1,))
    other_1, pairs = together(other_1, pairs)
    mixed_all_1, first_1, normed_c, queries, cross_part, stats, stats_far, query_far, weights_1_far = call(
        cross_kernel,
        place,
        [hidden, mixed_1, other_1, vecs, weights_1, query, pairs],
        [save(*shape_b), save(*shape_f), save(*shape_b), save(*shape_b), shape_b, both(*shape_stats)],
        name="cross_1",
        flops=4 * rows * width * width,
        keep=(4, 5),
    )
    cross_part_other, stats_other = swap(cross_part), swap(stats)
    if aligned:
        col_blocks = [(i * width, (i + 1) * width) for i in range(2 * FOLDS)]
        (feed_w1,) = call(functools.partial(reorder_late_kernel, order, col_blocks), place, [late(feed_last, *col_blocks)], [((width, 2 * half_ff), BF16)], name="reorder_late")
    else:
        (feed_w1,) = reordered(feed_last, order, 1, [2 * half_ff])
    middle_1_far, cross_mixed_far, factor, normed_f1, slope_f1, active_1, part_1, cross_out_far = call(
        feed_second_kernel,
        place,
        [late(first_1), cross_part, cross_part_other, stats, stats_other, vecs, cross_out_w, feed_w1],
        [save(*shape_f), save(*shape_b), save(*shape_factor), shape_b, shape_active, shape_active, shape_b],
        name="feed_1",
        flops=feed_flops,
        keep=(6,),
    )
    own_cols = lambda v: pick(section, v[..., :half], v[..., half:])

    def meet_sums(rings, *values):
        flat = together(*[v for ring in rings for v in ring.front()], *values)
        for i, ring in enumerate(rings):
            ring.put_front(flat[2 * i : 2 * i + 2])
        return flat[2 * len(rings) :]

    def scatter(value):
        return lax.psum_scatter(value, "dp", scatter_dimension=0, tiled=True, axis_index_groups=groups)

    bias_grad_1, down_bias_grad_1, slope_1, back_1 = call(
        feed_back_last_kernel, place, [cot_all, vecs, feed_w1, slope_f1], [save(*shape_bias), save(*shape_one), shape_active, shape_b], name="feed_back_1", flops=feed_flops
    )
    back_1_other = swap(back_1)
    (feed_grad_1,) = call(
        functools.partial(products_kernel, order, ((0, 1), (2, 3))),
        place,
        [normed_f1, slope_1, active_1, cot_all],
        [save((width, 2 * half_ff), BF16)],
        name="feed_grads_1",
        flops=feed_flops,
    )
    back_1_other, feed_grad_1 = together(back_1_other, feed_grad_1)
    feed_got_1 = scatter(feed_grad_1)
    grad_middle_1, grad_low_1, feed_vec_1, query_part, grad_pairs = call(
        cross_back_kernel,
        place,
        [back_1, back_1_other, late(middle_1_far), late(vecs_far), late(cot_all), late(cross_out_far), late(queries), pairs, late(stats_far), late(factor), late(cross_mixed_far)],
        [shape_f, shape_b, save(*shape_vec), shape_b, shape_pairs],
        scratch=[pltpu.VMEM((rows, width), BF16)],
        name="cross_back",
        flops=4 * rows * width * width,
    )
    query_part_other = swap(query_part)
    ring_shape = lambda cols: ((count // 2, piece, cols), BF16)
    second_cols = 3 * half + 3 * width
    if aligned:
        *keys_grads, first_now, query_now, weights_now, qkv_now = call(
            functools.partial(keys_products_kernel, count, 3 * half + width),
            place,
            [late(image), grad_pairs],
            [save(*ring_shape(second_cols)), save(*ring_shape(second_cols))],
            vmem=20,
            name="keys_grads",
            flops=pair_flops,
            fetch=(first_1, query_far, weights_1_far, qkv_1),
        )
        query_part_other, *keys_grads = together(query_part_other, *keys_grads)
    else:
        first_now, query_now, weights_now, qkv_now = first_1, query_far, weights_1_far, qkv_1
    grad_first_1, head_low_1, grad_queries, grad_qkv_1, self_back_1, cross_vec_1 = call(
        self_back_second_kernel,
        place,
        [lengths, grad_middle_1, query_part, query_part_other, first_now, late(vecs_far), query_now, weights_now, qkv_now],
        [shape_f, save(*shape_b), shape_b, shape_qkv, shape_b, save(*shape_vec)],
        scratch=half_scratch,
        name="self_back_1",
        flops=2 * self_flops,
    )
    self_back_1_other = swap(self_back_1)
    if aligned:
        second_grads = call(
            functools.partial(second_products_kernel, count),
            place,
            [late(normed_c), grad_queries, late(cross_mixed_far), grad_low_1, late(normed_a1), grad_qkv_1],
            [save(*ring_shape(second_cols)), save(*ring_shape(second_cols))],
            vmem=20,
            name="second_grads",
            flops=2 * rows * width * (width + 3 * half),
            over=keys_grads,
        )
    else:
        pair_rows = lambda v: v.reshape(2, count, cross_piece, v.shape[1]).transpose(1, 0, 2, 3).reshape(width, v.shape[1])
        flat = lambda v: v.reshape(captions * half_image, v.shape[2])
        heads = pair_rows(jnp.concatenate([dot_tn(own_cols(normed_c), grad_queries), dot_tn(own_cols(cross_mixed_far), grad_low_1)], 0))
        second_grad = low(jnp.concatenate([dot_tn(normed_a1, grad_qkv_1), heads, pair_rows(dot_tn(flat(image), flat(grad_pairs)))], 1))
        parts = second_grad.reshape(count // 2, 2, piece, second_cols)
        second_grads = pick(core, parts[:, 0], parts[:, 1]), pick(core, parts[:, 1], parts[:, 0])
    early_grads = second_grads[1]
    self_back_1_other, *second_grads = together(self_back_1_other, *second_grads)
    ring_second = Scatter(*second_grads)
    ring_second.begin(early_grads)
    (self_back_1_other,) = ring_second.step(self_back_1_other)
    grad_hidden, grad_hidden_low, self_vec_1, bias_grad_0, down_bias_grad_0, slope_0, back_0 = call(
        feed_back_first_kernel,
        place,
        [grad_first_1, self_back_1, self_back_1_other, late(hidden_far), late(vecs_far), late(slope_f0, *[(i * width, (i + 1) * width) for i in range(FOLDS)]), late(feed_w0_far, *feed_blocks)],
        [shape_f, shape_b, save(*shape_vec), save(*shape_bias), save(*shape_one), shape_active, shape_b],
        name="feed_back_0",
        flops=feed_flops,
    )
    back_0_other = swap(back_0)
    (back_0,) = meet_sums([ring_second], back_0)
    (slope_0,) = ring_second.step(slope_0)
    (feed_grad_0,) = call(
        functools.partial(products_kernel, order, ((0, 1), (2, 3))),
        place,
        [late(normed_f0), slope_0, late(active_0), grad_hidden_low],
        [save((width, 2 * half_ff), BF16)],
        name="feed_grads_0",
        flops=feed_flops,
    )
    back_0_other, feed_grad_0, up, down = together(back_0_other, feed_grad_0, *ring_second.front())
    ring_second.put_front((up, down))
    feed_got_0 = scatter(feed_grad_0)
    (back_0_other,) = ring_second.step(back_0_other)
    grad_middle_0, head_low_0, grad_qkv_0, self_back_0, vecs_grad_0 = call(
        self_back_first_kernel,
        place,
        [lengths, grad_hidden, back_0, back_0_other, late(middle_0), text_all, late(vecs_far), late(qkv_0), late(weights_0_far, *attn_blocks)],
        [shape_f, shape_b, shape_qkv, shape_b, shape_vec],
        scratch=half_scratch,
        name="self_back_0",
        flops=2 * self_flops,
    )
    self_back_0_other = swap(self_back_0)
    (grad_qkv_0,) = meet_sums([ring_second], grad_qkv_0)
    grad_qkv_0, grad_pairs = ring_second.step(grad_qkv_0, grad_pairs)
    image_grad = by_caption(image_grad_kernel, grad_pairs, keys_far, jax.ShapeDtypeStruct((captions, half_image, width), F32), "image_grad", pair_flops)
    cross_vec_woven = cross_vec_1
    if not aligned:
        cross_vec_woven = cross_vec_1.reshape(8, 2, count, cross_piece).transpose(0, 2, 1, 3).reshape(8, width)
    last_grads = call(
        functools.partial(last_products_kernel, count if aligned else 0),
        place,
        [late(normed_a0), grad_qkv_0, late(mixed_all_0), late(mixed_all_1), head_low_0, late(head_low_1), vecs_grad_0]
        + [late(v) for v in (self_vec_1, feed_vec_1, cross_vec_woven, down_bias_grad_0, down_bias_grad_1, bias_grad_0, bias_grad_1)],
        [save(*ring_shape(core_cols + 128)), save(*ring_shape(core_cols + 128))],
        vmem=20,
        name="last_grads",
        flops=2 * rows * width * core_cols,
    )
    *last_grads, feed_got_1, self_back_0_other, image_grad = meet_sums([ring_second], *last_grads, feed_got_1, self_back_0_other, image_grad)
    ring_last = Scatter(*last_grads)
    ring_last.begin()
    (grad_middle_0,) = ring_last.step(grad_middle_0)
    (text_grad,) = call(text_grad_kernel, place, [grad_middle_0, self_back_0, self_back_0_other, text_all, late(vecs_far)], [((rows, half), F32)], name="text_grad")
    (text_grad,) = meet_sums([ring_last], text_grad)
    (ring_second.mine,) = ring_last.step(ring_second.mine)
    second_got = low(ring_second.result())
    (second_got,) = meet_sums([ring_last], second_got)
    ring_last.step()

    def other_half(first, later):
        return swap(pick(section, low(later), low(first)))

    (feed_got_0,) = meet_sums([ring_last], feed_got_0)
    feed_other = other_half(feed_got_0, feed_got_1)
    ring_last.step()
    got_part = swap(pick(section, part_1[:, half:], part_1[:, :half]))
    layer_out = own_cols(middle_1_far) + (own_cols(part_1).astype(F32) + got_part.astype(F32)) + own_cols(vecs_far[LAYER_VECS + DOWN_BIAS])
    cross_got = second_got[:, 3 * half : 3 * half + width]
    keys_got = second_got[:, 3 * half + width :]
    keys_other = swap(pick(section, keys_got[cross_piece:], keys_got[:cross_piece]))
    feed_own = pick(section, feed_got_0, feed_got_1)
    into_got_1 = second_got[:, : 3 * half]
    if aligned:
        up_grad, down_grad = call(
            functools.partial(finish_feed_kernel, count),
            place,
            [feed_own, feed_other],
            [((piece, 2 * half_ff), F32), ((2 * FOLDS * piece, width), F32)],
            name="finish_feed",
        )
        cross_query_grad, cross_keys_grad, cross_out_grad = call(
            finish_cross_kernel,
            place,
            [cross_got, keys_got, keys_other],
            [((cross_piece, width), F32), ((cross_piece, 2 * width), F32), ((cross_piece, width), F32)],
            name="finish_cross",
        )
        keys_other, cross_query_grad = together(keys_other, cross_query_grad)
    else:
        feed_parts = [v.astype(F32) for v in (pick(section, feed_own, feed_other), pick(section, feed_other, feed_own))]
        up_parts = [v[:, :half_ff].reshape(piece, FOLDS, count, piece).transpose(0, 2, 1, 3) for v in feed_parts]
        up_grad = jnp.stack(up_parts, 2).reshape(piece, 2 * half_ff)
        down_parts = [v[:, half_ff:].reshape(piece, FOLDS, width).transpose(1, 0, 2) for v in feed_parts]
        down_grad = jnp.stack(down_parts, 0).reshape(2 * FOLDS * piece, width)
        cross_query_grad, cross_out_grad = cross_got[:cross_piece].astype(F32), cross_got[cross_piece:].astype(F32)
        own_keys = pick(section, keys_got[:cross_piece], keys_got[cross_piece:])
        cross_keys_grad = own_keys.astype(F32) + keys_other.astype(F32)
    last_got = ring_last.result()
    vec_got = last_got[:, core_cols:]
    last_other = swap(low(jnp.concatenate([pick(section, into_got_1.astype(F32), last_got[:, : 3 * half]), vec_got], 1)))
    into_own = pick(section, last_got[:, : 3 * half], into_got_1.astype(F32))
    if aligned:
        shape_row = ((1, piece), F32)
        heads_in_grad, heads_out_grad, *rows_out, up_bias_grad = call(
            functools.partial(finish_heads_kernel, cross_piece),
            place,
            [last_got, into_own, last_other],
            [((piece, 6 * half), F32), ((piece, width), F32)] + [shape_row] * 5 + [((1, cross_piece), F32)] * 2 + [((1, 2 * FOLDS * piece), F32)],
            name="finish_heads",
        )
        cross_gain_grad, cross_shift_grad = rows_out[5][0], rows_out[6][0]
    else:
        into_other = last_other[:, : 3 * half].astype(F32)
        into_parts = pick(section, into_own, into_other), pick(section, into_other, into_own)
        heads_in_grad = jnp.stack([v.reshape(piece, 3, half) for v in into_parts], 2).reshape(piece, 6 * half)
        heads_out_grad = last_got[:, 3 * half : core_cols]
        own_vec, other_vec = vec_got.T, last_other[:, 3 * half :].astype(F32).T
        mine = lambda v, begin, size: pick(section, v[begin : begin + size], v[begin + size : begin + 2 * size])
        self_vec = mine(own_vec, 0, 2) + mine(other_vec, 0, 2)
        rows_out = [self_vec[0:1], self_vec[1:2], own_vec[4:5], own_vec[5:6], own_vec[6:7]]
        bias = mine(own_vec, 7, FOLDS), mine(other_vec, 7, FOLDS)
        up_bias_grad = jnp.concatenate([pick(section, *bias), pick(section, *bias[::-1])], 0).reshape(1, 2 * FOLDS * piece)
        cross_vec = pick(section, own_vec[7 + 2 * FOLDS : 9 + 2 * FOLDS, :cross_piece], own_vec[7 + 2 * FOLDS : 9 + 2 * FOLDS, cross_piece:])
        cross_gain_grad, cross_shift_grad = cross_vec[0], cross_vec[1]
    return (
        layer_out,
        text_grad,
        image_grad,
        rows_out[0],
        rows_out[1],
        heads_in_grad[None],
        heads_out_grad[None],
        rows_out[2],
        rows_out[3],
        up_grad[None],
        up_bias_grad,
        down_grad[None],
        rows_out[4],
        cross_gain_grad,
        cross_shift_grad,
        cross_query_grad,
        cross_keys_grad,
        cross_out_grad,
    )


def solution(mesh):
    placed = (
        P("dp", "section"),
        P("dp", "section", None),
        P("dp"),
        P("section", "dp"),
        P("section", "dp"),
        P("section", "dp", None),
        P("section", "dp", None),
        P("section", "dp"),
        P("section", "dp"),
        P("section", "dp", None),
        P("section", "dp"),
        P("section", "dp", None),
        P("section", "dp"),
        P(("section", "dp")),
        P(("section", "dp")),
        P(("section", "dp"), None),
        P(("section", "dp"), None),
        P(("section", "dp"), None),
        P("dp", "section"),
    )
    return jax.shard_map(
        body,
        mesh=mesh,
        in_specs=placed,
        out_specs=(P("dp", "section"), P("dp", "section"), P("dp", "section", None)) + placed[3:18],
        check_vma=False,
    )
```
